32 devices in a mesh: gx: 8 (over z, y), gy: 4 (over x, core).
Axes of the slice: x: 2, y: 2, z: 4, core: 2. Of those that a mesh axis runs over, the one named last changes fastest.
Arguments:
- velocity: float32 [3, 32, 32, 128], P(None, 'gx', 'gy'), may hold values from -6 to 6
- cotangent: float32 [3, 32, 32, 128], P(None, 'gx', 'gy'), may hold values from -10.5 to 13.5
- weight_in: float32 [6, 64], replicated, may hold values from -2.5 to 2.5
- bias_in: float32 [64], replicated, may hold values from -3 to 3
- weight_out: float32 [64, 3], replicated, may hold values from -0.75 to 0.75
Outputs:
- new_velocity: float32 [3, 32, 32, 128], P(None, 'gx', 'gy')
- grad_velocity: float32 [3, 32, 32, 128], P(None, 'gx', 'gy')
- grad_weight_in: float32 [6, 64], replicated
- grad_bias_in: float32 [64], replicated
- grad_weight_out: float32 [64, 3], replicated
The draws below stay inside these ranges and needn't reach their ends.
All inputs are finite; a program needn't handle non-finite values.
Results may differ from the reference program's by a relative error of at most 0.0003.
Values sent between devices are 32-bit elements; how exact they have to be, the bound alone decides.
No kernel may reach another device: no remote copies, remote signals or barrier semaphores. Data moves between devices by JAX's collectives and lax.ppermute only.
A program may use at most 64 MiB of HBM per device.

```python
import jax
import jax.numpy as jnp
from jax import lax

UNITS = 64
X_CELLS = 32
Y_CELLS = 32
Z_CELLS = 128
ALL_CELLS = 131072


def draw_cotangent(key, part):
    shape = (3, X_CELLS, Y_CELLS, Z_CELLS)
    base = jnp.clip(jax.random.normal(key, shape, jnp.float32), -4.0, 4.0)
    position = lax_ramp(shape)
    return ((0.5 + base) * position).astype(jnp.float32)


def lax_ramp(shape):
    across = jnp.arange(shape[1], dtype=jnp.float32) / float(max(shape[1] - 1, 1))
    return (1.0 + 2.0 * across)[None, :, None, None]


def level_of(own_key, shape, split, smallest, high):
    level, own = 1.0, jax.random.fold_in(own_key, 6)
    for axis_at, shards_of in split:
        draws = jnp.exp(jax.random.uniform(jax.random.fold_in(own, axis_at), (shards_of,), jnp.float32, smallest / len(split), high / len(split)))
        level = level * jnp.repeat(draws, shape[axis_at] // shards_of).reshape([-1 if axis == axis_at else 1 for axis in range(len(shape))])
    return level


def gaussian(stream_key, shape, width, bound, split=(), kind=jnp.bfloat16):
    values = width * jax.random.normal(stream_key, shape, jnp.float32)
    if split:
        values = values * level_of(stream_key, shape, split, -0.22, 0.18)
    return jnp.clip(values, -bound, bound).astype(kind)


def setup_inputs(seed: int = 0) -> dict:
    arg_keys = jax.random.split(jax.random.key(seed), 6)
    return {
        "velocity": gaussian(arg_keys[0], (3, X_CELLS, Y_CELLS, Z_CELLS), 1.0, 6.0, ((1, 8), (2, 4)), jnp.float32),
        "cotangent": draw_cotangent(jax.random.fold_in(arg_keys[5], 71), 0),
        "weight_in": gaussian(arg_keys[2], (6, UNITS), 6 ** -0.5, 2.5, (), jnp.float32),
        "bias_in": gaussian(arg_keys[3], (UNITS,), 0.5, 3.0, (), jnp.float32),
        "weight_out": gaussian(arg_keys[4], (UNITS, 3), UNITS ** -0.5, 0.75, (), jnp.float32),
    }


FILTER_ALPHA = 0.499
FILTER_GAIN = 0.5 + FILTER_ALPHA
COMPACT_ALPHA = 1.0 / 3.0
STEP_SIZE = 0.5
PRECISE = lax.Precision.HIGHEST

def shifted(values, axis, offset):
    length = values.shape[axis]
    padding = [(0, 0)] * values.ndim
    padding[axis] = (2, 2)
    padded = jnp.pad(values, padding)
    return lax.slice_in_dim(padded, 2 + offset, 2 + offset + length, axis=axis)

def solve_along(right_side, axis, coupling):
    moved = jnp.moveaxis(right_side, axis, 0)
    shape = moved.shape
    flat = moved.reshape(shape[0], -1)
    length = shape[0]
    diagonal = jnp.ones((length,), flat.dtype)
    beside = jnp.full((length,), coupling, flat.dtype)
    below = beside.at[0].set(0.0)
    above = beside.at[length - 1].set(0.0)
    solved = lax.linalg.tridiagonal_solve(below, diagonal, above, flat)
    return jnp.moveaxis(solved.reshape(shape), 0, axis)

def stencil(values, axis):
    return 7.0 / 9.0 * (shifted(values, axis, 1) - shifted(values, axis, -1)) + 1.0 / 36.0 * (shifted(values, axis, 2) - shifted(values, axis, -2))

def derive(values, axis):
    return solve_along(stencil(values, axis), axis, COMPACT_ALPHA)

def derive_adjoint(values, axis):
    return -stencil(solve_along(values, axis, COMPACT_ALPHA), axis)

def smooth(values):
    right_side = FILTER_GAIN * values + 0.5 * FILTER_GAIN * (shifted(values, 1, 1) + shifted(values, 1, -1))
    return solve_along(right_side, 1, FILTER_ALPHA)

def closure_plane(feature_plane, cotangent_plane, weight_in, bias_in, weight_out):
    pre = jnp.dot(weight_in.T, feature_plane, precision=PRECISE) + bias_in[:, None]
    hidden = jnp.tanh(pre)
    forcing = jnp.dot(weight_out.T, hidden, precision=PRECISE)
    grad_out = STEP_SIZE * cotangent_plane
    grad_hidden = jnp.dot(weight_out, grad_out, precision=PRECISE)
    grad_pre = grad_hidden * (1.0 - hidden * hidden)
    grad_feature = jnp.dot(weight_in, grad_pre, precision=PRECISE)
    sum_in = jnp.dot(feature_plane, grad_pre.T, precision=PRECISE)
    sum_bias = jnp.sum(grad_pre, axis=1)
    sum_out = jnp.dot(hidden, grad_out.T, precision=PRECISE)
    return (forcing, grad_feature, sum_in, sum_bias, sum_out)

def reference(velocity, cotangent, weight_in, bias_in, weight_out):
    smoothed = smooth(velocity)
    features = jnp.concatenate([derive(smoothed, 2), derive(smoothed, 3)], axis=0)
    plane_cells = Y_CELLS * Z_CELLS
    feature_planes = jnp.moveaxis(features, 1, 0).reshape(X_CELLS, 6, plane_cells)
    cotangent_planes = jnp.moveaxis(cotangent, 1, 0).reshape(X_CELLS, 3, plane_cells)

    def one_plane(pair):
        return closure_plane(pair[0], pair[1], weight_in, bias_in, weight_out)
    forcing, grad_feature, sum_in, sum_bias, sum_out = lax.map(one_plane, (feature_planes, cotangent_planes))
    forcing = jnp.moveaxis(forcing.reshape(X_CELLS, 3, Y_CELLS, Z_CELLS), 0, 1)
    grad_feature = jnp.moveaxis(grad_feature.reshape(X_CELLS, 6, Y_CELLS, Z_CELLS), 0, 1)
    new_velocity = velocity + STEP_SIZE * forcing
    back = derive_adjoint(grad_feature[0:3], 2) + derive_adjoint(grad_feature[3:6], 3)
    grad_velocity = cotangent + smooth(back)
    cells = float(ALL_CELLS)
    return (new_velocity, grad_velocity, jnp.sum(sum_in, axis=0) / cells, jnp.sum(sum_bias, axis=0) / cells, jnp.sum(sum_out, axis=0) / cells)
```

```python
import jax
import jax.numpy as jnp
import numpy as np
from jax import lax
from jax.sharding import PartitionSpec as P

FILTER_ALPHA = 0.499
FILTER_GAIN = 0.5 + FILTER_ALPHA
COMPACT_ALPHA = 1.0 / 3.0
STEP_SIZE = 0.5
PRECISE = lax.Precision.HIGHEST


def beside(length, offset):
    return np.eye(length, k=offset) + np.eye(length, k=-offset)


def smooth_table(length):
    left = np.eye(length) + FILTER_ALPHA * beside(length, 1)
    right = FILTER_GAIN * np.eye(length) + 0.5 * FILTER_GAIN * beside(length, 1)
    return np.linalg.solve(left, right)


def derivative_table(length):
    left = np.eye(length) + COMPACT_ALPHA * beside(length, 1)
    right = 7.0 / 9.0 * (np.eye(length, k=1) - np.eye(length, k=-1)) + 1.0 / 36.0 * (
        np.eye(length, k=2) - np.eye(length, k=-2)
    )
    return np.linalg.solve(left, right)


def table(values):
    return jnp.asarray(values.astype(np.float32))


def local(velocity, cotangent, weight_in, bias_in, weight_out):
    axes = ("gx", "gy")
    x_devices, y_devices = lax.axis_size("gx"), lax.axis_size("gy")
    devices = x_devices * y_devices
    _, x_rows, y_rows, z_length = velocity.shape
    x_length, y_length = x_rows * x_devices, y_rows * y_devices
    units = weight_in.shape[1]
    z_rows = -(-z_length // devices)
    padding = z_rows * devices - z_length

    z_table = table(derivative_table(z_length))
    y_table = table(derivative_table(y_length))
    x_table = table(smooth_table(x_length))

    along_z = jnp.einsum("ab,kxyb->kxya", z_table, velocity, precision=PRECISE)
    fields = jnp.concatenate([velocity, along_z, cotangent], axis=0)
    fields = jnp.pad(fields, ((0, 0), (0, 0), (0, 0), (0, padding)))
    fields = fields.reshape(9, x_rows, y_rows, z_rows, devices)
    fields = fields.transpose(4, 0, 3, 1, 2).reshape(devices, 9, z_rows * x_rows * y_rows)
    fields = lax.all_to_all(fields, axes, 0, 0, tiled=True)
    fields = fields.reshape(x_devices, y_devices, 9, z_rows, x_rows, y_rows)
    fields = fields.transpose(2, 0, 4, 3, 1, 5).reshape(9, x_length, z_rows, y_length)

    smoothed = jnp.einsum("ab,kbzy->kazy", x_table, fields[:6], precision=PRECISE)
    along_y = jnp.einsum("ab,kxzb->kxza", y_table, smoothed[:3], precision=PRECISE)
    features = jnp.concatenate([along_y, smoothed[3:]], axis=0).reshape(6, -1)
    grad_out = STEP_SIZE * fields[6:].reshape(3, -1)

    hidden = jnp.tanh(jnp.dot(weight_in.T, features, precision=PRECISE) + bias_in[:, None])
    forcing = jnp.dot(weight_out.T, hidden, precision=PRECISE)
    grad_pre = jnp.dot(weight_out, grad_out, precision=PRECISE) * (1.0 - hidden * hidden)
    grad_features = jnp.dot(weight_in, grad_pre, precision=PRECISE)
    sum_in = jnp.dot(features, grad_pre.T, precision=PRECISE)
    sum_bias = jnp.sum(grad_pre, axis=1)
    sum_out = jnp.dot(grad_out, hidden.T, precision=PRECISE)

    grad_features = grad_features.reshape(6, x_length, z_rows, y_length)
    back_y = jnp.einsum("ba,kxzb->kxza", y_table, grad_features[:3], precision=PRECISE)
    back = jnp.concatenate([back_y, grad_features[3:]], axis=0)
    back = jnp.einsum("ab,kbzy->kazy", x_table, back, precision=PRECISE)
    back = jnp.concatenate([forcing.reshape(3, x_length, z_rows, y_length), back], axis=0)
    back = back.reshape(9, x_devices, x_rows, z_rows, y_devices, y_rows)
    back = back.transpose(1, 4, 0, 3, 2, 5).reshape(devices, -1)
    sums = jnp.concatenate([sum_in, sum_bias[None], sum_out], axis=0).reshape(1, -1)
    cells = back.shape[1]
    back = jnp.concatenate([back, jnp.broadcast_to(sums, (devices, 10 * units))], axis=1)
    back = lax.all_to_all(back, axes, 0, 0, tiled=True)

    sums = jnp.sum(back[:, cells:], axis=0).reshape(10, units)
    sums = sums / float(x_length * y_length * z_length)
    back = back[:, :cells].reshape(devices, 9, z_rows, x_rows, y_rows)
    back = back.transpose(1, 3, 4, 2, 0).reshape(9, x_rows, y_rows, -1)[..., :z_length]
    new_velocity = velocity + STEP_SIZE * back[:3]
    back_z = jnp.einsum("ba,kxyb->kxya", z_table, back[6:], precision=PRECISE)
    grad_velocity = cotangent + back[3:6] + back_z
    return (new_velocity, grad_velocity, sums[:6], sums[6], sums[7:].T)


def solution(mesh):
    in_specs = (P(None, "gx", "gy", None), P(None, "gx", "gy", None), P(), P(), P())
    out_specs = (P(None, "gx", "gy", None), P(None, "gx", "gy", None), P(), P(), P())
    return jax.shard_map(local, mesh=mesh, in_specs=in_specs, out_specs=out_specs, check_vma=False)
```

```python
import functools

import jax
import jax.numpy as jnp
import numpy as np
from jax import lax
from jax.experimental import pallas as pl
from jax.experimental.pallas import tpu as pltpu
from jax.sharding import PartitionSpec as P

FILTER_ALPHA = 0.499
FILTER_GAIN = 0.5 + FILTER_ALPHA
COMPACT_ALPHA = 1.0 / 3.0
STEP_SIZE = 0.5
PRECISE = lax.Precision.HIGHEST
LANES = 128
SENT = 9
RETURNED = 14


def beside(length, offset):
    return np.eye(length, k=offset) + np.eye(length, k=-offset)


def smooth_table(length):
    left = np.eye(length) + FILTER_ALPHA * beside(length, 1)
    right = FILTER_GAIN * np.eye(length) + 0.5 * FILTER_GAIN * beside(length, 1)
    return np.linalg.solve(left, right)


def derivative_table(length):
    left = np.eye(length) + COMPACT_ALPHA * beside(length, 1)
    right = 7.0 / 9.0 * (np.eye(length, k=1) - np.eye(length, k=-1)) + 1.0 / 36.0 * (
        np.eye(length, k=2) - np.eye(length, k=-2)
    )
    return np.linalg.solve(left, right)


def table(values):
    return jnp.asarray(values.astype(np.float32))


def local_plain(velocity, cotangent, weight_in, bias_in, weight_out):
    axes = ("gx", "gy")
    x_devices, y_devices = lax.axis_size("gx"), lax.axis_size("gy")
    devices = x_devices * y_devices
    _, x_rows, y_rows, z_length = velocity.shape
    x_length, y_length = x_rows * x_devices, y_rows * y_devices
    units = weight_in.shape[1]
    z_rows = -(-z_length // devices)
    padding = z_rows * devices - z_length

    z_table = table(derivative_table(z_length))
    y_table = table(derivative_table(y_length))
    x_table = table(smooth_table(x_length))

    along_z = jnp.einsum("ab,kxyb->kxya", z_table, velocity, precision=PRECISE)
    fields = jnp.concatenate([velocity, along_z, cotangent], axis=0)
    fields = jnp.pad(fields, ((0, 0), (0, 0), (0, 0), (0, padding)))
    fields = fields.reshape(9, x_rows, y_rows, z_rows, devices)
    fields = fields.transpose(4, 0, 3, 1, 2).reshape(devices, 9, z_rows * x_rows * y_rows)
    fields = lax.all_to_all(fields, axes, 0, 0, tiled=True)
    fields = fields.reshape(x_devices, y_devices, 9, z_rows, x_rows, y_rows)
    fields = fields.transpose(2, 0, 4, 3, 1, 5).reshape(9, x_length, z_rows, y_length)

    smoothed = jnp.einsum("ab,kbzy->kazy", x_table, fields[:6], precision=PRECISE)
    along_y = jnp.einsum("ab,kxzb->kxza", y_table, smoothed[:3], precision=PRECISE)
    features = jnp.concatenate([along_y, smoothed[3:]], axis=0).reshape(6, -1)
    grad_out = STEP_SIZE * fields[6:].reshape(3, -1)

    hidden = jnp.tanh(jnp.dot(weight_in.T, features, precision=PRECISE) + bias_in[:, None])
    forcing = jnp.dot(weight_out.T, hidden, precision=PRECISE)
    grad_pre = jnp.dot(weight_out, grad_out, precision=PRECISE) * (1.0 - hidden * hidden)
    grad_features = jnp.dot(weight_in, grad_pre, precision=PRECISE)
    sum_in = jnp.dot(features, grad_pre.T, precision=PRECISE)
    sum_bias = jnp.sum(grad_pre, axis=1)
    sum_out = jnp.dot(grad_out, hidden.T, precision=PRECISE)

    grad_features = grad_features.reshape(6, x_length, z_rows, y_length)
    back_y = jnp.einsum("ba,kxzb->kxza", y_table, grad_features[:3], precision=PRECISE)
    back = jnp.concatenate([back_y, grad_features[3:]], axis=0)
    back = jnp.einsum("ab,kbzy->kazy", x_table, back, precision=PRECISE)
    back = jnp.concatenate([forcing.reshape(3, x_length, z_rows, y_length), back], axis=0)
    back = back.reshape(9, x_devices, x_rows, z_rows, y_devices, y_rows)
    back = back.transpose(1, 4, 0, 3, 2, 5).reshape(devices, -1)
    sums = jnp.concatenate([sum_in, sum_bias[None], sum_out], axis=0).reshape(1, -1)
    cells = back.shape[1]
    back = jnp.concatenate([back, jnp.broadcast_to(sums, (devices, 10 * units))], axis=1)
    back = lax.all_to_all(back, axes, 0, 0, tiled=True)

    sums = jnp.sum(back[:, cells:], axis=0).reshape(10, units)
    sums = sums / float(x_length * y_length * z_length)
    back = back[:, :cells].reshape(devices, 9, z_rows, x_rows, y_rows)
    back = back.transpose(1, 3, 4, 2, 0).reshape(9, x_rows, y_rows, -1)[..., :z_length]
    new_velocity = velocity + STEP_SIZE * back[:3]
    back_z = jnp.einsum("ba,kxyb->kxya", z_table, back[6:], precision=PRECISE)
    grad_velocity = cotangent + back[3:6] + back_z
    return (new_velocity, grad_velocity, sums[:6], sums[6], sums[7:].T)


def exchange(parts, width):
    parts = list(parts)
    lane = lax.broadcasted_iota(jnp.int32, parts[0].shape, 1)
    step = len(parts) // 2
    while step:
        shift = step * width
        upper = (lane & shift) != 0
        for low in range(len(parts)):
            if low & step == 0:
                first, second = parts[low], parts[low + step]
                parts[low] = jnp.where(upper, pltpu.roll(second, shift, 1), first)
                parts[low + step] = jnp.where(upper, second, pltpu.roll(first, LANES - shift, 1))
        step //= 2
    return parts


def solve_rows(rows):
    length = len(rows)
    half = length // 2
    scales = []
    before = 0.0
    for _ in range(half):
        scales.append(1.0 / (1.0 - FILTER_ALPHA * FILTER_ALPHA * before))
        before = scales[-1]
    solved = [None] * length
    for sign in (1, -1):
        order = range(half) if sign == 1 else range(length - 1, length - 1 - half, -1)
        last = None
        for turn, row in enumerate(order):
            value = rows[row] * scales[turn]
            if last is not None:
                value = value - last * (FILTER_ALPHA * scales[turn])
            solved[row] = last = value
    below, above = solved[half - 1], solved[half]
    ratio = FILTER_ALPHA * scales[half - 1]
    middle = 1.0 / (1.0 - ratio * ratio)
    solved[half - 1] = (below - ratio * above) * middle
    solved[half] = (above - ratio * below) * middle
    for turn in reversed(range(half - 1)):
        factor = FILTER_ALPHA * scales[turn]
        solved[turn] = solved[turn] - factor * solved[turn + 1]
        row = length - 1 - turn
        solved[row] = solved[row] - factor * solved[row - 1]
    return solved


def smooth_rows(rows):
    own = 0.5 * FILTER_GAIN / FILTER_ALPHA
    solved = solve_rows(rows)
    return [own * row + (FILTER_GAIN - own) * value for row, value in zip(rows, solved)]


def times(left, right, contract=(1, 0)):
    dims = (((contract[0],), (contract[1],)), ((), ()))
    return lax.dot_general(left, right, dims, precision=PRECISE, preferred_element_type=jnp.float32)


def pack_kernel(velocity_ref, cotangent_ref, table_ref, out_ref):
    _, x_rows, y_rows, z_length = velocity_ref.shape
    block = x_rows * y_rows
    groups = LANES // block
    devices = z_length // groups
    velocity = velocity_ref[...].reshape(3 * block, z_length)
    cotangent = cotangent_ref[...].reshape(3 * block, z_length)
    along_z = times(velocity, table_ref[...])
    fill = jnp.zeros(((-SENT % groups) * block, z_length), jnp.float32)
    rows = jnp.concatenate(
        [velocity, along_z, cotangent[block:], cotangent[:block], fill], axis=0
    )
    for start in range(0, SENT, groups):
        turned = rows[start * block : (start + groups) * block].T
        parts = [turned[group * devices : (group + 1) * devices] for group in range(groups)]
        parts = exchange(parts, block)
        for field in range(start, min(start + groups, SENT)):
            out_ref[pl.ds(field, devices, stride=SENT), :] = parts[field - start]


def middle_kernel(x_devices, in_ref, y_ref, weight_in_ref, bias_ref, weight_out_ref, out_ref, tail_ref):
    y_devices = in_ref.shape[0] // SENT // x_devices
    x_rows = y_devices
    x_length = x_devices * x_rows
    units = weight_in_ref.shape[1]
    y_rows = y_ref.shape[0] // y_devices
    row8 = lax.broadcasted_iota(jnp.int32, (8, LANES), 0)

    planes = []
    for x_device in range(x_devices):
        first = x_device * y_devices
        parts = [in_ref[(first + turn) * SENT : (first + turn) * SENT + 8, :] for turn in range(y_devices)]
        planes.extend(exchange(parts, y_rows))
    tails = [
        in_ref[pl.ds(turn * SENT + 8, x_devices, stride=y_devices * SENT), :]
        for turn in range(y_devices)
    ]
    tails = exchange(tails, y_rows)

    groups = LANES // y_ref.shape[0]
    y_table = y_ref[...]
    y_wide = jnp.concatenate([jnp.concatenate([y_table] * groups, axis=1)] * groups, axis=0)
    same = [
        lax.broadcasted_iota(jnp.int32, (LANES, LANES), dim) // y_ref.shape[0] for dim in (0, 1)
    ]
    y_wide = jnp.where(same[0] == same[1], y_wide, 0.0)

    smoothed = smooth_rows(planes)
    along_y = times(jnp.concatenate(smoothed, axis=0), y_wide, (1, 1))
    upper_rows = []
    lower_rows = []
    for x in range(x_length):
        features = jnp.where(row8 < 3, along_y[8 * x : 8 * x + 8], smoothed[x])
        features = jnp.where(row8 < 6, features, jnp.where(row8 == 6, 1.0, 0.0))
        last = tails[x % x_rows][x // x_rows : x // x_rows + 1]
        upper_rows.append(features)
        lower_rows.append(jnp.where(row8 == 5, last, planes[x]))

    weight_out = weight_out_ref[...]
    weight_in = weight_in_ref[...]
    zeros = functools.partial(jnp.zeros, dtype=jnp.float32)
    before = jnp.concatenate(
        [
            jnp.concatenate([weight_in, bias_ref[...], zeros((9, units))], axis=0),
            jnp.concatenate([zeros((13, units)), STEP_SIZE * weight_out], axis=0),
        ],
        axis=1,
    )
    after = jnp.concatenate(
        [
            jnp.concatenate([zeros((6, units)), weight_out, zeros((7, units))], axis=0),
            jnp.concatenate([weight_in, zeros((10, units))], axis=0),
        ],
        axis=1,
    )

    at_once = 8
    sums = zeros((16, 2 * units))
    results = []
    for start in range(0, x_length, at_once):
        stop = start + at_once
        cells = jnp.concatenate(
            [
                jnp.concatenate(upper_rows[start:stop], axis=1),
                jnp.concatenate(lower_rows[start:stop], axis=1),
            ],
            axis=0,
        )
        both = times(before, cells, (0, 0))
        hidden = jnp.tanh(both[:units])
        grad_pre = both[units:] * (1.0 - hidden * hidden)
        both = jnp.concatenate([hidden, grad_pre], axis=0)
        sums = sums + times(cells, both, (1, 1))
        result = times(after, both)
        for turn in range(at_once):
            results.append(result[:8, turn * LANES : (turn + 1) * LANES])
            x = start + turn
            place = (x % x_rows) * x_devices + x // x_rows
            tail_ref[place : place + 1, :] = result[8:9, turn * LANES : (turn + 1) * LANES]

    back_y = times(jnp.concatenate(results, axis=0), y_wide)
    back = [
        jnp.where(row8 < 3, back_y[8 * x : 8 * x + 8], results[x]) for x in range(x_length)
    ]
    back = smooth_rows(back)
    back = [jnp.where(row8 < 6, value, result) for value, result in zip(back, results)]
    for x_device in range(x_devices):
        first = x_device * y_devices
        parts = exchange(back[first : first + x_rows], y_rows)
        for turn in range(y_devices):
            place = (first + turn) * RETURNED
            out_ref[place : place + 8, :] = parts[turn]
    tails = [tail_ref[x * x_devices : (x + 1) * x_devices, :] for x in range(x_rows)]
    tails = exchange(tails, y_rows)
    for turn in range(y_devices):
        out_ref[pl.ds(turn * RETURNED + 8, x_devices, stride=y_devices * RETURNED), :] = tails[turn]

    moved = jnp.concatenate([sums[5:7, units:], STEP_SIZE * sums[13:16, :units]], axis=0)
    packed = jnp.concatenate([sums[:5, units:], moved], axis=1)
    for device in range(x_devices * y_devices):
        place = device * RETURNED + SENT
        out_ref[place : place + 5, :] = packed


def unpack_kernel(cells, in_ref, velocity_ref, cotangent_ref, table_ref, new_ref, grad_ref, in_grad_ref, bias_grad_ref, out_grad_ref):
    _, x_rows, y_rows, z_length = velocity_ref.shape
    block = x_rows * y_rows
    groups = LANES // block
    devices = z_length // groups
    units = in_grad_ref.shape[1]
    fields = []
    for start in range(0, SENT, groups):
        parts = [
            in_ref[pl.ds(min(field, SENT - 1), devices, stride=RETURNED), :]
            for field in range(start, start + groups)
        ]
        turned = jnp.concatenate(exchange(parts, block), axis=0).T
        fields.extend(turned[turn * block : (turn + 1) * block] for turn in range(groups))
    shape = (3, x_rows, y_rows, z_length)
    forcing = jnp.concatenate(fields[6:9], axis=0).reshape(shape)
    new_ref[...] = velocity_ref[...] + STEP_SIZE * forcing
    back_z = times(jnp.concatenate(fields[3:6], axis=0), table_ref[...])
    back = jnp.concatenate(fields[:3], axis=0) + back_z
    grad_ref[...] = cotangent_ref[...] + back.reshape(shape)

    sums = in_ref[SENT : SENT + 5, :]
    for device in range(1, devices):
        place = device * RETURNED + SENT
        sums = sums + in_ref[place : place + 5, :]
    sums = sums / cells
    in_grad_ref[:5, :] = sums[:, :units]
    in_grad_ref[5:, :] = sums[:1, units:]
    bias_grad_ref[...] = sums[1:2, units:]
    out_grad_ref[...] = sums[2:, units:]


def on_device(kernel, shapes, scratch=()):
    return pl.pallas_call(
        kernel,
        out_shape=[jax.ShapeDtypeStruct(shape, jnp.float32) for shape in shapes],
        scratch_shapes=[pltpu.VMEM(shape, jnp.float32) for shape in scratch],
        compiler_params=pltpu.CompilerParams(vmem_limit_bytes=32 * 1024 * 1024),
    )


def fits(velocity, units):
    x_devices, y_devices = lax.axis_size("gx"), lax.axis_size("gy")
    _, x_rows, y_rows, z_length = velocity.shape
    return (
        z_length == LANES
        and x_rows * y_rows * LANES == LANES * LANES // 4
        and x_devices * y_devices * 4 == LANES
        and x_devices == 8
        and y_devices == x_rows
        and y_rows % 8 == 0
        and 2 * units == LANES
    )


def local_kernels(velocity, cotangent, weight_in, bias_in, weight_out):
    axes = ("gx", "gy")
    x_devices, y_devices = lax.axis_size("gx"), lax.axis_size("gy")
    devices = x_devices * y_devices
    _, x_rows, y_rows, z_length = velocity.shape
    units = weight_in.shape[1]
    cells = x_rows * x_devices * y_rows * y_devices * z_length
    z_table = derivative_table(z_length)

    (sent,) = on_device(pack_kernel, [(devices * SENT, LANES)])(velocity, cotangent, table(z_table.T))
    sent = sent.reshape(devices, 1, SENT * LANES)
    sent = lax.all_to_all(sent, axes, 0, 0, tiled=True).reshape(devices * SENT, LANES)
    (back,) = on_device(
        functools.partial(middle_kernel, x_devices),
        [(devices * RETURNED, LANES)],
        [(x_devices * x_rows, LANES)],
    )(sent, table(derivative_table(y_rows * y_devices)), weight_in, bias_in[None], weight_out.T)
    back = back.reshape(devices, 1, RETURNED * LANES)
    back = lax.all_to_all(back, axes, 0, 0, tiled=True).reshape(devices * RETURNED, LANES)
    shapes = [velocity.shape, velocity.shape, (6, units), (1, units), (3, units)]
    new, grad, grad_in, grad_bias, grad_out = on_device(
        functools.partial(unpack_kernel, float(cells)), shapes
    )(back, velocity, cotangent, table(z_table))
    return (new, grad, grad_in, grad_bias[0], grad_out.T)


def local(velocity, cotangent, weight_in, bias_in, weight_out):
    chosen = local_kernels if fits(velocity, weight_in.shape[1]) else local_plain
    return chosen(velocity, cotangent, weight_in, bias_in, weight_out)


def solution(mesh):
    in_specs = (P(None, "gx", "gy", None), P(None, "gx", "gy", None), P(), P(), P())
    out_specs = (P(None, "gx", "gy", None), P(None, "gx", "gy", None), P(), P(), P())
    return jax.shard_map(local, mesh=mesh, in_specs=in_specs, out_specs=out_specs, check_vma=False)
```

```python
import functools

import jax
import jax.numpy as jnp
import ml_dtypes
import numpy as np
from jax import lax
from jax.experimental import pallas as pl
from jax.experimental.pallas import tpu as pltpu
from jax.sharding import PartitionSpec as P

FILTER_ALPHA = 0.499
FILTER_GAIN = 0.5 + FILTER_ALPHA
COMPACT_ALPHA = 1.0 / 3.0
STEP_SIZE = 0.5
PRECISE = lax.Precision.HIGHEST
LANES = 128
SENT = 9
RETURNED = 14
LEFT_PIECES = (0, 1, 0, 2, 1, 0)
RIGHT_PIECES = (0, 0, 1, 0, 1, 2)


def beside(length, offset):
    return np.eye(length, k=offset) + np.eye(length, k=-offset)


def smooth_table(length):
    left = np.eye(length) + FILTER_ALPHA * beside(length, 1)
    right = FILTER_GAIN * np.eye(length) + 0.5 * FILTER_GAIN * beside(length, 1)
    return np.linalg.solve(left, right)


def derivative_table(length):
    left = np.eye(length) + COMPACT_ALPHA * beside(length, 1)
    right = 7.0 / 9.0 * (np.eye(length, k=1) - np.eye(length, k=-1)) + 1.0 / 36.0 * (
        np.eye(length, k=2) - np.eye(length, k=-2)
    )
    return np.linalg.solve(left, right)


def table(values):
    return jnp.asarray(values.astype(np.float32))


def split_table(values):
    pieces = []
    rest = values.astype(np.float32)
    for _ in range(3):
        pieces.append(rest.astype(ml_dtypes.bfloat16))
        rest = rest - pieces[-1].astype(np.float32)
    return jnp.asarray(np.concatenate([pieces[turn] for turn in RIGHT_PIECES], axis=0))


def local_plain(velocity, cotangent, weight_in, bias_in, weight_out):
    axes = ("gx", "gy")
    x_devices, y_devices = lax.axis_size("gx"), lax.axis_size("gy")
    devices = x_devices * y_devices
    _, x_rows, y_rows, z_length = velocity.shape
    x_length, y_length = x_rows * x_devices, y_rows * y_devices
    units = weight_in.shape[1]
    z_rows = -(-z_length // devices)
    padding = z_rows * devices - z_length

    z_table = table(derivative_table(z_length))
    y_table = table(derivative_table(y_length))
    x_table = table(smooth_table(x_length))

    along_z = jnp.einsum("ab,kxyb->kxya", z_table, velocity, precision=PRECISE)
    fields = jnp.concatenate([velocity, along_z, cotangent], axis=0)
    fields = jnp.pad(fields, ((0, 0), (0, 0), (0, 0), (0, padding)))
    fields = fields.reshape(9, x_rows, y_rows, z_rows, devices)
    fields = fields.transpose(4, 0, 3, 1, 2).reshape(devices, 9, z_rows * x_rows * y_rows)
    fields = lax.all_to_all(fields, axes, 0, 0, tiled=True)
    fields = fields.reshape(x_devices, y_devices, 9, z_rows, x_rows, y_rows)
    fields = fields.transpose(2, 0, 4, 3, 1, 5).reshape(9, x_length, z_rows, y_length)

    smoothed = jnp.einsum("ab,kbzy->kazy", x_table, fields[:6], precision=PRECISE)
    along_y = jnp.einsum("ab,kxzb->kxza", y_table, smoothed[:3], precision=PRECISE)
    features = jnp.concatenate([along_y, smoothed[3:]], axis=0).reshape(6, -1)
    grad_out = STEP_SIZE * fields[6:].reshape(3, -1)

    hidden = jnp.tanh(jnp.dot(weight_in.T, features, precision=PRECISE) + bias_in[:, None])
    forcing = jnp.dot(weight_out.T, hidden, precision=PRECISE)
    grad_pre = jnp.dot(weight_out, grad_out, precision=PRECISE) * (1.0 - hidden * hidden)
    grad_features = jnp.dot(weight_in, grad_pre, precision=PRECISE)
    sum_in = jnp.dot(features, grad_pre.T, precision=PRECISE)
    sum_bias = jnp.sum(grad_pre, axis=1)
    sum_out = jnp.dot(grad_out, hidden.T, precision=PRECISE)

    grad_features = grad_features.reshape(6, x_length, z_rows, y_length)
    back_y = jnp.einsum("ba,kxzb->kxza", y_table, grad_features[:3], precision=PRECISE)
    back = jnp.concatenate([back_y, grad_features[3:]], axis=0)
    back = jnp.einsum("ab,kbzy->kazy", x_table, back, precision=PRECISE)
    back = jnp.concatenate([forcing.reshape(3, x_length, z_rows, y_length), back], axis=0)
    back = back.reshape(9, x_devices, x_rows, z_rows, y_devices, y_rows)
    back = back.transpose(1, 4, 0, 3, 2, 5).reshape(devices, -1)
    sums = jnp.concatenate([sum_in, sum_bias[None], sum_out], axis=0).reshape(1, -1)
    cells = back.shape[1]
    back = jnp.concatenate([back, jnp.broadcast_to(sums, (devices, 10 * units))], axis=1)
    back = lax.all_to_all(back, axes, 0, 0, tiled=True)

    sums = jnp.sum(back[:, cells:], axis=0).reshape(10, units)
    sums = sums / float(x_length * y_length * z_length)
    back = back[:, :cells].reshape(devices, 9, z_rows, x_rows, y_rows)
    back = back.transpose(1, 3, 4, 2, 0).reshape(9, x_rows, y_rows, -1)[..., :z_length]
    new_velocity = velocity + STEP_SIZE * back[:3]
    back_z = jnp.einsum("ba,kxyb->kxya", z_table, back[6:], precision=PRECISE)
    grad_velocity = cotangent + back[3:6] + back_z
    return (new_velocity, grad_velocity, sums[:6], sums[6], sums[7:].T)


def exchange(parts, width):
    parts = list(parts)
    lane = lax.broadcasted_iota(jnp.int32, parts[0].shape, 1)
    step = len(parts) // 2
    while step:
        shift = step * width
        upper = (lane & shift) != 0
        for low in range(len(parts)):
            if low & step == 0:
                first, second = parts[low], parts[low + step]
                parts[low] = jnp.where(upper, pltpu.roll(second, shift, 1), first)
                parts[low + step] = jnp.where(upper, second, pltpu.roll(first, LANES - shift, 1))
        step //= 2
    return parts


def solve_rows(rows):
    length = len(rows)
    half = length // 2
    scales = []
    before = 0.0
    for _ in range(half):
        scales.append(1.0 / (1.0 - FILTER_ALPHA * FILTER_ALPHA * before))
        before = scales[-1]
    solved = [None] * length
    for sign in (1, -1):
        order = range(half) if sign == 1 else range(length - 1, length - 1 - half, -1)
        last = None
        for turn, row in enumerate(order):
            value = rows[row] * scales[turn]
            if last is not None:
                value = value - last * (FILTER_ALPHA * scales[turn])
            solved[row] = last = value
    below, above = solved[half - 1], solved[half]
    ratio = FILTER_ALPHA * scales[half - 1]
    middle = 1.0 / (1.0 - ratio * ratio)
    solved[half - 1] = (below - ratio * above) * middle
    solved[half] = (above - ratio * below) * middle
    for turn in reversed(range(half - 1)):
        factor = FILTER_ALPHA * scales[turn]
        solved[turn] = solved[turn] - factor * solved[turn + 1]
        row = length - 1 - turn
        solved[row] = solved[row] - factor * solved[row - 1]
    return solved


def smooth_rows(rows):
    own = 0.5 * FILTER_GAIN / FILTER_ALPHA
    solved = solve_rows(rows)
    return [own * row + (FILTER_GAIN - own) * value for row, value in zip(rows, solved)]


def times(left, right, contract=(1, 0)):
    dims = (((contract[0],), (contract[1],)), ((), ()))
    return lax.dot_general(left, right, dims, preferred_element_type=jnp.float32)


def split(values, count):
    pieces = []
    for turn in range(count):
        pieces.append(values.astype(jnp.bfloat16))
        if turn + 1 < count:
            values = values - pieces[-1].astype(jnp.float32)
    return pieces


def times_table(values, wide_table):
    pieces = split(values, 3)
    return times(jnp.concatenate([pieces[turn] for turn in LEFT_PIECES], axis=1), wide_table)


def pack_kernel(
    velocity_hbm,
    cotangent_hbm,
    z_hbm,
    weight_in_hbm,
    bias_hbm,
    weight_out_hbm,
    y_hbm,
    y_back_hbm,
    out_ref,
    before_ref,
    after_ref,
    y_ref,
    y_back_ref,
    velocity_ref,
    cotangent_ref,
    z_ref,
    weight_in_ref,
    bias_ref,
    weight_out_ref,
    arrived,
):
    pairs = [
        (velocity_hbm, velocity_ref),
        (z_hbm, z_ref),
        (cotangent_hbm, cotangent_ref),
        (weight_in_hbm, weight_in_ref),
        (bias_hbm, bias_ref),
        (weight_out_hbm, weight_out_ref),
        (y_hbm, y_ref),
        (y_back_hbm, y_back_ref),
    ]
    copies = [
        pltpu.make_async_copy(source, target, arrived.at[turn])
        for turn, (source, target) in enumerate(pairs)
    ]
    for copy in copies:
        copy.start()

    _, x_rows, y_rows, z_length = velocity_ref.shape
    block = x_rows * y_rows
    groups = LANES // block
    devices = z_length // groups
    copies[0].wait()
    velocity = velocity_ref[...].reshape(3 * block, z_length)
    copies[1].wait()
    along_z = times_table(velocity, z_ref[...])
    copies[2].wait()
    cotangent = cotangent_ref[...].reshape(3 * block, z_length)
    fill = jnp.zeros(((-SENT % groups) * block, z_length), jnp.float32)
    rows = jnp.concatenate(
        [velocity, along_z, cotangent[block:], cotangent[:block], fill], axis=0
    )
    for start in range(0, SENT, groups):
        turned = rows[start * block : (start + groups) * block].T
        parts = [turned[group * devices : (group + 1) * devices] for group in range(groups)]
        parts = exchange(parts, block)
        for field in range(start, min(start + groups, SENT)):
            out_ref[pl.ds(field, devices, stride=SENT), :] = parts[field - start]

    for copy in copies[3:]:
        copy.wait()
    weight_in = weight_in_ref[...]
    weight_out = weight_out_ref[...]
    units = weight_in.shape[1]
    zeros = functools.partial(jnp.zeros, dtype=jnp.float32)
    before = jnp.concatenate(
        [
            jnp.concatenate([weight_in, bias_ref[...], zeros((9, units))], axis=0),
            jnp.concatenate([zeros((13, units)), STEP_SIZE * weight_out], axis=0),
        ],
        axis=1,
    )
    after = jnp.concatenate(
        [
            jnp.concatenate([zeros((6, units)), weight_out, zeros((7, units))], axis=0),
            jnp.concatenate([weight_in, zeros((10, units))], axis=0),
        ],
        axis=1,
    )
    pieces = [piece.astype(jnp.float32) for piece in split(before, 3)]
    before = jnp.concatenate([pieces[turn] for turn in RIGHT_PIECES + (1, 2)], axis=0)
    before_ref[...] = before.T.astype(jnp.bfloat16)
    pieces = split(after, 3)
    after_ref[...] = jnp.concatenate(
        [
            jnp.concatenate([pieces[0], pieces[0]], axis=1),
            jnp.concatenate([pieces[1], pieces[1]], axis=1),
            jnp.concatenate([pieces[2], jnp.zeros_like(pieces[2])], axis=1),
        ],
        axis=0,
    )


def middle_kernel(x_devices, in_ref, before_ref, after_ref, y_ref, y_back_ref, out_ref, tail_ref):
    y_devices = in_ref.shape[0] // SENT // x_devices
    x_rows = y_devices
    x_length = x_devices * x_rows
    units = before_ref.shape[0] // 2
    y_rows = LANES // y_devices // x_rows
    row8 = lax.broadcasted_iota(jnp.int32, (8, LANES), 0)

    planes = []
    for x_device in range(x_devices):
        first = x_device * y_devices
        parts = [
            in_ref[(first + turn) * SENT : (first + turn) * SENT + 8, :]
            for turn in range(y_devices)
        ]
        planes.extend(exchange(parts, y_rows))
    tails = [
        in_ref[pl.ds(turn * SENT + 8, x_devices, stride=y_devices * SENT), :]
        for turn in range(y_devices)
    ]
    tails = exchange(tails, y_rows)

    smoothed = smooth_rows(planes)
    along_y = times_table(jnp.concatenate(smoothed, axis=0), y_ref[...])
    upper_rows = []
    lower_rows = []
    for x in range(x_length):
        features = jnp.where(row8 < 3, along_y[8 * x : 8 * x + 8], smoothed[x])
        features = jnp.where(row8 < 6, features, jnp.where(row8 == 6, 1.0, 0.0))
        last = tails[x % x_rows][x // x_rows : x // x_rows + 1]
        upper_rows.append(features)
        lower_rows.append(jnp.where(row8 == 5, last, planes[x]))

    before = before_ref[...]
    after = after_ref[...]
    at_once = 8
    sums = jnp.zeros((32, 4 * units), jnp.float32)
    results = []
    for start in range(0, x_length, at_once):
        stop = start + at_once
        cells = jnp.concatenate(
            [
                jnp.concatenate(upper_rows[start:stop], axis=1),
                jnp.concatenate(lower_rows[start:stop], axis=1),
            ],
            axis=0,
        )
        pieces = split(cells, 3)
        both = times(before, jnp.concatenate([pieces[turn] for turn in LEFT_PIECES + (2, 1)], axis=0))
        hidden = jnp.tanh(both[:units])
        grad_pre = both[units:] * (1.0 - hidden * hidden)
        both = jnp.concatenate([hidden, grad_pre], axis=0)
        both = jnp.concatenate(split(both, 2), axis=0)
        sums = sums + times(jnp.concatenate(pieces[:2], axis=0), both, (1, 1))
        result = times(after, both)
        result = result[:16] + result[16:32] + result[32:]
        for turn in range(at_once):
            results.append(result[:8, turn * LANES : (turn + 1) * LANES])
            x = start + turn
            place = (x % x_rows) * x_devices + x // x_rows
            tail_ref[place : place + 1, :] = result[8:9, turn * LANES : (turn + 1) * LANES]

    back_y = times_table(jnp.concatenate(results, axis=0), y_back_ref[...])
    back = [
        jnp.where(row8 < 3, back_y[8 * x : 8 * x + 8], results[x]) for x in range(x_length)
    ]
    back = smooth_rows(back)
    back = [jnp.where(row8 < 6, value, result) for value, result in zip(back, results)]
    for x_device in range(x_devices):
        first = x_device * y_devices
        parts = exchange(back[first : first + x_rows], y_rows)
        for turn in range(y_devices):
            place = (first + turn) * RETURNED
            out_ref[place : place + 8, :] = parts[turn]
    tails = [tail_ref[x * x_devices : (x + 1) * x_devices, :] for x in range(x_rows)]
    tails = exchange(tails, y_rows)
    for turn in range(y_devices):
        out_ref[pl.ds(turn * RETURNED + 8, x_devices, stride=y_devices * RETURNED), :] = tails[turn]

    sums = sums[:, : 2 * units] + sums[:, 2 * units :]
    sums = sums[:16] + sums[16:]
    moved = jnp.concatenate([sums[5:7, units:], STEP_SIZE * sums[13:16, :units]], axis=0)
    packed = jnp.concatenate([sums[:5, units:], moved], axis=1)
    for device in range(x_devices * y_devices):
        place = device * RETURNED + SENT
        out_ref[place : place + 5, :] = packed


def unpack_kernel(
    cells,
    in_ref,
    velocity_ref,
    cotangent_ref,
    z_ref,
    new_ref,
    grad_ref,
    in_grad_ref,
    bias_grad_ref,
    out_grad_ref,
):
    _, x_rows, y_rows, z_length = velocity_ref.shape
    block = x_rows * y_rows
    groups = LANES // block
    devices = z_length // groups
    units = in_grad_ref.shape[1]
    fields = []
    for start in range(0, SENT, groups):
        parts = [
            in_ref[pl.ds(min(field, SENT - 1), devices, stride=RETURNED), :]
            for field in range(start, start + groups)
        ]
        turned = jnp.concatenate(exchange(parts, block), axis=0).T
        fields.extend(turned[turn * block : (turn + 1) * block] for turn in range(groups))
    shape = (3, x_rows, y_rows, z_length)
    forcing = jnp.concatenate(fields[6:9], axis=0).reshape(shape)
    new_ref[...] = velocity_ref[...] + STEP_SIZE * forcing
    back_z = times_table(jnp.concatenate(fields[3:6], axis=0), z_ref[...])
    back = jnp.concatenate(fields[:3], axis=0) + back_z
    grad_ref[...] = cotangent_ref[...] + back.reshape(shape)

    sums = in_ref[SENT : SENT + 5, :]
    for device in range(1, devices):
        place = device * RETURNED + SENT
        sums = sums + in_ref[place : place + 5, :]
    sums = sums / cells
    in_grad_ref[:5, :] = sums[:, :units]
    in_grad_ref[5:, :] = sums[:1, units:]
    bias_grad_ref[...] = sums[1:2, units:]
    out_grad_ref[...] = sums[2:, units:]


def on_device(kernel, shapes, scratch=(), **more):
    return pl.pallas_call(
        kernel,
        out_shape=[jax.ShapeDtypeStruct(shape, kind) for shape, kind in shapes],
        scratch_shapes=[*scratch],
        compiler_params=pltpu.CompilerParams(vmem_limit_bytes=32 * 1024 * 1024),
        **more,
    )


def fits(velocity, units):
    x_devices, y_devices = lax.axis_size("gx"), lax.axis_size("gy")
    _, x_rows, y_rows, z_length = velocity.shape
    return (
        z_length == LANES
        and x_rows * y_rows * LANES == LANES * LANES // 4
        and x_devices * y_devices * 4 == LANES
        and x_devices == 8
        and y_devices == x_rows
        and y_rows % 8 == 0
        and 2 * units == LANES
    )


def local_kernels(velocity, cotangent, weight_in, bias_in, weight_out):
    axes = ("gx", "gy")
    x_devices, y_devices = lax.axis_size("gx"), lax.axis_size("gy")
    devices = x_devices * y_devices
    _, x_rows, y_rows, z_length = velocity.shape
    units = weight_in.shape[1]
    cells = x_rows * x_devices * y_rows * y_devices * z_length
    z_table = derivative_table(z_length)
    y_table = np.kron(np.eye(z_length // devices), derivative_table(y_rows * y_devices))
    single, half = jnp.float32, jnp.bfloat16
    wide = len(LEFT_PIECES) * LANES

    arguments = [
        velocity,
        cotangent,
        split_table(z_table.T),
        weight_in,
        bias_in[None],
        weight_out.T,
        split_table(y_table.T),
        split_table(y_table),
    ]
    arguments = [pltpu.with_memory_space_constraint(each, pltpu.HBM) for each in arguments]
    sent, *prepared = on_device(
        pack_kernel,
        [
            ((devices * SENT, LANES), single),
            ((2 * units, LANES), half),
            ((48, 4 * units), half),
            ((wide, LANES), half),
            ((wide, LANES), half),
        ],
        [pltpu.VMEM(values.shape, values.dtype) for values in arguments[:6]]
        + [pltpu.SemaphoreType.DMA((len(arguments),))],
        in_specs=[pl.BlockSpec(memory_space=pltpu.HBM)] * len(arguments),
    )(*arguments)
    sent = sent.reshape(devices, 1, SENT * LANES)
    sent = lax.all_to_all(sent, axes, 0, 0, tiled=True).reshape(devices * SENT, LANES)
    (back,) = on_device(
        functools.partial(middle_kernel, x_devices),
        [((devices * RETURNED, LANES), single)],
        [pltpu.VMEM((x_devices * x_rows, LANES), single)],
    )(sent, *prepared)
    back = back.reshape(devices, 1, RETURNED * LANES)
    back = lax.all_to_all(back, axes, 0, 0, tiled=True).reshape(devices * RETURNED, LANES)
    shapes = [velocity.shape, velocity.shape, (6, units), (1, units), (3, units)]
    new, grad, grad_in, grad_bias, grad_out = on_device(
        functools.partial(unpack_kernel, float(cells)), [(shape, single) for shape in shapes]
    )(back, velocity, cotangent, split_table(z_table))
    return (new, grad, grad_in, grad_bias[0], grad_out.T)


def local(velocity, cotangent, weight_in, bias_in, weight_out):
    chosen = local_kernels if fits(velocity, weight_in.shape[1]) else local_plain
    return chosen(velocity, cotangent, weight_in, bias_in, weight_out)


def solution(mesh):
    in_specs = (P(None, "gx", "gy", None), P(None, "gx", "gy", None), P(), P(), P())
    out_specs = (P(None, "gx", "gy", None), P(None, "gx", "gy", None), P(), P(), P())
    return jax.shard_map(local, mesh=mesh, in_specs=in_specs, out_specs=out_specs, check_vma=False)
```

```python
import functools

import jax
import jax.numpy as jnp
import numpy as np
from jax import lax
from jax.experimental import pallas as pl
from jax.experimental.pallas import tpu as pltpu
from jax.sharding import PartitionSpec as P

FILTER_ALPHA = 0.499
FILTER_GAIN = 0.5 + FILTER_ALPHA
COMPACT_ALPHA = 1.0 / 3.0
STEP_SIZE = 0.5
PRECISE = lax.Precision.HIGHEST
LANES = 128
SENT = 9
RETURNED = 14
LEFT_PIECES = (0, 1, 0, 2, 1, 0)
RIGHT_PIECES = (0, 0, 1, 0, 1, 2)


def beside(length, offset):
    return np.eye(length, k=offset) + np.eye(length, k=-offset)


def smooth_table(length):
    left = np.eye(length) + FILTER_ALPHA * beside(length, 1)
    right = FILTER_GAIN * np.eye(length) + 0.5 * FILTER_GAIN * beside(length, 1)
    return np.linalg.solve(left, right)


def derivative_table(length):
    left = np.eye(length) + COMPACT_ALPHA * beside(length, 1)
    right = 7.0 / 9.0 * (np.eye(length, k=1) - np.eye(length, k=-1)) + 1.0 / 36.0 * (
        np.eye(length, k=2) - np.eye(length, k=-2)
    )
    return np.linalg.solve(left, right)


def table(values):
    return jnp.asarray(values.astype(np.float32))


def local_plain(velocity, cotangent, weight_in, bias_in, weight_out):
    axes = ("gx", "gy")
    x_devices, y_devices = lax.axis_size("gx"), lax.axis_size("gy")
    devices = x_devices * y_devices
    _, x_rows, y_rows, z_length = velocity.shape
    x_length, y_length = x_rows * x_devices, y_rows * y_devices
    units = weight_in.shape[1]
    z_rows = -(-z_length // devices)
    padding = z_rows * devices - z_length

    z_table = table(derivative_table(z_length))
    y_table = table(derivative_table(y_length))
    x_table = table(smooth_table(x_length))

    along_z = jnp.einsum("ab,kxyb->kxya", z_table, velocity, precision=PRECISE)
    fields = jnp.concatenate([velocity, along_z, cotangent], axis=0)
    fields = jnp.pad(fields, ((0, 0), (0, 0), (0, 0), (0, padding)))
    fields = fields.reshape(9, x_rows, y_rows, z_rows, devices)
    fields = fields.transpose(4, 0, 3, 1, 2).reshape(devices, 9, z_rows * x_rows * y_rows)
    fields = lax.all_to_all(fields, axes, 0, 0, tiled=True)
    fields = fields.reshape(x_devices, y_devices, 9, z_rows, x_rows, y_rows)
    fields = fields.transpose(2, 0, 4, 3, 1, 5).reshape(9, x_length, z_rows, y_length)

    smoothed = jnp.einsum("ab,kbzy->kazy", x_table, fields[:6], precision=PRECISE)
    along_y = jnp.einsum("ab,kxzb->kxza", y_table, smoothed[:3], precision=PRECISE)
    features = jnp.concatenate([along_y, smoothed[3:]], axis=0).reshape(6, -1)
    grad_out = STEP_SIZE * fields[6:].reshape(3, -1)

    hidden = jnp.tanh(jnp.dot(weight_in.T, features, precision=PRECISE) + bias_in[:, None])
    forcing = jnp.dot(weight_out.T, hidden, precision=PRECISE)
    grad_pre = jnp.dot(weight_out, grad_out, precision=PRECISE) * (1.0 - hidden * hidden)
    grad_features = jnp.dot(weight_in, grad_pre, precision=PRECISE)
    sum_in = jnp.dot(features, grad_pre.T, precision=PRECISE)
    sum_bias = jnp.sum(grad_pre, axis=1)
    sum_out = jnp.dot(grad_out, hidden.T, precision=PRECISE)

    grad_features = grad_features.reshape(6, x_length, z_rows, y_length)
    back_y = jnp.einsum("ba,kxzb->kxza", y_table, grad_features[:3], precision=PRECISE)
    back = jnp.concatenate([back_y, grad_features[3:]], axis=0)
    back = jnp.einsum("ab,kbzy->kazy", x_table, back, precision=PRECISE)
    back = jnp.concatenate([forcing.reshape(3, x_length, z_rows, y_length), back], axis=0)
    back = back.reshape(9, x_devices, x_rows, z_rows, y_devices, y_rows)
    back = back.transpose(1, 4, 0, 3, 2, 5).reshape(devices, -1)
    sums = jnp.concatenate([sum_in, sum_bias[None], sum_out], axis=0).reshape(1, -1)
    cells = back.shape[1]
    back = jnp.concatenate([back, jnp.broadcast_to(sums, (devices, 10 * units))], axis=1)
    back = lax.all_to_all(back, axes, 0, 0, tiled=True)

    sums = jnp.sum(back[:, cells:], axis=0).reshape(10, units)
    sums = sums / float(x_length * y_length * z_length)
    back = back[:, :cells].reshape(devices, 9, z_rows, x_rows, y_rows)
    back = back.transpose(1, 3, 4, 2, 0).reshape(9, x_rows, y_rows, -1)[..., :z_length]
    new_velocity = velocity + STEP_SIZE * back[:3]
    back_z = jnp.einsum("ba,kxyb->kxya", z_table, back[6:], precision=PRECISE)
    grad_velocity = cotangent + back[3:6] + back_z
    return (new_velocity, grad_velocity, sums[:6], sums[6], sums[7:].T)


def exchange(parts, width):
    parts = list(parts)
    lane = lax.broadcasted_iota(jnp.int32, parts[0].shape, 1)
    step = len(parts) // 2
    while step:
        shift = step * width
        upper = (lane & shift) != 0
        for low in range(len(parts)):
            if low & step == 0:
                first, second = parts[low], parts[low + step]
                parts[low] = jnp.where(upper, pltpu.roll(second, shift, 1), first)
                parts[low + step] = jnp.where(upper, second, pltpu.roll(first, LANES - shift, 1))
        step //= 2
    return parts


def solve_rows(rows):
    length = len(rows)
    half = length // 2
    scales = []
    before = 0.0
    for _ in range(half):
        scales.append(1.0 / (1.0 - FILTER_ALPHA * FILTER_ALPHA * before))
        before = scales[-1]
    solved = [None] * length
    for sign in (1, -1):
        order = range(half) if sign == 1 else range(length - 1, length - 1 - half, -1)
        last = None
        for turn, row in enumerate(order):
            value = rows[row] * scales[turn]
            if last is not None:
                value = value - last * (FILTER_ALPHA * scales[turn])
            solved[row] = last = value
    below, above = solved[half - 1], solved[half]
    ratio = FILTER_ALPHA * scales[half - 1]
    middle = 1.0 / (1.0 - ratio * ratio)
    solved[half - 1] = (below - ratio * above) * middle
    solved[half] = (above - ratio * below) * middle
    for turn in reversed(range(half - 1)):
        factor = FILTER_ALPHA * scales[turn]
        solved[turn] = solved[turn] - factor * solved[turn + 1]
        row = length - 1 - turn
        solved[row] = solved[row] - factor * solved[row - 1]
    return solved


def smooth_rows(rows):
    own = 0.5 * FILTER_GAIN / FILTER_ALPHA
    solved = solve_rows(rows)
    return [own * row + (FILTER_GAIN - own) * value for row, value in zip(rows, solved)]


def times(left, right, contract=(1, 0)):
    dims = (((contract[0],), (contract[1],)), ((), ()))
    return lax.dot_general(left, right, dims, preferred_element_type=jnp.float32)


def split(values, count):
    pieces = []
    for turn in range(count):
        pieces.append(values.astype(jnp.bfloat16))
        if turn + 1 < count:
            values = values - pieces[-1].astype(jnp.float32)
    return pieces


def times_table(values, square_table, turned=False):
    pieces = split(values, 3)
    left = jnp.concatenate([pieces[turn] for turn in LEFT_PIECES], axis=1)
    pieces = split(square_table, 3)
    axis = 1 if turned else 0
    right = jnp.concatenate([pieces[turn] for turn in RIGHT_PIECES], axis=axis)
    return times(left, right, (1, axis))


def pack_kernel(
    velocity_hbm,
    cotangent_hbm,
    z_hbm,
    weight_in_hbm,
    bias_hbm,
    weight_out_hbm,
    y_hbm,
    out_ref,
    before_ref,
    after_ref,
    y_ref,
    velocity_ref,
    cotangent_ref,
    z_ref,
    weight_in_ref,
    bias_ref,
    weight_out_ref,
    arrived,
):
    pairs = [
        (velocity_hbm, velocity_ref),
        (cotangent_hbm, cotangent_ref),
        (z_hbm, z_ref),
        (weight_in_hbm, weight_in_ref),
        (bias_hbm, bias_ref),
        (weight_out_hbm, weight_out_ref),
        (y_hbm, y_ref),
    ]
    copies = [
        pltpu.make_async_copy(source, target, arrived.at[turn])
        for turn, (source, target) in enumerate(pairs)
    ]
    for copy in copies:
        copy.start()
    for copy in copies:
        copy.wait()

    _, x_rows, y_rows, z_length = velocity_ref.shape
    block = x_rows * y_rows
    groups = LANES // block
    devices = z_length // groups
    velocity = velocity_ref[...].reshape(3 * block, z_length)
    cotangent = cotangent_ref[...].reshape(3 * block, z_length)
    along_z = times_table(velocity, z_ref[...], turned=True)
    fill = jnp.zeros(((-SENT % groups) * block, z_length), jnp.float32)
    rows = jnp.concatenate(
        [velocity, along_z, cotangent[block:], cotangent[:block], fill], axis=0
    )
    for start in range(0, SENT, groups):
        turned = rows[start * block : (start + groups) * block].T
        parts = [turned[group * devices : (group + 1) * devices] for group in range(groups)]
        parts = exchange(parts, block)
        for field in range(start, min(start + groups, SENT)):
            out_ref[pl.ds(field, devices, stride=SENT), :] = parts[field - start]

    weight_in = weight_in_ref[...]
    weight_out = weight_out_ref[...]
    units = weight_in.shape[1]
    zeros = functools.partial(jnp.zeros, dtype=jnp.float32)
    before = jnp.concatenate(
        [
            jnp.concatenate([weight_in, bias_ref[...], zeros((9, units))], axis=0),
            jnp.concatenate([zeros((13, units)), STEP_SIZE * weight_out], axis=0),
        ],
        axis=1,
    )
    after = jnp.concatenate(
        [
            jnp.concatenate([zeros((6, units)), weight_out, zeros((7, units))], axis=0),
            jnp.concatenate([weight_in, zeros((10, units))], axis=0),
        ],
        axis=1,
    )
    pieces = [piece.astype(jnp.float32) for piece in split(before, 3)]
    before = jnp.concatenate([pieces[turn] for turn in RIGHT_PIECES + (1, 2)], axis=0)
    before_ref[...] = before.T.astype(jnp.bfloat16)
    pieces = split(after, 3)
    after_ref[...] = jnp.concatenate(
        [
            jnp.concatenate([pieces[0], pieces[0]], axis=1),
            jnp.concatenate([pieces[1], pieces[1]], axis=1),
            jnp.concatenate([pieces[2], jnp.zeros_like(pieces[2])], axis=1),
        ],
        axis=0,
    )


def middle_kernel(x_devices, in_ref, before_ref, after_ref, y_ref, out_ref, tail_ref):
    y_devices = in_ref.shape[0] // SENT // x_devices
    x_rows = y_devices
    x_length = x_devices * x_rows
    units = before_ref.shape[0] // 2
    y_rows = LANES // y_devices // x_rows
    row8 = lax.broadcasted_iota(jnp.int32, (8, LANES), 0)

    planes = []
    for x_device in range(x_devices):
        first = x_device * y_devices
        parts = [
            in_ref[(first + turn) * SENT : (first + turn) * SENT + 8, :]
            for turn in range(y_devices)
        ]
        planes.extend(exchange(parts, y_rows))
    tails = [
        in_ref[pl.ds(turn * SENT + 8, x_devices, stride=y_devices * SENT), :]
        for turn in range(y_devices)
    ]
    tails = exchange(tails, y_rows)

    smoothed = smooth_rows(planes)
    along_y = times_table(jnp.concatenate(smoothed, axis=0), y_ref[...], turned=True)
    upper_rows = []
    lower_rows = []
    for x in range(x_length):
        features = jnp.where(row8 < 3, along_y[8 * x : 8 * x + 8], smoothed[x])
        features = jnp.where(row8 < 6, features, jnp.where(row8 == 6, 1.0, 0.0))
        last = tails[x % x_rows][x // x_rows : x // x_rows + 1]
        upper_rows.append(features)
        lower_rows.append(jnp.where(row8 == 5, last, planes[x]))

    before = before_ref[...]
    after = after_ref[...]
    at_once = 8
    sums = jnp.zeros((32, 4 * units), jnp.float32)
    results = []
    for start in range(0, x_length, at_once):
        stop = start + at_once
        cells = jnp.concatenate(
            [
                jnp.concatenate(upper_rows[start:stop], axis=1),
                jnp.concatenate(lower_rows[start:stop], axis=1),
            ],
            axis=0,
        )
        pieces = split(cells, 3)
        both = times(before, jnp.concatenate([pieces[turn] for turn in LEFT_PIECES + (2, 1)], axis=0))
        hidden = jnp.tanh(both[:units])
        grad_pre = both[units:] * (1.0 - hidden * hidden)
        both = jnp.concatenate([hidden, grad_pre], axis=0)
        both = jnp.concatenate(split(both, 2), axis=0)
        sums = sums + times(jnp.concatenate(pieces[:2], axis=0), both, (1, 1))
        result = times(after, both)
        result = result[:16] + result[16:32] + result[32:]
        for turn in range(at_once):
            results.append(result[:8, turn * LANES : (turn + 1) * LANES])
            x = start + turn
            place = (x % x_rows) * x_devices + x // x_rows
            tail_ref[place : place + 1, :] = result[8:9, turn * LANES : (turn + 1) * LANES]

    back_y = times_table(jnp.concatenate(results, axis=0), y_ref[...])
    back = [
        jnp.where(row8 < 3, back_y[8 * x : 8 * x + 8], results[x]) for x in range(x_length)
    ]
    back = smooth_rows(back)
    back = [jnp.where(row8 < 6, value, result) for value, result in zip(back, results)]
    for x_device in range(x_devices):
        first = x_device * y_devices
        parts = exchange(back[first : first + x_rows], y_rows)
        for turn in range(y_devices):
            place = (first + turn) * RETURNED
            out_ref[place : place + 8, :] = parts[turn]
    tails = [tail_ref[x * x_devices : (x + 1) * x_devices, :] for x in range(x_rows)]
    tails = exchange(tails, y_rows)
    for turn in range(y_devices):
        out_ref[pl.ds(turn * RETURNED + 8, x_devices, stride=y_devices * RETURNED), :] = tails[turn]

    sums = sums[:, : 2 * units] + sums[:, 2 * units :]
    sums = sums[:16] + sums[16:]
    moved = jnp.concatenate([sums[5:7, units:], STEP_SIZE * sums[13:16, :units]], axis=0)
    packed = jnp.concatenate([sums[:5, units:], moved], axis=1)
    for device in range(x_devices * y_devices):
        place = device * RETURNED + SENT
        out_ref[place : place + 5, :] = packed


def unpack_kernel(
    cells,
    in_ref,
    velocity_ref,
    cotangent_ref,
    z_ref,
    new_hbm,
    grad_hbm,
    in_grad_hbm,
    bias_grad_hbm,
    out_grad_hbm,
    new_ref,
    grad_ref,
    in_grad_ref,
    bias_grad_ref,
    out_grad_ref,
    arrived,
):
    pairs = [
        (new_ref, new_hbm),
        (grad_ref, grad_hbm),
        (in_grad_ref, in_grad_hbm),
        (bias_grad_ref, bias_grad_hbm),
        (out_grad_ref, out_grad_hbm),
    ]
    copies = [
        pltpu.make_async_copy(source, target, arrived.at[turn])
        for turn, (source, target) in enumerate(pairs)
    ]
    _, x_rows, y_rows, z_length = velocity_ref.shape
    block = x_rows * y_rows
    groups = LANES // block
    devices = z_length // groups
    units = in_grad_ref.shape[1]

    sums = [
        in_ref[device * RETURNED + SENT : device * RETURNED + SENT + 5, :]
        for device in range(devices)
    ]
    while len(sums) > 1:
        sums = [sum(sums[start : start + 2]) for start in range(0, len(sums), 2)]
    sums = sums[0] * (1.0 / cells)
    in_grad_ref[:5, :] = sums[:, :units]
    in_grad_ref[5:, :] = sums[:1, units:]
    bias_grad_ref[...] = sums[1:2, units:]
    out_grad_ref[...] = sums[2:, units:]
    for copy in copies[2:]:
        copy.start()

    fields = []
    for start in range(0, SENT, groups):
        parts = [
            in_ref[pl.ds(min(field, SENT - 1), devices, stride=RETURNED), :]
            for field in range(start, start + groups)
        ]
        turned = jnp.concatenate(exchange(parts, block), axis=0).T
        fields.extend(turned[turn * block : (turn + 1) * block] for turn in range(groups))
    shape = (3, x_rows, y_rows, z_length)
    forcing = jnp.concatenate(fields[6:9], axis=0).reshape(shape)
    back_z = times_table(jnp.concatenate(fields[3:6], axis=0), z_ref[...])
    new_ref[...] = velocity_ref[...] + STEP_SIZE * forcing
    copies[0].start()
    back = jnp.concatenate(fields[:3], axis=0) + back_z
    grad_ref[...] = cotangent_ref[...] + back.reshape(shape)
    copies[1].start()
    for copy in copies:
        copy.wait()


def on_device(kernel, shapes, scratch=(), **more):
    return pl.pallas_call(
        kernel,
        out_shape=[jax.ShapeDtypeStruct(shape, kind) for shape, kind in shapes],
        scratch_shapes=[*scratch],
        compiler_params=pltpu.CompilerParams(vmem_limit_bytes=32 * 1024 * 1024),
        **more,
    )


def fits(velocity, units):
    x_devices, y_devices = lax.axis_size("gx"), lax.axis_size("gy")
    _, x_rows, y_rows, z_length = velocity.shape
    return (
        z_length == LANES
        and x_rows * y_rows * LANES == LANES * LANES // 4
        and x_devices * y_devices * 4 == LANES
        and x_devices == 8
        and y_devices == x_rows
        and y_rows % 8 == 0
        and 2 * units == LANES
    )


def local_kernels(velocity, cotangent, weight_in, bias_in, weight_out):
    axes = ("gx", "gy")
    x_devices, y_devices = lax.axis_size("gx"), lax.axis_size("gy")
    devices = x_devices * y_devices
    _, x_rows, y_rows, z_length = velocity.shape
    units = weight_in.shape[1]
    cells = x_rows * x_devices * y_rows * y_devices * z_length
    z_table = derivative_table(z_length)
    y_table = np.kron(np.eye(z_length // devices), derivative_table(y_rows * y_devices))
    single, half = jnp.float32, jnp.bfloat16

    in_place = pl.BlockSpec(memory_space=pltpu.HBM)

    arguments = [
        velocity,
        cotangent,
        table(z_table),
        weight_in,
        bias_in[None],
        weight_out.T,
        table(y_table),
    ]
    arguments = [pltpu.with_memory_space_constraint(each, pltpu.HBM) for each in arguments]
    sent, *prepared = on_device(
        pack_kernel,
        [
            ((devices * SENT, LANES), single),
            ((2 * units, LANES), half),
            ((48, 4 * units), half),
            ((LANES, LANES), single),
        ],
        [pltpu.VMEM(values.shape, values.dtype) for values in arguments[:6]]
        + [pltpu.SemaphoreType.DMA((len(arguments),))],
        in_specs=[in_place] * len(arguments),
    )(*arguments)
    sent = sent.reshape(devices, 1, SENT * LANES)
    sent = lax.all_to_all(sent, axes, 0, 0, tiled=True).reshape(devices * SENT, LANES)
    (back,) = on_device(
        functools.partial(middle_kernel, x_devices),
        [((devices * RETURNED, LANES), single)],
        [pltpu.VMEM((x_devices * x_rows, LANES), single)],
    )(sent, *prepared)
    back = back.reshape(devices, 1, RETURNED * LANES)
    back = lax.all_to_all(back, axes, 0, 0, tiled=True).reshape(devices * RETURNED, LANES)
    shapes = [velocity.shape, velocity.shape, (6, units), (1, units), (3, units)]
    new, grad, grad_in, grad_bias, grad_out = on_device(
        functools.partial(unpack_kernel, float(cells)),
        [(shape, single) for shape in shapes],
        [pltpu.VMEM(shape, single) for shape in shapes]
        + [pltpu.SemaphoreType.DMA((len(shapes),))],
        out_specs=[in_place] * len(shapes),
    )(back, velocity, cotangent, table(z_table))
    return (new, grad, grad_in, grad_bias[0], grad_out.T)


def local(velocity, cotangent, weight_in, bias_in, weight_out):
    chosen = local_kernels if fits(velocity, weight_in.shape[1]) else local_plain
    return chosen(velocity, cotangent, weight_in, bias_in, weight_out)


def solution(mesh):
    in_specs = (P(None, "gx", "gy", None), P(None, "gx", "gy", None), P(), P(), P())
    out_specs = (P(None, "gx", "gy", None), P(None, "gx", "gy", None), P(), P(), P())
    return jax.shard_map(local, mesh=mesh, in_specs=in_specs, out_specs=out_specs, check_vma=False)
```

```python
import functools

import jax
import jax.numpy as jnp
import ml_dtypes
import numpy as np
from jax import lax
from jax.experimental import pallas as pl
from jax.experimental.pallas import tpu as pltpu
from jax.sharding import PartitionSpec as P

FILTER_ALPHA = 0.499
FILTER_GAIN = 0.5 + FILTER_ALPHA
COMPACT_ALPHA = 1.0 / 3.0
STEP_SIZE = 0.5
PRECISE = lax.Precision.HIGHEST
LANES = 128
SENT = 9
RETURNED = 14
LEFT_PIECES = (0, 1, 0, 2, 1, 0)
RIGHT_PIECES = (0, 0, 1, 0, 1, 2)


def beside(length, offset):
    return np.eye(length, k=offset) + np.eye(length, k=-offset)


def smooth_table(length):
    left = np.eye(length) + FILTER_ALPHA * beside(length, 1)
    right = FILTER_GAIN * np.eye(length) + 0.5 * FILTER_GAIN * beside(length, 1)
    return np.linalg.solve(left, right)


def derivative_table(length):
    left = np.eye(length) + COMPACT_ALPHA * beside(length, 1)
    right = 7.0 / 9.0 * (np.eye(length, k=1) - np.eye(length, k=-1)) + 1.0 / 36.0 * (
        np.eye(length, k=2) - np.eye(length, k=-2)
    )
    return np.linalg.solve(left, right)


def table(values):
    return jnp.asarray(values.astype(np.float32))


def split_table(values):
    pieces = []
    rest = values.astype(np.float32)
    for _ in range(3):
        pieces.append(rest.astype(ml_dtypes.bfloat16))
        rest = rest - pieces[-1].astype(np.float32)
    return jnp.asarray(np.concatenate([pieces[turn] for turn in RIGHT_PIECES], axis=0))


def local_plain(velocity, cotangent, weight_in, bias_in, weight_out):
    axes = ("gx", "gy")
    x_devices, y_devices = lax.axis_size("gx"), lax.axis_size("gy")
    devices = x_devices * y_devices
    _, x_rows, y_rows, z_length = velocity.shape
    x_length, y_length = x_rows * x_devices, y_rows * y_devices
    units = weight_in.shape[1]
    z_rows = -(-z_length // devices)
    padding = z_rows * devices - z_length

    z_table = table(derivative_table(z_length))
    y_table = table(derivative_table(y_length))
    x_table = table(smooth_table(x_length))

    along_z = jnp.einsum("ab,kxyb->kxya", z_table, velocity, precision=PRECISE)
    fields = jnp.concatenate([velocity, along_z, cotangent], axis=0)
    fields = jnp.pad(fields, ((0, 0), (0, 0), (0, 0), (0, padding)))
    fields = fields.reshape(9, x_rows, y_rows, z_rows, devices)
    fields = fields.transpose(4, 0, 3, 1, 2).reshape(devices, 9, z_rows * x_rows * y_rows)
    fields = lax.all_to_all(fields, axes, 0, 0, tiled=True)
    fields = fields.reshape(x_devices, y_devices, 9, z_rows, x_rows, y_rows)
    fields = fields.transpose(2, 0, 4, 3, 1, 5).reshape(9, x_length, z_rows, y_length)

    smoothed = jnp.einsum("ab,kbzy->kazy", x_table, fields[:6], precision=PRECISE)
    along_y = jnp.einsum("ab,kxzb->kxza", y_table, smoothed[:3], precision=PRECISE)
    features = jnp.concatenate([along_y, smoothed[3:]], axis=0).reshape(6, -1)
    grad_out = STEP_SIZE * fields[6:].reshape(3, -1)

    hidden = jnp.tanh(jnp.dot(weight_in.T, features, precision=PRECISE) + bias_in[:, None])
    forcing = jnp.dot(weight_out.T, hidden, precision=PRECISE)
    grad_pre = jnp.dot(weight_out, grad_out, precision=PRECISE) * (1.0 - hidden * hidden)
    grad_features = jnp.dot(weight_in, grad_pre, precision=PRECISE)
    sum_in = jnp.dot(features, grad_pre.T, precision=PRECISE)
    sum_bias = jnp.sum(grad_pre, axis=1)
    sum_out = jnp.dot(grad_out, hidden.T, precision=PRECISE)

    grad_features = grad_features.reshape(6, x_length, z_rows, y_length)
    back_y = jnp.einsum("ba,kxzb->kxza", y_table, grad_features[:3], precision=PRECISE)
    back = jnp.concatenate([back_y, grad_features[3:]], axis=0)
    back = jnp.einsum("ab,kbzy->kazy", x_table, back, precision=PRECISE)
    back = jnp.concatenate([forcing.reshape(3, x_length, z_rows, y_length), back], axis=0)
    back = back.reshape(9, x_devices, x_rows, z_rows, y_devices, y_rows)
    back = back.transpose(1, 4, 0, 3, 2, 5).reshape(devices, -1)
    sums = jnp.concatenate([sum_in, sum_bias[None], sum_out], axis=0).reshape(1, -1)
    cells = back.shape[1]
    back = jnp.concatenate([back, jnp.broadcast_to(sums, (devices, 10 * units))], axis=1)
    back = lax.all_to_all(back, axes, 0, 0, tiled=True)

    sums = jnp.sum(back[:, cells:], axis=0).reshape(10, units)
    sums = sums / float(x_length * y_length * z_length)
    back = back[:, :cells].reshape(devices, 9, z_rows, x_rows, y_rows)
    back = back.transpose(1, 3, 4, 2, 0).reshape(9, x_rows, y_rows, -1)[..., :z_length]
    new_velocity = velocity + STEP_SIZE * back[:3]
    back_z = jnp.einsum("ba,kxyb->kxya", z_table, back[6:], precision=PRECISE)
    grad_velocity = cotangent + back[3:6] + back_z
    return (new_velocity, grad_velocity, sums[:6], sums[6], sums[7:].T)


def exchange(parts, width):
    parts = list(parts)
    lane = lax.broadcasted_iota(jnp.int32, parts[0].shape, 1)
    step = len(parts) // 2
    while step:
        shift = step * width
        upper = (lane & shift) != 0
        for low in range(len(parts)):
            if low & step == 0:
                first, second = parts[low], parts[low + step]
                parts[low] = jnp.where(upper, pltpu.roll(second, shift, 1), first)
                parts[low + step] = jnp.where(upper, second, pltpu.roll(first, LANES - shift, 1))
        step //= 2
    return parts


def solve_rows(rows):
    length = len(rows)
    half = length // 2
    scales = []
    before = 0.0
    for _ in range(half):
        scales.append(1.0 / (1.0 - FILTER_ALPHA * FILTER_ALPHA * before))
        before = scales[-1]
    solved = [None] * length
    for sign in (1, -1):
        order = range(half) if sign == 1 else range(length - 1, length - 1 - half, -1)
        last = None
        for turn, row in enumerate(order):
            value = rows[row] * scales[turn]
            if last is not None:
                value = value - last * (FILTER_ALPHA * scales[turn])
            solved[row] = last = value
    below, above = solved[half - 1], solved[half]
    ratio = FILTER_ALPHA * scales[half - 1]
    middle = 1.0 / (1.0 - ratio * ratio)
    solved[half - 1] = (below - ratio * above) * middle
    solved[half] = (above - ratio * below) * middle
    for turn in reversed(range(half - 1)):
        factor = FILTER_ALPHA * scales[turn]
        solved[turn] = solved[turn] - factor * solved[turn + 1]
        row = length - 1 - turn
        solved[row] = solved[row] - factor * solved[row - 1]
    return solved


def smooth_rows(rows):
    own = 0.5 * FILTER_GAIN / FILTER_ALPHA
    solved = solve_rows(rows)
    return [own * row + (FILTER_GAIN - own) * value for row, value in zip(rows, solved)]


def times(left, right, contract=(1, 0)):
    dims = (((contract[0],), (contract[1],)), ((), ()))
    return lax.dot_general(left, right, dims, preferred_element_type=jnp.float32)


def split(values, count):
    pieces = []
    for turn in range(count):
        pieces.append(values.astype(jnp.bfloat16))
        if turn + 1 < count:
            values = values - pieces[-1].astype(jnp.float32)
    return pieces


def times_table(values, wide_table):
    pieces = split(values, 3)
    return times(jnp.concatenate([pieces[turn] for turn in LEFT_PIECES], axis=1), wide_table)


def widened(square_table):
    pieces = split(square_table, 3)
    return jnp.concatenate([pieces[turn] for turn in RIGHT_PIECES], axis=0)


def pack_kernel(
    velocity_hbm,
    cotangent_hbm,
    z_hbm,
    weight_in_hbm,
    bias_hbm,
    weight_out_hbm,
    out_ref,
    before_ref,
    after_ref,
    velocity_ref,
    cotangent_ref,
    z_ref,
    weight_in_ref,
    bias_ref,
    weight_out_ref,
    arrived,
):
    pairs = [
        (velocity_hbm, velocity_ref),
        (cotangent_hbm, cotangent_ref),
        (z_hbm, z_ref),
        (weight_in_hbm, weight_in_ref),
        (bias_hbm, bias_ref),
        (weight_out_hbm, weight_out_ref),
    ]
    copies = [
        pltpu.make_async_copy(source, target, arrived.at[turn])
        for turn, (source, target) in enumerate(pairs)
    ]
    for copy in copies:
        copy.start()
    for copy in copies:
        copy.wait()

    _, x_rows, y_rows, z_length = velocity_ref.shape
    block = x_rows * y_rows
    groups = LANES // block
    devices = z_length // groups
    velocity = velocity_ref[...].reshape(3 * block, z_length)
    cotangent = cotangent_ref[...].reshape(3 * block, z_length)
    along_z = times_table(velocity, widened(z_ref[...]))
    fill = jnp.zeros(((-SENT % groups) * block, z_length), jnp.float32)
    rows = jnp.concatenate(
        [velocity, along_z, cotangent[block:], cotangent[:block], fill], axis=0
    )
    for start in range(0, SENT, groups):
        turned = rows[start * block : (start + groups) * block].T
        parts = [turned[group * devices : (group + 1) * devices] for group in range(groups)]
        parts = exchange(parts, block)
        for field in range(start, min(start + groups, SENT)):
            out_ref[pl.ds(field, devices, stride=SENT), :] = parts[field - start]

    weight_in = weight_in_ref[...]
    weight_out = weight_out_ref[...]
    units = weight_in.shape[1]
    zeros = functools.partial(jnp.zeros, dtype=jnp.float32)
    before = jnp.concatenate(
        [
            jnp.concatenate([weight_in, bias_ref[...], zeros((9, units))], axis=0),
            jnp.concatenate([zeros((13, units)), STEP_SIZE * weight_out], axis=0),
        ],
        axis=1,
    )
    after = jnp.concatenate(
        [
            jnp.concatenate([zeros((6, units)), weight_out, zeros((7, units))], axis=0),
            jnp.concatenate([weight_in, zeros((10, units))], axis=0),
        ],
        axis=1,
    )
    pieces = [piece.astype(jnp.float32) for piece in split(before, 3)]
    before = jnp.concatenate([pieces[turn] for turn in RIGHT_PIECES + (1, 2)], axis=0)
    before_ref[...] = before.T.astype(jnp.bfloat16)
    pieces = split(after, 3)
    after_ref[...] = jnp.concatenate(
        [
            jnp.concatenate([pieces[0], pieces[0]], axis=1),
            jnp.concatenate([pieces[1], pieces[1]], axis=1),
            jnp.concatenate([pieces[2], jnp.zeros_like(pieces[2])], axis=1),
        ],
        axis=0,
    )


def middle_kernel(x_devices, in_ref, before_ref, after_ref, y_ref, y_back_ref, out_ref, tail_ref):
    y_devices = in_ref.shape[0] // SENT // x_devices
    x_rows = y_devices
    x_length = x_devices * x_rows
    units = before_ref.shape[0] // 2
    y_rows = LANES // y_devices // x_rows
    row8 = lax.broadcasted_iota(jnp.int32, (8, LANES), 0)

    planes = []
    for x_device in range(x_devices):
        places = [(turn * x_devices + x_device) * SENT for turn in range(y_devices)]
        parts = [in_ref[place : place + 8, :] for place in places]
        planes.extend(exchange(parts, y_rows))
    tails = [
        in_ref[pl.ds(turn * x_devices * SENT + 8, x_devices, stride=SENT), :]
        for turn in range(y_devices)
    ]
    tails = exchange(tails, y_rows)

    smoothed = smooth_rows(planes)
    along_y = times_table(jnp.concatenate(smoothed, axis=0), y_ref[...])
    upper_rows = []
    lower_rows = []
    for x in range(x_length):
        features = jnp.where(row8 < 3, along_y[8 * x : 8 * x + 8], smoothed[x])
        features = jnp.where(row8 < 6, features, jnp.where(row8 == 6, 1.0, 0.0))
        last = tails[x % x_rows][x // x_rows : x // x_rows + 1]
        upper_rows.append(features)
        lower_rows.append(jnp.where(row8 == 5, last, planes[x]))

    before = before_ref[...]
    after = after_ref[...]
    at_once = 8
    sums = jnp.zeros((32, 4 * units), jnp.float32)
    results = []
    for start in range(0, x_length, at_once):
        stop = start + at_once
        cells = jnp.concatenate(
            [
                jnp.concatenate(upper_rows[start:stop], axis=1),
                jnp.concatenate(lower_rows[start:stop], axis=1),
            ],
            axis=0,
        )
        pieces = split(cells, 3)
        both = times(before, jnp.concatenate([pieces[turn] for turn in LEFT_PIECES + (2, 1)], axis=0))
        hidden = jnp.tanh(both[:units])
        grad_pre = both[units:] * (1.0 - hidden * hidden)
        both = jnp.concatenate([hidden, grad_pre], axis=0)
        both = jnp.concatenate(split(both, 2), axis=0)
        sums = sums + times(jnp.concatenate(pieces[:2], axis=0), both, (1, 1))
        result = times(after, both)
        result = result[:16] + result[16:32] + result[32:]
        for turn in range(at_once):
            results.append(result[:8, turn * LANES : (turn + 1) * LANES])
            x = start + turn
            place = (x % x_rows) * x_devices + x // x_rows
            tail_ref[place : place + 1, :] = result[8:9, turn * LANES : (turn + 1) * LANES]

    back_y = times_table(jnp.concatenate(results, axis=0), y_back_ref[...])
    back = [
        jnp.where(row8 < 3, back_y[8 * x : 8 * x + 8], results[x]) for x in range(x_length)
    ]
    back = smooth_rows(back)
    back = [jnp.where(row8 < 6, value, result) for value, result in zip(back, results)]
    for x_device in range(x_devices):
        first = x_device * x_rows
        parts = exchange(back[first : first + x_rows], y_rows)
        for turn in range(y_devices):
            place = (turn * x_devices + x_device) * RETURNED
            out_ref[place : place + 8, :] = parts[turn]
    tails = [tail_ref[x * x_devices : (x + 1) * x_devices, :] for x in range(x_rows)]
    tails = exchange(tails, y_rows)
    for turn in range(y_devices):
        place = turn * x_devices * RETURNED + 8
        out_ref[pl.ds(place, x_devices, stride=RETURNED), :] = tails[turn]

    sums = sums[:, : 2 * units] + sums[:, 2 * units :]
    sums = sums[:16] + sums[16:]
    moved = jnp.concatenate([sums[5:7, units:], STEP_SIZE * sums[13:16, :units]], axis=0)
    packed = jnp.concatenate([sums[:5, units:], moved], axis=1)
    for device in range(x_devices * y_devices):
        place = device * RETURNED + SENT
        out_ref[place : place + 5, :] = packed


def unpack_kernel(
    cells,
    in_ref,
    velocity_ref,
    cotangent_ref,
    z_ref,
    new_ref,
    grad_ref,
    in_grad_ref,
    bias_grad_ref,
    out_grad_ref,
):
    _, x_rows, y_rows, z_length = velocity_ref.shape
    block = x_rows * y_rows
    groups = LANES // block
    devices = z_length // groups
    units = in_grad_ref.shape[1]
    fields = []
    for start in range(0, SENT, groups):
        parts = [
            in_ref[pl.ds(min(field, SENT - 1), devices, stride=RETURNED), :]
            for field in range(start, start + groups)
        ]
        turned = jnp.concatenate(exchange(parts, block), axis=0).T
        fields.extend(turned[turn * block : (turn + 1) * block] for turn in range(groups))
    shape = (3, x_rows, y_rows, z_length)
    forcing = jnp.concatenate(fields[6:9], axis=0).reshape(shape)
    new_ref[...] = velocity_ref[...] + STEP_SIZE * forcing
    back_z = times_table(jnp.concatenate(fields[3:6], axis=0), z_ref[...])
    back = jnp.concatenate(fields[:3], axis=0) + back_z
    grad_ref[...] = cotangent_ref[...] + back.reshape(shape)

    sums = in_ref[SENT : SENT + 5, :]
    for device in range(1, devices):
        place = device * RETURNED + SENT
        sums = sums + in_ref[place : place + 5, :]
    sums = sums * (1.0 / cells)
    in_grad_ref[:5, :] = sums[:, :units]
    in_grad_ref[5:, :] = sums[:1, units:]
    bias_grad_ref[...] = sums[1:2, units:]
    out_grad_ref[...] = sums[2:, units:]


def on_device(kernel, shapes, scratch=(), **more):
    return pl.pallas_call(
        kernel,
        out_shape=[jax.ShapeDtypeStruct(shape, kind) for shape, kind in shapes],
        scratch_shapes=[*scratch],
        compiler_params=pltpu.CompilerParams(vmem_limit_bytes=32 * 1024 * 1024),
        **more,
    )


def fits(velocity, units):
    x_devices, y_devices = lax.axis_size("gx"), lax.axis_size("gy")
    _, x_rows, y_rows, z_length = velocity.shape
    return (
        z_length == LANES
        and x_rows * y_rows * LANES == LANES * LANES // 4
        and x_devices * y_devices * 4 == LANES
        and x_devices == 8
        and y_devices == x_rows
        and y_rows % 8 == 0
        and 2 * units == LANES
    )


def local_kernels(velocity, cotangent, weight_in, bias_in, weight_out):
    axes = ("gy", "gx")
    x_devices, y_devices = lax.axis_size("gx"), lax.axis_size("gy")
    devices = x_devices * y_devices
    _, x_rows, y_rows, z_length = velocity.shape
    units = weight_in.shape[1]
    cells = x_rows * x_devices * y_rows * y_devices * z_length
    z_table = derivative_table(z_length)
    y_table = np.kron(np.eye(z_length // devices), derivative_table(y_rows * y_devices))
    single, half = jnp.float32, jnp.bfloat16

    in_place = pl.BlockSpec(memory_space=pltpu.HBM)

    arguments = [
        velocity,
        cotangent,
        table(z_table.T),
        weight_in,
        bias_in[None],
        weight_out.T,
    ]
    arguments = [pltpu.with_memory_space_constraint(each, pltpu.HBM) for each in arguments]
    sent, *prepared = on_device(
        pack_kernel,
        [
            ((devices * SENT, LANES), single),
            ((2 * units, LANES), half),
            ((48, 4 * units), half),
        ],
        [pltpu.VMEM(values.shape, values.dtype) for values in arguments]
        + [pltpu.SemaphoreType.DMA((len(arguments),))],
        in_specs=[in_place] * len(arguments),
    )(*arguments)
    sent = sent.reshape(devices, 1, SENT * LANES)
    sent = lax.all_to_all(sent, axes, 0, 0, tiled=True).reshape(devices * SENT, LANES)
    (back,) = on_device(
        functools.partial(middle_kernel, x_devices),
        [((devices * RETURNED, LANES), single)],
        [pltpu.VMEM((x_devices * x_rows, LANES), single)],
    )(sent, *prepared, split_table(y_table.T), split_table(y_table))
    back = back.reshape(devices, 1, RETURNED * LANES)
    back = lax.all_to_all(back, axes, 0, 0, tiled=True).reshape(devices * RETURNED, LANES)
    shapes = [velocity.shape, velocity.shape, (6, units), (1, units), (3, units)]
    new, grad, grad_in, grad_bias, grad_out = on_device(
        functools.partial(unpack_kernel, float(cells)), [(shape, single) for shape in shapes]
    )(back, velocity, cotangent, split_table(z_table))
    return (new, grad, grad_in, grad_bias[0], grad_out.T)


def local(velocity, cotangent, weight_in, bias_in, weight_out):
    chosen = local_kernels if fits(velocity, weight_in.shape[1]) else local_plain
    return chosen(velocity, cotangent, weight_in, bias_in, weight_out)


def solution(mesh):
    in_specs = (P(None, "gx", "gy", None), P(None, "gx", "gy", None), P(), P(), P())
    out_specs = (P(None, "gx", "gy", None), P(None, "gx", "gy", None), P(), P(), P())
    return jax.shard_map(local, mesh=mesh, in_specs=in_specs, out_specs=out_specs, check_vma=False)
```

```python
import functools

import jax
import jax.numpy as jnp
import ml_dtypes
import numpy as np
from jax import lax
from jax.experimental import pallas as pl
from jax.experimental.pallas import tpu as pltpu
from jax.sharding import PartitionSpec as P

FILTER_ALPHA = 0.499
FILTER_GAIN = 0.5 + FILTER_ALPHA
COMPACT_ALPHA = 1.0 / 3.0
STEP_SIZE = 0.5
PRECISE = lax.Precision.HIGHEST
LANES = 128
SENT = 9
RETURNED = 14
LEFT_PIECES = (0, 1, 0, 2, 1, 0)
RIGHT_PIECES = (0, 0, 1, 0, 1, 2)


def beside(length, offset):
    return np.eye(length, k=offset) + np.eye(length, k=-offset)


def smooth_table(length):
    left = np.eye(length) + FILTER_ALPHA * beside(length, 1)
    right = FILTER_GAIN * np.eye(length) + 0.5 * FILTER_GAIN * beside(length, 1)
    return np.linalg.solve(left, right)


def derivative_table(length):
    left = np.eye(length) + COMPACT_ALPHA * beside(length, 1)
    right = 7.0 / 9.0 * (np.eye(length, k=1) - np.eye(length, k=-1)) + 1.0 / 36.0 * (
        np.eye(length, k=2) - np.eye(length, k=-2)
    )
    return np.linalg.solve(left, right)


def table(values):
    return jnp.asarray(values.astype(np.float32))


def split_table(values):
    pieces = []
    rest = values.astype(np.float32)
    for _ in range(3):
        pieces.append(rest.astype(ml_dtypes.bfloat16))
        rest = rest - pieces[-1].astype(np.float32)
    return jnp.asarray(np.concatenate([pieces[turn] for turn in RIGHT_PIECES], axis=0))


def local_plain(velocity, cotangent, weight_in, bias_in, weight_out):
    axes = ("gx", "gy")
    x_devices, y_devices = lax.axis_size("gx"), lax.axis_size("gy")
    devices = x_devices * y_devices
    _, x_rows, y_rows, z_length = velocity.shape
    x_length, y_length = x_rows * x_devices, y_rows * y_devices
    units = weight_in.shape[1]
    z_rows = -(-z_length // devices)
    padding = z_rows * devices - z_length

    z_table = table(derivative_table(z_length))
    y_table = table(derivative_table(y_length))
    x_table = table(smooth_table(x_length))

    along_z = jnp.einsum("ab,kxyb->kxya", z_table, velocity, precision=PRECISE)
    fields = jnp.concatenate([velocity, along_z, cotangent], axis=0)
    fields = jnp.pad(fields, ((0, 0), (0, 0), (0, 0), (0, padding)))
    fields = fields.reshape(9, x_rows, y_rows, z_rows, devices)
    fields = fields.transpose(4, 0, 3, 1, 2).reshape(devices, 9, z_rows * x_rows * y_rows)
    fields = lax.all_to_all(fields, axes, 0, 0, tiled=True)
    fields = fields.reshape(x_devices, y_devices, 9, z_rows, x_rows, y_rows)
    fields = fields.transpose(2, 0, 4, 3, 1, 5).reshape(9, x_length, z_rows, y_length)

    smoothed = jnp.einsum("ab,kbzy->kazy", x_table, fields[:6], precision=PRECISE)
    along_y = jnp.einsum("ab,kxzb->kxza", y_table, smoothed[:3], precision=PRECISE)
    features = jnp.concatenate([along_y, smoothed[3:]], axis=0).reshape(6, -1)
    grad_out = STEP_SIZE * fields[6:].reshape(3, -1)

    hidden = jnp.tanh(jnp.dot(weight_in.T, features, precision=PRECISE) + bias_in[:, None])
    forcing = jnp.dot(weight_out.T, hidden, precision=PRECISE)
    grad_pre = jnp.dot(weight_out, grad_out, precision=PRECISE) * (1.0 - hidden * hidden)
    grad_features = jnp.dot(weight_in, grad_pre, precision=PRECISE)
    sum_in = jnp.dot(features, grad_pre.T, precision=PRECISE)
    sum_bias = jnp.sum(grad_pre, axis=1)
    sum_out = jnp.dot(grad_out, hidden.T, precision=PRECISE)

    grad_features = grad_features.reshape(6, x_length, z_rows, y_length)
    back_y = jnp.einsum("ba,kxzb->kxza", y_table, grad_features[:3], precision=PRECISE)
    back = jnp.concatenate([back_y, grad_features[3:]], axis=0)
    back = jnp.einsum("ab,kbzy->kazy", x_table, back, precision=PRECISE)
    back = jnp.concatenate([forcing.reshape(3, x_length, z_rows, y_length), back], axis=0)
    back = back.reshape(9, x_devices, x_rows, z_rows, y_devices, y_rows)
    back = back.transpose(1, 4, 0, 3, 2, 5).reshape(devices, -1)
    sums = jnp.concatenate([sum_in, sum_bias[None], sum_out], axis=0).reshape(1, -1)
    cells = back.shape[1]
    back = jnp.concatenate([back, jnp.broadcast_to(sums, (devices, 10 * units))], axis=1)
    back = lax.all_to_all(back, axes, 0, 0, tiled=True)

    sums = jnp.sum(back[:, cells:], axis=0).reshape(10, units)
    sums = sums / float(x_length * y_length * z_length)
    back = back[:, :cells].reshape(devices, 9, z_rows, x_rows, y_rows)
    back = back.transpose(1, 3, 4, 2, 0).reshape(9, x_rows, y_rows, -1)[..., :z_length]
    new_velocity = velocity + STEP_SIZE * back[:3]
    back_z = jnp.einsum("ba,kxyb->kxya", z_table, back[6:], precision=PRECISE)
    grad_velocity = cotangent + back[3:6] + back_z
    return (new_velocity, grad_velocity, sums[:6], sums[6], sums[7:].T)


def exchange(parts, width):
    parts = list(parts)
    lane = lax.broadcasted_iota(jnp.int32, parts[0].shape, 1)
    step = len(parts) // 2
    while step:
        shift = step * width
        upper = (lane & shift) != 0
        for low in range(len(parts)):
            if low & step == 0:
                first, second = parts[low], parts[low + step]
                parts[low] = jnp.where(upper, pltpu.roll(second, shift, 1), first)
                parts[low + step] = jnp.where(upper, second, pltpu.roll(first, LANES - shift, 1))
        step //= 2
    return parts


def solve_rows(rows):
    length = len(rows)
    half = length // 2
    scales = []
    before = 0.0
    for _ in range(half):
        scales.append(1.0 / (1.0 - FILTER_ALPHA * FILTER_ALPHA * before))
        before = scales[-1]
    solved = [None] * length
    for sign in (1, -1):
        order = range(half) if sign == 1 else range(length - 1, length - 1 - half, -1)
        last = None
        for turn, row in enumerate(order):
            value = rows[row] * scales[turn]
            if last is not None:
                value = value - last * (FILTER_ALPHA * scales[turn])
            solved[row] = last = value
    below, above = solved[half - 1], solved[half]
    ratio = FILTER_ALPHA * scales[half - 1]
    middle = 1.0 / (1.0 - ratio * ratio)
    solved[half - 1] = (below - ratio * above) * middle
    solved[half] = (above - ratio * below) * middle
    for turn in reversed(range(half - 1)):
        factor = FILTER_ALPHA * scales[turn]
        solved[turn] = solved[turn] - factor * solved[turn + 1]
        row = length - 1 - turn
        solved[row] = solved[row] - factor * solved[row - 1]
    return solved


def smooth_rows(rows):
    own = 0.5 * FILTER_GAIN / FILTER_ALPHA
    solved = solve_rows(rows)
    return [own * row + (FILTER_GAIN - own) * value for row, value in zip(rows, solved)]


def times(left, right, contract=(1, 0)):
    dims = (((contract[0],), (contract[1],)), ((), ()))
    return lax.dot_general(left, right, dims, preferred_element_type=jnp.float32)


def split(values, count):
    pieces = []
    for turn in range(count):
        pieces.append(values.astype(jnp.bfloat16))
        if turn + 1 < count:
            values = values - pieces[-1].astype(jnp.float32)
    return pieces


def times_table(values, wide_table):
    pieces = split(values, 3)
    return times(jnp.concatenate([pieces[turn] for turn in LEFT_PIECES], axis=1), wide_table)


def widened(square_table):
    pieces = split(square_table, 3)
    return jnp.concatenate([pieces[turn] for turn in RIGHT_PIECES], axis=0)


def pack_kernel(
    velocity_hbm, cotangent_hbm, z_hbm, out_ref, velocity_ref, cotangent_ref, z_ref, arrived
):
    pairs = [(velocity_hbm, velocity_ref), (cotangent_hbm, cotangent_ref), (z_hbm, z_ref)]
    copies = [
        pltpu.make_async_copy(source, target, arrived.at[turn])
        for turn, (source, target) in enumerate(pairs)
    ]
    for copy in copies:
        copy.start()
    for copy in copies:
        copy.wait()

    _, x_rows, y_rows, z_length = velocity_ref.shape
    block = x_rows * y_rows
    groups = LANES // block
    devices = z_length // groups
    velocity = velocity_ref[...].reshape(3 * block, z_length)
    cotangent = cotangent_ref[...].reshape(3 * block, z_length)
    along_z = times_table(velocity, widened(z_ref[...]))
    fill = jnp.zeros(((-SENT % groups) * block, z_length), jnp.float32)
    rows = jnp.concatenate(
        [velocity, along_z, cotangent[block:], cotangent[:block], fill], axis=0
    )
    for start in range(0, SENT, groups):
        turned = rows[start * block : (start + groups) * block].T
        parts = [turned[group * devices : (group + 1) * devices] for group in range(groups)]
        parts = exchange(parts, block)
        for field in range(start, min(start + groups, SENT)):
            out_ref[pl.ds(field, devices, stride=SENT), :] = parts[field - start]


def prepare_kernel(weight_in_ref, bias_ref, weight_out_ref, before_ref, after_ref):
    weight_in = weight_in_ref[...]
    weight_out = weight_out_ref[...]
    units = weight_in.shape[1]
    zeros = functools.partial(jnp.zeros, dtype=jnp.float32)
    before = jnp.concatenate(
        [
            jnp.concatenate([weight_in, bias_ref[...], zeros((9, units))], axis=0),
            jnp.concatenate([zeros((13, units)), STEP_SIZE * weight_out], axis=0),
        ],
        axis=1,
    )
    after = jnp.concatenate(
        [
            jnp.concatenate([zeros((6, units)), weight_out, zeros((7, units))], axis=0),
            jnp.concatenate([weight_in, zeros((10, units))], axis=0),
        ],
        axis=1,
    )
    pieces = [piece.astype(jnp.float32) for piece in split(before, 3)]
    before = jnp.concatenate([pieces[turn] for turn in RIGHT_PIECES + (1, 2)], axis=0)
    before_ref[...] = before.T.astype(jnp.bfloat16)
    pieces = split(after, 3)
    after_ref[...] = jnp.concatenate(
        [
            jnp.concatenate([pieces[0], pieces[0]], axis=1),
            jnp.concatenate([pieces[1], pieces[1]], axis=1),
            jnp.concatenate([pieces[2], jnp.zeros_like(pieces[2])], axis=1),
        ],
        axis=0,
    )


def middle_kernel(x_devices, in_ref, before_ref, after_ref, y_ref, y_back_ref, out_ref, tail_ref):
    y_devices = in_ref.shape[0] // SENT // x_devices
    x_rows = y_devices
    x_length = x_devices * x_rows
    units = before_ref.shape[0] // 2
    y_rows = LANES // y_devices // x_rows
    row8 = lax.broadcasted_iota(jnp.int32, (8, LANES), 0)

    planes = []
    for x_device in range(x_devices):
        places = [(turn * x_devices + x_device) * SENT for turn in range(y_devices)]
        parts = [in_ref[place : place + 8, :] for place in places]
        planes.extend(exchange(parts, y_rows))
    tails = [
        in_ref[pl.ds(turn * x_devices * SENT + 8, x_devices, stride=SENT), :]
        for turn in range(y_devices)
    ]
    tails = exchange(tails, y_rows)

    smoothed = smooth_rows(planes)
    along_y = times_table(jnp.concatenate(smoothed, axis=0), y_ref[...])
    upper_rows = []
    lower_rows = []
    for x in range(x_length):
        features = jnp.where(row8 < 3, along_y[8 * x : 8 * x + 8], smoothed[x])
        features = jnp.where(row8 < 6, features, jnp.where(row8 == 6, 1.0, 0.0))
        last = tails[x % x_rows][x // x_rows : x // x_rows + 1]
        upper_rows.append(features)
        lower_rows.append(jnp.where(row8 == 5, last, planes[x]))

    before = before_ref[...]
    after = after_ref[...]
    at_once = 8
    sums = jnp.zeros((32, 4 * units), jnp.float32)
    results = []
    for start in range(0, x_length, at_once):
        stop = start + at_once
        cells = jnp.concatenate(
            [
                jnp.concatenate(upper_rows[start:stop], axis=1),
                jnp.concatenate(lower_rows[start:stop], axis=1),
            ],
            axis=0,
        )
        pieces = split(cells, 3)
        both = times(before, jnp.concatenate([pieces[turn] for turn in LEFT_PIECES + (2, 1)], axis=0))
        hidden = jnp.tanh(both[:units])
        grad_pre = both[units:] * (1.0 - hidden * hidden)
        both = jnp.concatenate([hidden, grad_pre], axis=0)
        both = jnp.concatenate(split(both, 2), axis=0)
        sums = sums + times(jnp.concatenate(pieces[:2], axis=0), both, (1, 1))
        result = times(after, both)
        result = result[:16] + result[16:32] + result[32:]
        for turn in range(at_once):
            results.append(result[:8, turn * LANES : (turn + 1) * LANES])
            x = start + turn
            place = (x % x_rows) * x_devices + x // x_rows
            tail_ref[place : place + 1, :] = result[8:9, turn * LANES : (turn + 1) * LANES]

    back_y = times_table(jnp.concatenate(results, axis=0), y_back_ref[...])
    back = [
        jnp.where(row8 < 3, back_y[8 * x : 8 * x + 8], results[x]) for x in range(x_length)
    ]
    back = smooth_rows(back)
    back = [jnp.where(row8 < 6, value, result) for value, result in zip(back, results)]
    for x_device in range(x_devices):
        first = x_device * x_rows
        parts = exchange(back[first : first + x_rows], y_rows)
        for turn in range(y_devices):
            place = (turn * x_devices + x_device) * RETURNED
            out_ref[place : place + 8, :] = parts[turn]
    tails = [tail_ref[x * x_devices : (x + 1) * x_devices, :] for x in range(x_rows)]
    tails = exchange(tails, y_rows)
    for turn in range(y_devices):
        place = turn * x_devices * RETURNED + 8
        out_ref[pl.ds(place, x_devices, stride=RETURNED), :] = tails[turn]

    sums = sums[:, : 2 * units] + sums[:, 2 * units :]
    sums = sums[:16] + sums[16:]
    moved = jnp.concatenate([sums[5:7, units:], STEP_SIZE * sums[13:16, :units]], axis=0)
    packed = jnp.concatenate([sums[:5, units:], moved], axis=1)
    for device in range(x_devices * y_devices):
        place = device * RETURNED + SENT
        out_ref[place : place + 5, :] = packed


def unpack_kernel(
    cells,
    in_ref,
    velocity_ref,
    cotangent_ref,
    z_ref,
    new_ref,
    grad_ref,
    in_grad_ref,
    bias_grad_ref,
    out_grad_ref,
):
    _, x_rows, y_rows, z_length = velocity_ref.shape
    block = x_rows * y_rows
    groups = LANES // block
    devices = z_length // groups
    units = in_grad_ref.shape[1]
    fields = []
    for start in range(0, SENT, groups):
        parts = [
            in_ref[pl.ds(min(field, SENT - 1), devices, stride=RETURNED), :]
            for field in range(start, start + groups)
        ]
        turned = jnp.concatenate(exchange(parts, block), axis=0).T
        fields.extend(turned[turn * block : (turn + 1) * block] for turn in range(groups))
    shape = (3, x_rows, y_rows, z_length)
    forcing = jnp.concatenate(fields[6:9], axis=0).reshape(shape)
    new_ref[...] = velocity_ref[...] + STEP_SIZE * forcing
    back_z = times_table(jnp.concatenate(fields[3:6], axis=0), z_ref[...])
    back = jnp.concatenate(fields[:3], axis=0) + back_z
    grad_ref[...] = cotangent_ref[...] + back.reshape(shape)

    sums = in_ref[SENT : SENT + 5, :]
    for device in range(1, devices):
        place = device * RETURNED + SENT
        sums = sums + in_ref[place : place + 5, :]
    sums = sums * (1.0 / cells)
    in_grad_ref[:5, :] = sums[:, :units]
    in_grad_ref[5:, :] = sums[:1, units:]
    bias_grad_ref[...] = sums[1:2, units:]
    out_grad_ref[...] = sums[2:, units:]


def on_device(kernel, shapes, scratch=(), **more):
    return pl.pallas_call(
        kernel,
        out_shape=[jax.ShapeDtypeStruct(shape, kind) for shape, kind in shapes],
        scratch_shapes=[*scratch],
        compiler_params=pltpu.CompilerParams(vmem_limit_bytes=32 * 1024 * 1024),
        **more,
    )


def fits(velocity, units):
    x_devices, y_devices = lax.axis_size("gx"), lax.axis_size("gy")
    _, x_rows, y_rows, z_length = velocity.shape
    return (
        z_length == LANES
        and x_rows * y_rows * LANES == LANES * LANES // 4
        and x_devices * y_devices * 4 == LANES
        and x_devices == 8
        and y_devices == x_rows
        and y_rows % 8 == 0
        and 2 * units == LANES
    )


def local_kernels(velocity, cotangent, weight_in, bias_in, weight_out):
    axes = ("gy", "gx")
    x_devices, y_devices = lax.axis_size("gx"), lax.axis_size("gy")
    devices = x_devices * y_devices
    _, x_rows, y_rows, z_length = velocity.shape
    units = weight_in.shape[1]
    cells = x_rows * x_devices * y_rows * y_devices * z_length
    z_table = derivative_table(z_length)
    y_table = np.kron(np.eye(z_length // devices), derivative_table(y_rows * y_devices))
    single, half = jnp.float32, jnp.bfloat16

    arguments = [velocity, cotangent, table(z_table.T)]
    arguments = [pltpu.with_memory_space_constraint(each, pltpu.HBM) for each in arguments]
    (sent,) = on_device(
        pack_kernel,
        [((devices * SENT, LANES), single)],
        [pltpu.VMEM(values.shape, values.dtype) for values in arguments]
        + [pltpu.SemaphoreType.DMA((len(arguments),))],
        in_specs=[pl.BlockSpec(memory_space=pltpu.HBM)] * len(arguments),
    )(*arguments)
    prepared = on_device(
        prepare_kernel,
        [((2 * units, LANES), half), ((48, 4 * units), half)],
        cost_estimate=pl.CostEstimate(flops=1 << 22, bytes_accessed=1 << 20, transcendentals=0),
    )(weight_in, bias_in[None], weight_out.T)
    sent = sent.reshape(devices, 1, SENT * LANES)
    sent = lax.all_to_all(sent, axes, 0, 0, tiled=True).reshape(devices * SENT, LANES)
    (back,) = on_device(
        functools.partial(middle_kernel, x_devices),
        [((devices * RETURNED, LANES), single)],
        [pltpu.VMEM((x_devices * x_rows, LANES), single)],
    )(sent, *prepared, split_table(y_table.T), split_table(y_table))
    back = back.reshape(devices, 1, RETURNED * LANES)
    back = lax.all_to_all(back, axes, 0, 0, tiled=True).reshape(devices * RETURNED, LANES)
    shapes = [velocity.shape, velocity.shape, (6, units), (1, units), (3, units)]
    new, grad, grad_in, grad_bias, grad_out = on_device(
        functools.partial(unpack_kernel, float(cells)), [(shape, single) for shape in shapes]
    )(back, velocity, cotangent, split_table(z_table))
    return (new, grad, grad_in, grad_bias[0], grad_out.T)


def local(velocity, cotangent, weight_in, bias_in, weight_out):
    chosen = local_kernels if fits(velocity, weight_in.shape[1]) else local_plain
    return chosen(velocity, cotangent, weight_in, bias_in, weight_out)


def solution(mesh):
    in_specs = (P(None, "gx", "gy", None), P(None, "gx", "gy", None), P(), P(), P())
    out_specs = (P(None, "gx", "gy", None), P(None, "gx", "gy", None), P(), P(), P())
    return jax.shard_map(local, mesh=mesh, in_specs=in_specs, out_specs=out_specs, check_vma=False)
```

```python
import functools

import jax
import jax.numpy as jnp
import ml_dtypes
import numpy as np
from jax import lax
from jax.experimental import pallas as pl
from jax.experimental.pallas import tpu as pltpu
from jax.sharding import PartitionSpec as P

FILTER_ALPHA = 0.499
FILTER_GAIN = 0.5 + FILTER_ALPHA
COMPACT_ALPHA = 1.0 / 3.0
STEP_SIZE = 0.5
PRECISE = lax.Precision.HIGHEST
LANES = 128
SENT = 9
RETURNED = 14
LEFT_PIECES = (0, 1, 0, 2, 1, 0)
RIGHT_PIECES = (0, 0, 1, 0, 1, 2)


def beside(length, offset):
    return np.eye(length, k=offset) + np.eye(length, k=-offset)


def smooth_table(length):
    left = np.eye(length) + FILTER_ALPHA * beside(length, 1)
    right = FILTER_GAIN * np.eye(length) + 0.5 * FILTER_GAIN * beside(length, 1)
    return np.linalg.solve(left, right)


def derivative_table(length):
    left = np.eye(length) + COMPACT_ALPHA * beside(length, 1)
    right = 7.0 / 9.0 * (np.eye(length, k=1) - np.eye(length, k=-1)) + 1.0 / 36.0 * (
        np.eye(length, k=2) - np.eye(length, k=-2)
    )
    return np.linalg.solve(left, right)


def table(values):
    return jnp.asarray(values.astype(np.float32))


def split_table(values):
    pieces = []
    rest = values.astype(np.float32)
    for _ in range(3):
        pieces.append(rest.astype(ml_dtypes.bfloat16))
        rest = rest - pieces[-1].astype(np.float32)
    return jnp.asarray(np.concatenate([pieces[turn] for turn in RIGHT_PIECES], axis=0))


def local_plain(velocity, cotangent, weight_in, bias_in, weight_out):
    axes = ("gx", "gy")
    x_devices, y_devices = lax.axis_size("gx"), lax.axis_size("gy")
    devices = x_devices * y_devices
    _, x_rows, y_rows, z_length = velocity.shape
    x_length, y_length = x_rows * x_devices, y_rows * y_devices
    units = weight_in.shape[1]
    z_rows = -(-z_length // devices)
    padding = z_rows * devices - z_length

    z_table = table(derivative_table(z_length))
    y_table = table(derivative_table(y_length))
    x_table = table(smooth_table(x_length))

    along_z = jnp.einsum("ab,kxyb->kxya", z_table, velocity, precision=PRECISE)
    fields = jnp.concatenate([velocity, along_z, cotangent], axis=0)
    fields = jnp.pad(fields, ((0, 0), (0, 0), (0, 0), (0, padding)))
    fields = fields.reshape(9, x_rows, y_rows, z_rows, devices)
    fields = fields.transpose(4, 0, 3, 1, 2).reshape(devices, 9, z_rows * x_rows * y_rows)
    fields = lax.all_to_all(fields, axes, 0, 0, tiled=True)
    fields = fields.reshape(x_devices, y_devices, 9, z_rows, x_rows, y_rows)
    fields = fields.transpose(2, 0, 4, 3, 1, 5).reshape(9, x_length, z_rows, y_length)

    smoothed = jnp.einsum("ab,kbzy->kazy", x_table, fields[:6], precision=PRECISE)
    along_y = jnp.einsum("ab,kxzb->kxza", y_table, smoothed[:3], precision=PRECISE)
    features = jnp.concatenate([along_y, smoothed[3:]], axis=0).reshape(6, -1)
    grad_out = STEP_SIZE * fields[6:].reshape(3, -1)

    hidden = jnp.tanh(jnp.dot(weight_in.T, features, precision=PRECISE) + bias_in[:, None])
    forcing = jnp.dot(weight_out.T, hidden, precision=PRECISE)
    grad_pre = jnp.dot(weight_out, grad_out, precision=PRECISE) * (1.0 - hidden * hidden)
    grad_features = jnp.dot(weight_in, grad_pre, precision=PRECISE)
    sum_in = jnp.dot(features, grad_pre.T, precision=PRECISE)
    sum_bias = jnp.sum(grad_pre, axis=1)
    sum_out = jnp.dot(grad_out, hidden.T, precision=PRECISE)

    grad_features = grad_features.reshape(6, x_length, z_rows, y_length)
    back_y = jnp.einsum("ba,kxzb->kxza", y_table, grad_features[:3], precision=PRECISE)
    back = jnp.concatenate([back_y, grad_features[3:]], axis=0)
    back = jnp.einsum("ab,kbzy->kazy", x_table, back, precision=PRECISE)
    back = jnp.concatenate([forcing.reshape(3, x_length, z_rows, y_length), back], axis=0)
    back = back.reshape(9, x_devices, x_rows, z_rows, y_devices, y_rows)
    back = back.transpose(1, 4, 0, 3, 2, 5).reshape(devices, -1)
    sums = jnp.concatenate([sum_in, sum_bias[None], sum_out], axis=0).reshape(1, -1)
    cells = back.shape[1]
    back = jnp.concatenate([back, jnp.broadcast_to(sums, (devices, 10 * units))], axis=1)
    back = lax.all_to_all(back, axes, 0, 0, tiled=True)

    sums = jnp.sum(back[:, cells:], axis=0).reshape(10, units)
    sums = sums / float(x_length * y_length * z_length)
    back = back[:, :cells].reshape(devices, 9, z_rows, x_rows, y_rows)
    back = back.transpose(1, 3, 4, 2, 0).reshape(9, x_rows, y_rows, -1)[..., :z_length]
    new_velocity = velocity + STEP_SIZE * back[:3]
    back_z = jnp.einsum("ba,kxyb->kxya", z_table, back[6:], precision=PRECISE)
    grad_velocity = cotangent + back[3:6] + back_z
    return (new_velocity, grad_velocity, sums[:6], sums[6], sums[7:].T)


def exchange(parts, width):
    parts = list(parts)
    lane = lax.broadcasted_iota(jnp.int32, parts[0].shape, 1)
    step = len(parts) // 2
    while step:
        shift = step * width
        upper = (lane & shift) != 0
        for low in range(len(parts)):
            if low & step == 0:
                first, second = parts[low], parts[low + step]
                parts[low] = jnp.where(upper, pltpu.roll(second, shift, 1), first)
                parts[low + step] = jnp.where(upper, second, pltpu.roll(first, LANES - shift, 1))
        step //= 2
    return parts


def smooth_rows(rows):
    length = len(rows)
    half = length // 2
    scales = []
    before = 0.0
    for _ in range(half):
        scales.append(1.0 / (1.0 - FILTER_ALPHA * FILTER_ALPHA * before))
        before = scales[-1]
    factors = [-FILTER_ALPHA * scale for scale in scales]
    forward = np.cumprod([1.0] + factors[1:])
    backward = np.cumprod([1.0] + factors[-2::-1])[::-1]
    own = 0.5 * FILTER_GAIN / FILTER_ALPHA

    sides = [list(range(half)), list(range(length - 1, half - 1, -1))]
    running = []
    for side in sides:
        sums = []
        for turn, row in enumerate(side):
            value = rows[row] * float(scales[turn] / forward[turn])
            sums.append(value if turn == 0 else sums[-1] + value)
        running.append(sums)
    middle = forward[-1] / (1.0 - factors[-1] * factors[-1])
    cross = middle * factors[-1]
    smoothed = [None] * length
    for side, sums, others in zip(sides, running, running[::-1]):
        value = float(middle) * sums[-1] + float(cross) * others[-1]
        for turn in reversed(range(half)):
            if turn < half - 1:
                value = value + float(forward[turn] / backward[turn]) * sums[turn]
            row = side[turn]
            smoothed[row] = own * rows[row] + float((FILTER_GAIN - own) * backward[turn]) * value
    return smoothed


def times(left, right, contract=(1, 0)):
    dims = (((contract[0],), (contract[1],)), ((), ()))
    return lax.dot_general(left, right, dims, preferred_element_type=jnp.float32)


def split(values, count):
    pieces = []
    for turn in range(count):
        pieces.append(values.astype(jnp.bfloat16))
        if turn + 1 < count:
            values = values - pieces[-1].astype(jnp.float32)
    return pieces


def times_table(values, wide_table):
    pieces = split(values, 3)
    return times(jnp.concatenate([pieces[turn] for turn in LEFT_PIECES], axis=1), wide_table)


def widened(square_table):
    pieces = split(square_table, 3)
    return jnp.concatenate([pieces[turn] for turn in RIGHT_PIECES], axis=0)


def pack_kernel(
    velocity_hbm,
    cotangent_hbm,
    z_hbm,
    weight_in_hbm,
    bias_hbm,
    weight_out_hbm,
    out_ref,
    before_ref,
    after_ref,
    velocity_ref,
    cotangent_ref,
    z_ref,
    weight_in_ref,
    bias_ref,
    weight_out_ref,
    arrived,
):
    pairs = [
        (weight_in_hbm, weight_in_ref),
        (bias_hbm, bias_ref),
        (weight_out_hbm, weight_out_ref),
        (velocity_hbm, velocity_ref),
        (cotangent_hbm, cotangent_ref),
        (z_hbm, z_ref),
    ]
    copies = [
        pltpu.make_async_copy(source, target, arrived.at[turn])
        for turn, (source, target) in enumerate(pairs)
    ]
    for copy in copies:
        copy.start()

    for copy in copies[:3]:
        copy.wait()
    weight_in = weight_in_ref[...]
    weight_out = weight_out_ref[...]
    units = weight_in.shape[1]
    zeros = functools.partial(jnp.zeros, dtype=jnp.float32)
    before = jnp.concatenate(
        [
            jnp.concatenate([weight_in, bias_ref[...], zeros((9, units))], axis=0),
            jnp.concatenate([zeros((13, units)), STEP_SIZE * weight_out], axis=0),
        ],
        axis=1,
    )
    after = jnp.concatenate(
        [
            jnp.concatenate([zeros((6, units)), weight_out, zeros((7, units))], axis=0),
            jnp.concatenate([weight_in, zeros((10, units))], axis=0),
        ],
        axis=1,
    )
    pieces = [piece.astype(jnp.float32) for piece in split(before, 3)]
    before = jnp.concatenate([pieces[turn] for turn in RIGHT_PIECES + (1, 2)], axis=0)
    before_ref[...] = before.T.astype(jnp.bfloat16)
    pieces = split(after, 3)
    after_ref[...] = jnp.concatenate(
        [
            jnp.concatenate([pieces[0], pieces[0]], axis=1),
            jnp.concatenate([pieces[1], pieces[1]], axis=1),
            jnp.concatenate([pieces[2], jnp.zeros_like(pieces[2])], axis=1),
        ],
        axis=0,
    )

    for copy in copies[3:]:
        copy.wait()
    _, x_rows, y_rows, z_length = velocity_ref.shape
    block = x_rows * y_rows
    groups = LANES // block
    devices = z_length // groups
    velocity = velocity_ref[...].reshape(3 * block, z_length)
    cotangent = cotangent_ref[...].reshape(3 * block, z_length)
    along_z = times_table(velocity, widened(z_ref[...]))
    fill = jnp.zeros(((-SENT % groups) * block, z_length), jnp.float32)
    rows = jnp.concatenate(
        [velocity, along_z, cotangent[block:], cotangent[:block], fill], axis=0
    )
    for start in range(0, SENT, groups):
        turned = rows[start * block : (start + groups) * block].T
        parts = [turned[group * devices : (group + 1) * devices] for group in range(groups)]
        parts = exchange(parts, block)
        for field in range(start, min(start + groups, SENT)):
            out_ref[pl.ds(field, devices, stride=SENT), :] = parts[field - start]


def middle_kernel(x_devices, in_ref, before_ref, after_ref, y_ref, y_back_ref, out_ref, tail_ref):
    y_devices = in_ref.shape[0] // SENT // x_devices
    x_rows = y_devices
    x_length = x_devices * x_rows
    units = before_ref.shape[0] // 2
    y_rows = LANES // y_devices // x_rows
    row8 = lax.broadcasted_iota(jnp.int32, (8, LANES), 0)

    planes = []
    for x_device in range(x_devices):
        places = [(turn * x_devices + x_device) * SENT for turn in range(y_devices)]
        parts = [in_ref[place : place + 8, :] for place in places]
        planes.extend(exchange(parts, y_rows))
    tails = [
        in_ref[pl.ds(turn * x_devices * SENT + 8, x_devices, stride=SENT), :]
        for turn in range(y_devices)
    ]
    tails = exchange(tails, y_rows)

    smoothed = smooth_rows(planes)
    along_y = times_table(jnp.concatenate(smoothed, axis=0), y_ref[...])
    upper_rows = []
    lower_rows = []
    for x in range(x_length):
        features = jnp.where(row8 < 3, along_y[8 * x : 8 * x + 8], smoothed[x])
        features = jnp.where(row8 < 6, features, jnp.where(row8 == 6, 1.0, 0.0))
        last = tails[x % x_rows][x // x_rows : x // x_rows + 1]
        upper_rows.append(features)
        lower_rows.append(jnp.where(row8 == 5, last, planes[x]))

    before = before_ref[...]
    after = after_ref[...]
    at_once = 8
    sums = jnp.zeros((32, 4 * units), jnp.float32)
    results = []
    for start in range(0, x_length, at_once):
        stop = start + at_once
        cells = jnp.concatenate(
            [
                jnp.concatenate(upper_rows[start:stop], axis=1),
                jnp.concatenate(lower_rows[start:stop], axis=1),
            ],
            axis=0,
        )
        pieces = split(cells, 3)
        both = times(before, jnp.concatenate([pieces[turn] for turn in LEFT_PIECES + (2, 1)], axis=0))
        hidden = jnp.tanh(both[:units])
        grad_pre = both[units:] * (1.0 - hidden * hidden)
        both = jnp.concatenate([hidden, grad_pre], axis=0)
        both = jnp.concatenate(split(both, 2), axis=0)
        sums = sums + times(jnp.concatenate(pieces[:2], axis=0), both, (1, 1))
        result = times(after, both)
        result = result[:16] + result[16:32] + result[32:]
        for turn in range(at_once):
            results.append(result[:8, turn * LANES : (turn + 1) * LANES])
            x = start + turn
            place = (x % x_rows) * x_devices + x // x_rows
            tail_ref[place : place + 1, :] = result[8:9, turn * LANES : (turn + 1) * LANES]

    back_y = times_table(jnp.concatenate(results, axis=0), y_back_ref[...])
    back = [
        jnp.where(row8 < 3, back_y[8 * x : 8 * x + 8], results[x]) for x in range(x_length)
    ]
    back = smooth_rows(back)
    back = [jnp.where(row8 < 6, value, result) for value, result in zip(back, results)]
    for x_device in range(x_devices):
        first = x_device * x_rows
        parts = exchange(back[first : first + x_rows], y_rows)
        for turn in range(y_devices):
            place = (turn * x_devices + x_device) * RETURNED
            out_ref[place : place + 8, :] = parts[turn]
    tails = [tail_ref[x * x_devices : (x + 1) * x_devices, :] for x in range(x_rows)]
    tails = exchange(tails, y_rows)
    for turn in range(y_devices):
        place = turn * x_devices * RETURNED + 8
        out_ref[pl.ds(place, x_devices, stride=RETURNED), :] = tails[turn]

    sums = sums[:, : 2 * units] + sums[:, 2 * units :]
    sums = sums[:16] + sums[16:]
    moved = jnp.concatenate([sums[5:7, units:], STEP_SIZE * sums[13:16, :units]], axis=0)
    packed = jnp.concatenate([sums[:5, units:], moved], axis=1)
    for device in range(x_devices * y_devices):
        place = device * RETURNED + SENT
        out_ref[place : place + 5, :] = packed


def unpack_kernel(
    cells,
    in_ref,
    velocity_ref,
    cotangent_ref,
    z_ref,
    new_hbm,
    grad_hbm,
    in_grad_hbm,
    bias_grad_hbm,
    out_grad_hbm,
    new_ref,
    grad_ref,
    in_grad_ref,
    bias_grad_ref,
    out_grad_ref,
    arrived,
):
    pairs = [
        (new_ref, new_hbm),
        (grad_ref, grad_hbm),
        (in_grad_ref, in_grad_hbm),
        (bias_grad_ref, bias_grad_hbm),
        (out_grad_ref, out_grad_hbm),
    ]
    copies = [
        pltpu.make_async_copy(source, target, arrived.at[turn])
        for turn, (source, target) in enumerate(pairs)
    ]
    _, x_rows, y_rows, z_length = velocity_ref.shape
    block = x_rows * y_rows
    groups = LANES // block
    devices = z_length // groups
    units = in_grad_ref.shape[1]

    fields = []
    for start in range(0, SENT, groups):
        parts = [
            in_ref[pl.ds(min(field, SENT - 1), devices, stride=RETURNED), :]
            for field in range(start, start + groups)
        ]
        turned = jnp.concatenate(exchange(parts, block), axis=0).T
        fields.extend(turned[turn * block : (turn + 1) * block] for turn in range(groups))
    shape = (3, x_rows, y_rows, z_length)
    forcing = jnp.concatenate(fields[6:9], axis=0).reshape(shape)
    back_z = times_table(jnp.concatenate(fields[3:6], axis=0), z_ref[...])
    new_ref[...] = velocity_ref[...] + STEP_SIZE * forcing
    copies[0].start()
    back = jnp.concatenate(fields[:3], axis=0) + back_z
    grad_ref[...] = cotangent_ref[...] + back.reshape(shape)
    copies[1].start()
    sums = [
        in_ref[device * RETURNED + SENT : device * RETURNED + SENT + 5, :]
        for device in range(devices)
    ]
    while len(sums) > 1:
        sums = [one + other for one, other in zip(sums[::2], sums[1::2])]
    sums = sums[0] * (1.0 / cells)
    in_grad_ref[:5, :] = sums[:, :units]
    in_grad_ref[5:, :] = sums[:1, units:]
    bias_grad_ref[...] = sums[1:2, units:]
    out_grad_ref[...] = sums[2:, units:]
    for copy in copies[2:]:
        copy.start()
    for copy in copies:
        copy.wait()


def on_device(kernel, shapes, scratch=(), **more):
    return pl.pallas_call(
        kernel,
        out_shape=[jax.ShapeDtypeStruct(shape, kind) for shape, kind in shapes],
        scratch_shapes=[*scratch],
        compiler_params=pltpu.CompilerParams(vmem_limit_bytes=32 * 1024 * 1024),
        **more,
    )


def fits(velocity, units):
    x_devices, y_devices = lax.axis_size("gx"), lax.axis_size("gy")
    _, x_rows, y_rows, z_length = velocity.shape
    return (
        z_length == LANES
        and x_rows * y_rows * LANES == LANES * LANES // 4
        and x_devices * y_devices * 4 == LANES
        and x_devices == 8
        and y_devices == x_rows
        and y_rows % 8 == 0
        and 2 * units == LANES
    )


def local_kernels(velocity, cotangent, weight_in, bias_in, weight_out):
    axes = ("gy", "gx")
    x_devices, y_devices = lax.axis_size("gx"), lax.axis_size("gy")
    devices = x_devices * y_devices
    _, x_rows, y_rows, z_length = velocity.shape
    units = weight_in.shape[1]
    cells = x_rows * x_devices * y_rows * y_devices * z_length
    z_table = derivative_table(z_length)
    y_table = np.kron(np.eye(z_length // devices), derivative_table(y_rows * y_devices))
    single, half = jnp.float32, jnp.bfloat16

    in_place = pl.BlockSpec(memory_space=pltpu.HBM)

    arguments = [
        velocity,
        cotangent,
        table(z_table.T),
        weight_in,
        bias_in[None],
        weight_out.T,
    ]
    arguments = [pltpu.with_memory_space_constraint(each, pltpu.HBM) for each in arguments]
    sent, *prepared = on_device(
        pack_kernel,
        [
            ((devices * SENT, LANES), single),
            ((2 * units, LANES), half),
            ((48, 4 * units), half),
        ],
        [pltpu.VMEM(values.shape, values.dtype) for values in arguments]
        + [pltpu.SemaphoreType.DMA((len(arguments),))],
        in_specs=[in_place] * len(arguments),
    )(*arguments)
    sent = sent.reshape(devices, 1, SENT * LANES)
    sent = lax.all_to_all(sent, axes, 0, 0, tiled=True).reshape(devices * SENT, LANES)
    (back,) = on_device(
        functools.partial(middle_kernel, x_devices),
        [((devices * RETURNED, LANES), single)],
        [pltpu.VMEM((x_devices * x_rows, LANES), single)],
    )(sent, *prepared, split_table(y_table.T), split_table(y_table))
    back = back.reshape(devices, 1, RETURNED * LANES)
    back = lax.all_to_all(back, axes, 0, 0, tiled=True).reshape(devices * RETURNED, LANES)
    shapes = [velocity.shape, velocity.shape, (6, units), (1, units), (3, units)]
    new, grad, grad_in, grad_bias, grad_out = on_device(
        functools.partial(unpack_kernel, float(cells)),
        [(shape, single) for shape in shapes],
        [pltpu.VMEM(shape, single) for shape in shapes]
        + [pltpu.SemaphoreType.DMA((len(shapes),))],
        out_specs=[in_place] * len(shapes),
    )(back, velocity, cotangent, split_table(z_table))
    return (new, grad, grad_in, grad_bias[0], grad_out.T)


def local(velocity, cotangent, weight_in, bias_in, weight_out):
    chosen = local_kernels if fits(velocity, weight_in.shape[1]) else local_plain
    return chosen(velocity, cotangent, weight_in, bias_in, weight_out)


def solution(mesh):
    in_specs = (P(None, "gx", "gy", None), P(None, "gx", "gy", None), P(), P(), P())
    out_specs = (P(None, "gx", "gy", None), P(None, "gx", "gy", None), P(), P(), P())
    return jax.shard_map(local, mesh=mesh, in_specs=in_specs, out_specs=out_specs, check_vma=False)
```

```python
import functools

import jax
import jax.numpy as jnp
import ml_dtypes
import numpy as np
from jax import lax
from jax.experimental import pallas as pl
from jax.experimental.pallas import tpu as pltpu
from jax.sharding import PartitionSpec as P

FILTER_ALPHA = 0.499
FILTER_GAIN = 0.5 + FILTER_ALPHA
COMPACT_ALPHA = 1.0 / 3.0
STEP_SIZE = 0.5
PRECISE = lax.Precision.HIGHEST
LANES = 128
SENT = 9
RETURNED = 14
LEFT_PIECES = (0, 1, 0, 2, 1, 0)
RIGHT_PIECES = (0, 0, 1, 0, 1, 2)


def beside(length, offset):
    return np.eye(length, k=offset) + np.eye(length, k=-offset)


def smooth_table(length):
    left = np.eye(length) + FILTER_ALPHA * beside(length, 1)
    right = FILTER_GAIN * np.eye(length) + 0.5 * FILTER_GAIN * beside(length, 1)
    return np.linalg.solve(left, right)


def derivative_table(length):
    left = np.eye(length) + COMPACT_ALPHA * beside(length, 1)
    right = 7.0 / 9.0 * (np.eye(length, k=1) - np.eye(length, k=-1)) + 1.0 / 36.0 * (
        np.eye(length, k=2) - np.eye(length, k=-2)
    )
    return np.linalg.solve(left, right)


def table(values):
    return jnp.asarray(values.astype(np.float32))


def split_table(values):
    pieces = []
    rest = values.astype(np.float32)
    for _ in range(3):
        pieces.append(rest.astype(ml_dtypes.bfloat16))
        rest = rest - pieces[-1].astype(np.float32)
    return jnp.asarray(np.concatenate([pieces[turn] for turn in RIGHT_PIECES], axis=0))


def local_plain(velocity, cotangent, weight_in, bias_in, weight_out):
    axes = ("gx", "gy")
    x_devices, y_devices = lax.axis_size("gx"), lax.axis_size("gy")
    devices = x_devices * y_devices
    _, x_rows, y_rows, z_length = velocity.shape
    x_length, y_length = x_rows * x_devices, y_rows * y_devices
    units = weight_in.shape[1]
    z_rows = -(-z_length // devices)
    padding = z_rows * devices - z_length

    z_table = table(derivative_table(z_length))
    y_table = table(derivative_table(y_length))
    x_table = table(smooth_table(x_length))

    along_z = jnp.einsum("ab,kxyb->kxya", z_table, velocity, precision=PRECISE)
    fields = jnp.concatenate([velocity, along_z, cotangent], axis=0)
    fields = jnp.pad(fields, ((0, 0), (0, 0), (0, 0), (0, padding)))
    fields = fields.reshape(9, x_rows, y_rows, z_rows, devices)
    fields = fields.transpose(4, 0, 3, 1, 2).reshape(devices, 9, z_rows * x_rows * y_rows)
    fields = lax.all_to_all(fields, axes, 0, 0, tiled=True)
    fields = fields.reshape(x_devices, y_devices, 9, z_rows, x_rows, y_rows)
    fields = fields.transpose(2, 0, 4, 3, 1, 5).reshape(9, x_length, z_rows, y_length)

    smoothed = jnp.einsum("ab,kbzy->kazy", x_table, fields[:6], precision=PRECISE)
    along_y = jnp.einsum("ab,kxzb->kxza", y_table, smoothed[:3], precision=PRECISE)
    features = jnp.concatenate([along_y, smoothed[3:]], axis=0).reshape(6, -1)
    grad_out = STEP_SIZE * fields[6:].reshape(3, -1)

    hidden = jnp.tanh(jnp.dot(weight_in.T, features, precision=PRECISE) + bias_in[:, None])
    forcing = jnp.dot(weight_out.T, hidden, precision=PRECISE)
    grad_pre = jnp.dot(weight_out, grad_out, precision=PRECISE) * (1.0 - hidden * hidden)
    grad_features = jnp.dot(weight_in, grad_pre, precision=PRECISE)
    sum_in = jnp.dot(features, grad_pre.T, precision=PRECISE)
    sum_bias = jnp.sum(grad_pre, axis=1)
    sum_out = jnp.dot(grad_out, hidden.T, precision=PRECISE)

    grad_features = grad_features.reshape(6, x_length, z_rows, y_length)
    back_y = jnp.einsum("ba,kxzb->kxza", y_table, grad_features[:3], precision=PRECISE)
    back = jnp.concatenate([back_y, grad_features[3:]], axis=0)
    back = jnp.einsum("ab,kbzy->kazy", x_table, back, precision=PRECISE)
    back = jnp.concatenate([forcing.reshape(3, x_length, z_rows, y_length), back], axis=0)
    back = back.reshape(9, x_devices, x_rows, z_rows, y_devices, y_rows)
    back = back.transpose(1, 4, 0, 3, 2, 5).reshape(devices, -1)
    sums = jnp.concatenate([sum_in, sum_bias[None], sum_out], axis=0).reshape(1, -1)
    cells = back.shape[1]
    back = jnp.concatenate([back, jnp.broadcast_to(sums, (devices, 10 * units))], axis=1)
    back = lax.all_to_all(back, axes, 0, 0, tiled=True)

    sums = jnp.sum(back[:, cells:], axis=0).reshape(10, units)
    sums = sums / float(x_length * y_length * z_length)
    back = back[:, :cells].reshape(devices, 9, z_rows, x_rows, y_rows)
    back = back.transpose(1, 3, 4, 2, 0).reshape(9, x_rows, y_rows, -1)[..., :z_length]
    new_velocity = velocity + STEP_SIZE * back[:3]
    back_z = jnp.einsum("ba,kxyb->kxya", z_table, back[6:], precision=PRECISE)
    grad_velocity = cotangent + back[3:6] + back_z
    return (new_velocity, grad_velocity, sums[:6], sums[6], sums[7:].T)


def exchange(parts, width):
    parts = list(parts)
    lane = lax.broadcasted_iota(jnp.int32, parts[0].shape, 1)
    step = len(parts) // 2
    while step:
        shift = step * width
        upper = (lane & shift) != 0
        for low in range(len(parts)):
            if low & step == 0:
                first, second = parts[low], parts[low + step]
                parts[low] = jnp.where(upper, pltpu.roll(second, shift, 1), first)
                parts[low + step] = jnp.where(upper, second, pltpu.roll(first, LANES - shift, 1))
        step //= 2
    return parts


def smooth_rows(rows):
    length = len(rows)
    half = length // 2
    scales = []
    before = 0.0
    for _ in range(half):
        scales.append(1.0 / (1.0 - FILTER_ALPHA * FILTER_ALPHA * before))
        before = scales[-1]
    factors = [-FILTER_ALPHA * scale for scale in scales]
    forward = np.cumprod([1.0] + factors[1:])
    backward = np.cumprod([1.0] + factors[-2::-1])[::-1]
    own = 0.5 * FILTER_GAIN / FILTER_ALPHA

    sides = [list(range(half)), list(range(length - 1, half - 1, -1))]
    running = []
    for side in sides:
        sums = []
        for turn, row in enumerate(side):
            value = rows[row] * float(scales[turn] / forward[turn])
            sums.append(value if turn == 0 else sums[-1] + value)
        running.append(sums)
    middle = forward[-1] / (1.0 - factors[-1] * factors[-1])
    cross = middle * factors[-1]
    smoothed = [None] * length
    for side, sums, others in zip(sides, running, running[::-1]):
        value = float(middle) * sums[-1] + float(cross) * others[-1]
        for turn in reversed(range(half)):
            if turn < half - 1:
                value = value + float(forward[turn] / backward[turn]) * sums[turn]
            row = side[turn]
            smoothed[row] = own * rows[row] + float((FILTER_GAIN - own) * backward[turn]) * value
    return smoothed


def times(left, right, contract=(1, 0)):
    dims = (((contract[0],), (contract[1],)), ((), ()))
    return lax.dot_general(left, right, dims, preferred_element_type=jnp.float32)


def split(values, count):
    pieces = []
    for turn in range(count):
        pieces.append(values.astype(jnp.bfloat16))
        if turn + 1 < count:
            values = values - pieces[-1].astype(jnp.float32)
    return pieces


def times_table(values, wide_table):
    pieces = split(values, 3)
    return times(jnp.concatenate([pieces[turn] for turn in LEFT_PIECES], axis=1), wide_table)


def widened(square_table):
    pieces = split(square_table, 3)
    return jnp.concatenate([pieces[turn] for turn in RIGHT_PIECES], axis=0)


def pack_kernel(
    velocity_hbm,
    cotangent_hbm,
    z_hbm,
    weight_in_hbm,
    bias_hbm,
    weight_out_hbm,
    out_ref,
    before_ref,
    after_ref,
    velocity_ref,
    cotangent_ref,
    z_ref,
    weight_in_ref,
    bias_ref,
    weight_out_ref,
    arrived,
):
    pairs = [
        (weight_in_hbm, weight_in_ref),
        (bias_hbm, bias_ref),
        (weight_out_hbm, weight_out_ref),
        (velocity_hbm, velocity_ref),
        (cotangent_hbm, cotangent_ref),
        (z_hbm, z_ref),
    ]
    copies = [
        pltpu.make_async_copy(source, target, arrived.at[turn])
        for turn, (source, target) in enumerate(pairs)
    ]
    for copy in copies:
        copy.start()

    for copy in copies[:3]:
        copy.wait()
    weight_in = weight_in_ref[...]
    weight_out = weight_out_ref[...]
    units = weight_in.shape[1]
    zeros = functools.partial(jnp.zeros, dtype=jnp.float32)
    before = jnp.concatenate(
        [
            jnp.concatenate([weight_in, bias_ref[...], zeros((9, units))], axis=0),
            jnp.concatenate([zeros((13, units)), STEP_SIZE * weight_out], axis=0),
        ],
        axis=1,
    )
    after = jnp.concatenate(
        [
            jnp.concatenate([zeros((6, units)), weight_out, zeros((7, units))], axis=0),
            jnp.concatenate([weight_in, zeros((10, units))], axis=0),
        ],
        axis=1,
    )
    pieces = [piece.astype(jnp.float32) for piece in split(before, 3)]
    before = jnp.concatenate([pieces[turn] for turn in RIGHT_PIECES + (1, 2)], axis=0)
    before_ref[...] = before.T.astype(jnp.bfloat16)
    pieces = split(after, 3)
    after_ref[...] = jnp.concatenate(
        [
            jnp.concatenate([pieces[0], pieces[0]], axis=1),
            jnp.concatenate([pieces[1], pieces[1]], axis=1),
            jnp.concatenate([pieces[2], jnp.zeros_like(pieces[2])], axis=1),
        ],
        axis=0,
    )

    for copy in copies[3:]:
        copy.wait()
    _, x_rows, y_rows, z_length = velocity_ref.shape
    block = x_rows * y_rows
    groups = LANES // block
    devices = z_length // groups
    velocity = velocity_ref[...].reshape(3 * block, z_length)
    cotangent = cotangent_ref[...].reshape(3 * block, z_length)
    along_z = times_table(velocity, widened(z_ref[...]))
    fill = jnp.zeros(((-SENT % groups) * block, z_length), jnp.float32)
    rows = jnp.concatenate(
        [velocity, along_z, cotangent[block:], cotangent[:block], fill], axis=0
    )
    for start in range(0, SENT, groups):
        turned = rows[start * block : (start + groups) * block].T
        parts = [turned[group * devices : (group + 1) * devices] for group in range(groups)]
        parts = exchange(parts, block)
        for field in range(start, min(start + groups, SENT)):
            out_ref[pl.ds(field, devices, stride=SENT), :] = parts[field - start]


def middle_kernel(
    x_devices,
    in_ref,
    before_ref,
    after_ref,
    y_ref,
    y_back_ref,
    out_ref,
    cells_ref,
    result_ref,
    tail_ref,
):
    y_devices = in_ref.shape[0] // SENT // x_devices
    x_rows = y_devices
    x_length = x_devices * x_rows
    units = before_ref.shape[0] // 2
    y_rows = LANES // y_devices // x_rows
    row8 = lax.broadcasted_iota(jnp.int32, (8, LANES), 0)

    planes = []
    for x_device in range(x_devices):
        places = [(turn * x_devices + x_device) * SENT for turn in range(y_devices)]
        parts = [in_ref[place : place + 8, :] for place in places]
        planes.extend(exchange(parts, y_rows))
    tails = [
        in_ref[pl.ds(turn * x_devices * SENT + 8, x_devices, stride=SENT), :]
        for turn in range(y_devices)
    ]
    tails = exchange(tails, y_rows)

    smoothed = smooth_rows(planes)
    along_y = times_table(jnp.concatenate(smoothed, axis=0), y_ref[...])
    for x in range(x_length):
        features = jnp.where(row8 < 3, along_y[8 * x : 8 * x + 8], smoothed[x])
        features = jnp.where(row8 < 6, features, jnp.where(row8 == 6, 1.0, 0.0))
        last = tails[x % x_rows][x // x_rows : x // x_rows + 1]
        cells_ref[:8, x * LANES : (x + 1) * LANES] = features
        cells_ref[8:, x * LANES : (x + 1) * LANES] = jnp.where(row8 == 5, last, planes[x])

    at_once = 2 * x_rows

    def network(chunk, sums):
        start = pl.multiple_of(chunk * at_once * LANES, LANES)
        pieces = split(cells_ref[:, pl.ds(start, at_once * LANES)], 3)
        wide = jnp.concatenate([pieces[turn] for turn in LEFT_PIECES + (2, 1)], axis=0)
        both = times(before_ref[...], wide)
        hidden = jnp.tanh(both[:units])
        grad_pre = both[units:] * (1.0 - hidden * hidden)
        both = jnp.concatenate([hidden, grad_pre], axis=0)
        both = jnp.concatenate(split(both, 2), axis=0)
        sums = sums + times(jnp.concatenate(pieces[:2], axis=0), both, (1, 1))
        result = times(after_ref[...], both)
        result = result[:16] + result[16:32] + result[32:]
        for turn in range(at_once):
            part = result[:9, turn * LANES : (turn + 1) * LANES]
            row = pl.multiple_of((chunk * at_once + turn) * 8, 8)
            result_ref[pl.ds(row, 8), :] = part[:8]
            place = (turn % x_rows) * x_devices + chunk * 2 + turn // x_rows
            tail_ref[pl.ds(place, 1), :] = part[8:]
        return sums

    sums = jnp.zeros((32, 4 * units), jnp.float32)
    sums = lax.fori_loop(0, x_length // at_once, network, sums)
    results = [result_ref[8 * x : 8 * x + 8, :] for x in range(x_length)]
    back_y = times_table(jnp.concatenate(results, axis=0), y_back_ref[...])
    back = [
        jnp.where(row8 < 3, back_y[8 * x : 8 * x + 8], results[x]) for x in range(x_length)
    ]
    back = smooth_rows(back)
    back = [jnp.where(row8 < 6, value, result) for value, result in zip(back, results)]
    for x_device in range(x_devices):
        first = x_device * x_rows
        parts = exchange(back[first : first + x_rows], y_rows)
        for turn in range(y_devices):
            place = (turn * x_devices + x_device) * RETURNED
            out_ref[place : place + 8, :] = parts[turn]
    tails = [tail_ref[x * x_devices : (x + 1) * x_devices, :] for x in range(x_rows)]
    tails = exchange(tails, y_rows)
    for turn in range(y_devices):
        place = turn * x_devices * RETURNED + 8
        out_ref[pl.ds(place, x_devices, stride=RETURNED), :] = tails[turn]

    sums = sums[:, : 2 * units] + sums[:, 2 * units :]
    sums = sums[:16] + sums[16:]
    moved = jnp.concatenate([sums[5:7, units:], STEP_SIZE * sums[13:16, :units]], axis=0)
    packed = jnp.concatenate([sums[:5, units:], moved], axis=1)
    for device in range(x_devices * y_devices):
        place = device * RETURNED + SENT
        out_ref[place : place + 5, :] = packed


def unpack_kernel(
    cells,
    in_ref,
    velocity_ref,
    cotangent_ref,
    z_ref,
    new_ref,
    grad_ref,
    in_grad_ref,
    bias_grad_ref,
    out_grad_ref,
):
    _, x_rows, y_rows, z_length = velocity_ref.shape
    block = x_rows * y_rows
    groups = LANES // block
    devices = z_length // groups
    units = in_grad_ref.shape[1]
    fields = []
    for start in range(0, SENT, groups):
        parts = [
            in_ref[pl.ds(min(field, SENT - 1), devices, stride=RETURNED), :]
            for field in range(start, start + groups)
        ]
        turned = jnp.concatenate(exchange(parts, block), axis=0).T
        fields.extend(turned[turn * block : (turn + 1) * block] for turn in range(groups))
    shape = (3, x_rows, y_rows, z_length)
    forcing = jnp.concatenate(fields[6:9], axis=0).reshape(shape)
    new_ref[...] = velocity_ref[...] + STEP_SIZE * forcing
    back_z = times_table(jnp.concatenate(fields[3:6], axis=0), z_ref[...])
    back = jnp.concatenate(fields[:3], axis=0) + back_z
    grad_ref[...] = cotangent_ref[...] + back.reshape(shape)

    sums = in_ref[SENT : SENT + 5, :]
    for device in range(1, devices):
        place = device * RETURNED + SENT
        sums = sums + in_ref[place : place + 5, :]
    sums = sums * (1.0 / cells)
    in_grad_ref[:5, :] = sums[:, :units]
    in_grad_ref[5:, :] = sums[:1, units:]
    bias_grad_ref[...] = sums[1:2, units:]
    out_grad_ref[...] = sums[2:, units:]


def on_device(kernel, shapes, scratch=(), **more):
    return pl.pallas_call(
        kernel,
        out_shape=[jax.ShapeDtypeStruct(shape, kind) for shape, kind in shapes],
        scratch_shapes=[*scratch],
        compiler_params=pltpu.CompilerParams(vmem_limit_bytes=32 * 1024 * 1024),
        **more,
    )


def fits(velocity, units):
    x_devices, y_devices = lax.axis_size("gx"), lax.axis_size("gy")
    _, x_rows, y_rows, z_length = velocity.shape
    return (
        z_length == LANES
        and x_rows * y_rows * LANES == LANES * LANES // 4
        and x_devices * y_devices * 4 == LANES
        and x_devices == 8
        and y_devices == x_rows
        and y_rows % 8 == 0
        and 2 * units == LANES
    )


def local_kernels(velocity, cotangent, weight_in, bias_in, weight_out):
    axes = ("gy", "gx")
    x_devices, y_devices = lax.axis_size("gx"), lax.axis_size("gy")
    devices = x_devices * y_devices
    _, x_rows, y_rows, z_length = velocity.shape
    units = weight_in.shape[1]
    cells = x_rows * x_devices * y_rows * y_devices * z_length
    z_table = derivative_table(z_length)
    y_table = np.kron(np.eye(z_length // devices), derivative_table(y_rows * y_devices))
    single, half = jnp.float32, jnp.bfloat16

    in_place = pl.BlockSpec(memory_space=pltpu.HBM)

    arguments = [
        velocity,
        cotangent,
        table(z_table.T),
        weight_in,
        bias_in[None],
        weight_out.T,
    ]
    arguments = [pltpu.with_memory_space_constraint(each, pltpu.HBM) for each in arguments]
    sent, *prepared = on_device(
        pack_kernel,
        [
            ((devices * SENT, LANES), single),
            ((2 * units, LANES), half),
            ((48, 4 * units), half),
        ],
        [pltpu.VMEM(values.shape, values.dtype) for values in arguments]
        + [pltpu.SemaphoreType.DMA((len(arguments),))],
        in_specs=[in_place] * len(arguments),
    )(*arguments)
    sent = sent.reshape(devices, 1, SENT * LANES)
    sent = lax.all_to_all(sent, axes, 0, 0, tiled=True).reshape(devices * SENT, LANES)
    (back,) = on_device(
        functools.partial(middle_kernel, x_devices),
        [((devices * RETURNED, LANES), single)],
        [
            pltpu.VMEM((16, x_devices * x_rows * LANES), single),
            pltpu.VMEM((8 * x_devices * x_rows, LANES), single),
            pltpu.VMEM((x_devices * x_rows, LANES), single),
        ],
    )(sent, *prepared, split_table(y_table.T), split_table(y_table))
    back = back.reshape(devices, 1, RETURNED * LANES)
    back = lax.all_to_all(back, axes, 0, 0, tiled=True).reshape(devices * RETURNED, LANES)
    shapes = [velocity.shape, velocity.shape, (6, units), (1, units), (3, units)]
    new, grad, grad_in, grad_bias, grad_out = on_device(
        functools.partial(unpack_kernel, float(cells)), [(shape, single) for shape in shapes]
    )(back, velocity, cotangent, split_table(z_table))
    return (new, grad, grad_in, grad_bias[0], grad_out.T)


def local(velocity, cotangent, weight_in, bias_in, weight_out):
    chosen = local_kernels if fits(velocity, weight_in.shape[1]) else local_plain
    return chosen(velocity, cotangent, weight_in, bias_in, weight_out)


def solution(mesh):
    in_specs = (P(None, "gx", "gy", None), P(None, "gx", "gy", None), P(), P(), P())
    out_specs = (P(None, "gx", "gy", None), P(None, "gx", "gy", None), P(), P(), P())
    return jax.shard_map(local, mesh=mesh, in_specs=in_specs, out_specs=out_specs, check_vma=False)
```

```python
import functools

import jax
import jax.numpy as jnp
import ml_dtypes
import numpy as np
from jax import lax
from jax.experimental import pallas as pl
from jax.experimental.pallas import tpu as pltpu
from jax.sharding import PartitionSpec as P

FILTER_ALPHA = 0.499
FILTER_GAIN = 0.5 + FILTER_ALPHA
COMPACT_ALPHA = 1.0 / 3.0
STEP_SIZE = 0.5
PRECISE = lax.Precision.HIGHEST
LANES = 128
SENT = 9
RETURNED = 14
LEFT_PIECES = (0, 1, 0, 2, 1, 0)
RIGHT_PIECES = (0, 0, 1, 0, 1, 2)


def beside(length, offset):
    return np.eye(length, k=offset) + np.eye(length, k=-offset)


def smooth_table(length):
    left = np.eye(length) + FILTER_ALPHA * beside(length, 1)
    right = FILTER_GAIN * np.eye(length) + 0.5 * FILTER_GAIN * beside(length, 1)
    return np.linalg.solve(left, right)


def derivative_table(length):
    left = np.eye(length) + COMPACT_ALPHA * beside(length, 1)
    right = 7.0 / 9.0 * (np.eye(length, k=1) - np.eye(length, k=-1)) + 1.0 / 36.0 * (
        np.eye(length, k=2) - np.eye(length, k=-2)
    )
    return np.linalg.solve(left, right)


def table(values):
    return jnp.asarray(values.astype(np.float32))


def split_table(values):
    pieces = []
    rest = values.astype(np.float32)
    for _ in range(3):
        pieces.append(rest.astype(ml_dtypes.bfloat16))
        rest = rest - pieces[-1].astype(np.float32)
    return jnp.asarray(np.concatenate([pieces[turn] for turn in RIGHT_PIECES], axis=0))


def local_plain(velocity, cotangent, weight_in, bias_in, weight_out):
    axes = ("gx", "gy")
    x_devices, y_devices = lax.axis_size("gx"), lax.axis_size("gy")
    devices = x_devices * y_devices
    _, x_rows, y_rows, z_length = velocity.shape
    x_length, y_length = x_rows * x_devices, y_rows * y_devices
    units = weight_in.shape[1]
    z_rows = -(-z_length // devices)
    padding = z_rows * devices - z_length

    z_table = table(derivative_table(z_length))
    y_table = table(derivative_table(y_length))
    x_table = table(smooth_table(x_length))

    along_z = jnp.einsum("ab,kxyb->kxya", z_table, velocity, precision=PRECISE)
    fields = jnp.concatenate([velocity, along_z, cotangent], axis=0)
    fields = jnp.pad(fields, ((0, 0), (0, 0), (0, 0), (0, padding)))
    fields = fields.reshape(9, x_rows, y_rows, z_rows, devices)
    fields = fields.transpose(4, 0, 3, 1, 2).reshape(devices, 9, z_rows * x_rows * y_rows)
    fields = lax.all_to_all(fields, axes, 0, 0, tiled=True)
    fields = fields.reshape(x_devices, y_devices, 9, z_rows, x_rows, y_rows)
    fields = fields.transpose(2, 0, 4, 3, 1, 5).reshape(9, x_length, z_rows, y_length)

    smoothed = jnp.einsum("ab,kbzy->kazy", x_table, fields[:6], precision=PRECISE)
    along_y = jnp.einsum("ab,kxzb->kxza", y_table, smoothed[:3], precision=PRECISE)
    features = jnp.concatenate([along_y, smoothed[3:]], axis=0).reshape(6, -1)
    grad_out = STEP_SIZE * fields[6:].reshape(3, -1)

    hidden = jnp.tanh(jnp.dot(weight_in.T, features, precision=PRECISE) + bias_in[:, None])
    forcing = jnp.dot(weight_out.T, hidden, precision=PRECISE)
    grad_pre = jnp.dot(weight_out, grad_out, precision=PRECISE) * (1.0 - hidden * hidden)
    grad_features = jnp.dot(weight_in, grad_pre, precision=PRECISE)
    sum_in = jnp.dot(features, grad_pre.T, precision=PRECISE)
    sum_bias = jnp.sum(grad_pre, axis=1)
    sum_out = jnp.dot(grad_out, hidden.T, precision=PRECISE)

    grad_features = grad_features.reshape(6, x_length, z_rows, y_length)
    back_y = jnp.einsum("ba,kxzb->kxza", y_table, grad_features[:3], precision=PRECISE)
    back = jnp.concatenate([back_y, grad_features[3:]], axis=0)
    back = jnp.einsum("ab,kbzy->kazy", x_table, back, precision=PRECISE)
    back = jnp.concatenate([forcing.reshape(3, x_length, z_rows, y_length), back], axis=0)
    back = back.reshape(9, x_devices, x_rows, z_rows, y_devices, y_rows)
    back = back.transpose(1, 4, 0, 3, 2, 5).reshape(devices, -1)
    sums = jnp.concatenate([sum_in, sum_bias[None], sum_out], axis=0).reshape(1, -1)
    cells = back.shape[1]
    back = jnp.concatenate([back, jnp.broadcast_to(sums, (devices, 10 * units))], axis=1)
    back = lax.all_to_all(back, axes, 0, 0, tiled=True)

    sums = jnp.sum(back[:, cells:], axis=0).reshape(10, units)
    sums = sums / float(x_length * y_length * z_length)
    back = back[:, :cells].reshape(devices, 9, z_rows, x_rows, y_rows)
    back = back.transpose(1, 3, 4, 2, 0).reshape(9, x_rows, y_rows, -1)[..., :z_length]
    new_velocity = velocity + STEP_SIZE * back[:3]
    back_z = jnp.einsum("ba,kxyb->kxya", z_table, back[6:], precision=PRECISE)
    grad_velocity = cotangent + back[3:6] + back_z
    return (new_velocity, grad_velocity, sums[:6], sums[6], sums[7:].T)


def exchange(parts, width):
    parts = list(parts)
    lane = lax.broadcasted_iota(jnp.int32, parts[0].shape, 1)
    step = len(parts) // 2
    while step:
        shift = step * width
        upper = (lane & shift) != 0
        for low in range(len(parts)):
            if low & step == 0:
                first, second = parts[low], parts[low + step]
                parts[low] = jnp.where(upper, pltpu.roll(second, shift, 1), first)
                parts[low + step] = jnp.where(upper, second, pltpu.roll(first, LANES - shift, 1))
        step //= 2
    return parts


def smooth_rows(rows):
    length = len(rows)
    half = length // 2
    scales = []
    before = 0.0
    for _ in range(half):
        scales.append(1.0 / (1.0 - FILTER_ALPHA * FILTER_ALPHA * before))
        before = scales[-1]
    factors = [-FILTER_ALPHA * scale for scale in scales]
    forward = np.cumprod([1.0] + factors[1:])
    backward = np.cumprod([1.0] + factors[-2::-1])[::-1]
    own = 0.5 * FILTER_GAIN / FILTER_ALPHA

    sides = [list(range(half)), list(range(length - 1, half - 1, -1))]
    running = []
    for side in sides:
        sums = []
        for turn, row in enumerate(side):
            value = rows[row] * float(scales[turn] / forward[turn])
            sums.append(value if turn == 0 else sums[-1] + value)
        running.append(sums)
    middle = forward[-1] / (1.0 - factors[-1] * factors[-1])
    cross = middle * factors[-1]
    smoothed = [None] * length
    for side, sums, others in zip(sides, running, running[::-1]):
        value = float(middle) * sums[-1] + float(cross) * others[-1]
        for turn in reversed(range(half)):
            if turn < half - 1:
                value = value + float(forward[turn] / backward[turn]) * sums[turn]
            row = side[turn]
            smoothed[row] = own * rows[row] + float((FILTER_GAIN - own) * backward[turn]) * value
    return smoothed


def times(left, right, contract=(1, 0)):
    dims = (((contract[0],), (contract[1],)), ((), ()))
    return lax.dot_general(left, right, dims, preferred_element_type=jnp.float32)


def split(values, count):
    pieces = []
    for turn in range(count):
        pieces.append(values.astype(jnp.bfloat16))
        if turn + 1 < count:
            values = values - pieces[-1].astype(jnp.float32)
    return pieces


def times_table(values, wide_table):
    pieces = split(values, 3)
    return times(jnp.concatenate([pieces[turn] for turn in LEFT_PIECES], axis=1), wide_table)


def widened(square_table):
    pieces = split(square_table, 3)
    return jnp.concatenate([pieces[turn] for turn in RIGHT_PIECES], axis=0)


def by_parts(rows, wide_table):
    half = len(rows) // 2
    outs = []
    for start in (0, half):
        out = times_table(jnp.concatenate(rows[start : start + half], axis=0), wide_table)
        outs.extend(out[8 * turn : 8 * turn + 8] for turn in range(half))
    return outs


def pack_kernel(
    velocity_hbm,
    cotangent_hbm,
    z_hbm,
    weight_in_hbm,
    bias_hbm,
    weight_out_hbm,
    out_ref,
    before_ref,
    after_ref,
    velocity_ref,
    cotangent_ref,
    z_ref,
    weight_in_ref,
    bias_ref,
    weight_out_ref,
    arrived,
):
    pairs = [
        (weight_in_hbm, weight_in_ref),
        (bias_hbm, bias_ref),
        (weight_out_hbm, weight_out_ref),
        (velocity_hbm, velocity_ref),
        (cotangent_hbm, cotangent_ref),
        (z_hbm, z_ref),
    ]
    copies = [
        pltpu.make_async_copy(source, target, arrived.at[turn])
        for turn, (source, target) in enumerate(pairs)
    ]
    for copy in copies:
        copy.start()

    for copy in copies[:3]:
        copy.wait()
    weight_in = weight_in_ref[...]
    weight_out = weight_out_ref[...]
    units = weight_in.shape[1]
    zeros = functools.partial(jnp.zeros, dtype=jnp.float32)
    before = jnp.concatenate(
        [
            jnp.concatenate([weight_in, bias_ref[...], zeros((9, units))], axis=0),
            jnp.concatenate([zeros((13, units)), STEP_SIZE * weight_out], axis=0),
        ],
        axis=1,
    )
    after = jnp.concatenate(
        [
            jnp.concatenate([zeros((6, units)), weight_out, zeros((7, units))], axis=0),
            jnp.concatenate([weight_in, zeros((10, units))], axis=0),
        ],
        axis=1,
    )
    pieces = [piece.astype(jnp.float32) for piece in split(before, 3)]
    before = jnp.concatenate([pieces[turn] for turn in RIGHT_PIECES + (1, 2)], axis=0)
    before_ref[...] = before.T.astype(jnp.bfloat16)
    pieces = split(after, 3)
    after_ref[...] = jnp.concatenate(
        [
            jnp.concatenate([pieces[0], pieces[0]], axis=1),
            jnp.concatenate([pieces[1], pieces[1]], axis=1),
            jnp.concatenate([pieces[2], jnp.zeros_like(pieces[2])], axis=1),
        ],
        axis=0,
    )

    for copy in copies[3:]:
        copy.wait()
    _, x_rows, y_rows, z_length = velocity_ref.shape
    block = x_rows * y_rows
    groups = LANES // block
    devices = z_length // groups
    velocity = velocity_ref[...].reshape(3 * block, z_length)
    cotangent = cotangent_ref[...].reshape(3 * block, z_length)
    along_z = times_table(velocity, widened(z_ref[...]))
    fill = jnp.zeros(((-SENT % groups) * block, z_length), jnp.float32)
    rows = jnp.concatenate(
        [velocity, along_z, cotangent[block:], cotangent[:block], fill], axis=0
    )
    for start in range(0, SENT, groups):
        turned = rows[start * block : (start + groups) * block].T
        parts = [turned[group * devices : (group + 1) * devices] for group in range(groups)]
        parts = exchange(parts, block)
        for field in range(start, min(start + groups, SENT)):
            out_ref[pl.ds(field, devices, stride=SENT), :] = parts[field - start]


def middle_kernel(x_devices, in_ref, before_ref, after_ref, y_ref, y_back_ref, out_ref, tail_ref):
    y_devices = in_ref.shape[0] // SENT // x_devices
    x_rows = y_devices
    x_length = x_devices * x_rows
    units = before_ref.shape[0] // 2
    y_rows = LANES // y_devices // x_rows
    row8 = lax.broadcasted_iota(jnp.int32, (8, LANES), 0)

    planes = []
    for x_device in range(x_devices):
        places = [(turn * x_devices + x_device) * SENT for turn in range(y_devices)]
        parts = [in_ref[place : place + 8, :] for place in places]
        planes.extend(exchange(parts, y_rows))
    tails = [
        in_ref[pl.ds(turn * x_devices * SENT + 8, x_devices, stride=SENT), :]
        for turn in range(y_devices)
    ]
    tails = exchange(tails, y_rows)

    smoothed = smooth_rows(planes)
    along_y = by_parts(smoothed, y_ref[...])
    upper_rows = []
    lower_rows = []
    for x in range(x_length):
        features = jnp.where(row8 < 3, along_y[x], smoothed[x])
        features = jnp.where(row8 < 6, features, jnp.where(row8 == 6, 1.0, 0.0))
        last = tails[x % x_rows][x // x_rows : x // x_rows + 1]
        upper_rows.append(features)
        lower_rows.append(jnp.where(row8 == 5, last, planes[x]))

    before = before_ref[...]
    after = after_ref[...]
    at_once = 8
    sums = jnp.zeros((32, 4 * units), jnp.float32)
    results = []
    for start in range(0, x_length, at_once):
        stop = start + at_once
        cells = jnp.concatenate(
            [
                jnp.concatenate(upper_rows[start:stop], axis=1),
                jnp.concatenate(lower_rows[start:stop], axis=1),
            ],
            axis=0,
        )
        pieces = split(cells, 3)
        both = times(before, jnp.concatenate([pieces[turn] for turn in LEFT_PIECES + (2, 1)], axis=0))
        hidden = jnp.tanh(both[:units])
        grad_pre = both[units:] * (1.0 - hidden * hidden)
        both = jnp.concatenate([hidden, grad_pre], axis=0)
        both = jnp.concatenate(split(both, 2), axis=0)
        sums = sums + times(jnp.concatenate(pieces[:2], axis=0), both, (1, 1))
        result = times(after, both)
        result = result[:16] + result[16:32] + result[32:]
        for turn in range(at_once):
            results.append(result[:8, turn * LANES : (turn + 1) * LANES])
            x = start + turn
            place = (x % x_rows) * x_devices + x // x_rows
            tail_ref[place : place + 1, :] = result[8:9, turn * LANES : (turn + 1) * LANES]

    back_y = by_parts(results, y_back_ref[...])
    back = [jnp.where(row8 < 3, back_y[x], results[x]) for x in range(x_length)]
    back = smooth_rows(back)
    back = [jnp.where(row8 < 6, value, result) for value, result in zip(back, results)]
    for x_device in range(x_devices):
        first = x_device * x_rows
        parts = exchange(back[first : first + x_rows], y_rows)
        for turn in range(y_devices):
            place = (turn * x_devices + x_device) * RETURNED
            out_ref[place : place + 8, :] = parts[turn]
    tails = [tail_ref[x * x_devices : (x + 1) * x_devices, :] for x in range(x_rows)]
    tails = exchange(tails, y_rows)
    for turn in range(y_devices):
        place = turn * x_devices * RETURNED + 8
        out_ref[pl.ds(place, x_devices, stride=RETURNED), :] = tails[turn]

    sums = sums[:, : 2 * units] + sums[:, 2 * units :]
    sums = sums[:16] + sums[16:]
    moved = jnp.concatenate([sums[5:7, units:], STEP_SIZE * sums[13:16, :units]], axis=0)
    packed = jnp.concatenate([sums[:5, units:], moved], axis=1)
    for device in range(x_devices * y_devices):
        place = device * RETURNED + SENT
        out_ref[place : place + 5, :] = packed


def unpack_kernel(
    cells,
    in_ref,
    velocity_ref,
    cotangent_ref,
    z_ref,
    new_ref,
    grad_ref,
    in_grad_ref,
    bias_grad_ref,
    out_grad_ref,
):
    _, x_rows, y_rows, z_length = velocity_ref.shape
    block = x_rows * y_rows
    groups = LANES // block
    devices = z_length // groups
    units = in_grad_ref.shape[1]
    fields = []
    for start in range(0, SENT, groups):
        parts = [
            in_ref[pl.ds(min(field, SENT - 1), devices, stride=RETURNED), :]
            for field in range(start, start + groups)
        ]
        turned = jnp.concatenate(exchange(parts, block), axis=0).T
        fields.extend(turned[turn * block : (turn + 1) * block] for turn in range(groups))
    shape = (3, x_rows, y_rows, z_length)
    forcing = jnp.concatenate(fields[6:9], axis=0).reshape(shape)
    new_ref[...] = velocity_ref[...] + STEP_SIZE * forcing
    back_z = times_table(jnp.concatenate(fields[3:6], axis=0), z_ref[...])
    back = jnp.concatenate(fields[:3], axis=0) + back_z
    grad_ref[...] = cotangent_ref[...] + back.reshape(shape)

    sums = in_ref[SENT : SENT + 5, :]
    for device in range(1, devices):
        place = device * RETURNED + SENT
        sums = sums + in_ref[place : place + 5, :]
    sums = sums * (1.0 / cells)
    in_grad_ref[:5, :] = sums[:, :units]
    in_grad_ref[5:, :] = sums[:1, units:]
    bias_grad_ref[...] = sums[1:2, units:]
    out_grad_ref[...] = sums[2:, units:]


def on_device(kernel, shapes, scratch=(), **more):
    return pl.pallas_call(
        kernel,
        out_shape=[jax.ShapeDtypeStruct(shape, kind) for shape, kind in shapes],
        scratch_shapes=[*scratch],
        compiler_params=pltpu.CompilerParams(vmem_limit_bytes=32 * 1024 * 1024),
        **more,
    )


def fits(velocity, units):
    x_devices, y_devices = lax.axis_size("gx"), lax.axis_size("gy")
    _, x_rows, y_rows, z_length = velocity.shape
    return (
        z_length == LANES
        and x_rows * y_rows * LANES == LANES * LANES // 4
        and x_devices * y_devices * 4 == LANES
        and x_devices == 8
        and y_devices == x_rows
        and y_rows % 8 == 0
        and 2 * units == LANES
    )


def local_kernels(velocity, cotangent, weight_in, bias_in, weight_out):
    axes = ("gy", "gx")
    x_devices, y_devices = lax.axis_size("gx"), lax.axis_size("gy")
    devices = x_devices * y_devices
    _, x_rows, y_rows, z_length = velocity.shape
    units = weight_in.shape[1]
    cells = x_rows * x_devices * y_rows * y_devices * z_length
    z_table = derivative_table(z_length)
    y_table = np.kron(np.eye(z_length // devices), derivative_table(y_rows * y_devices))
    single, half = jnp.float32, jnp.bfloat16

    in_place = pl.BlockSpec(memory_space=pltpu.HBM)

    arguments = [
        velocity,
        cotangent,
        table(z_table.T),
        weight_in,
        bias_in[None],
        weight_out.T,
    ]
    arguments = [pltpu.with_memory_space_constraint(each, pltpu.HBM) for each in arguments]
    sent, *prepared = on_device(
        pack_kernel,
        [
            ((devices * SENT, LANES), single),
            ((2 * units, LANES), half),
            ((48, 4 * units), half),
        ],
        [pltpu.VMEM(values.shape, values.dtype) for values in arguments]
        + [pltpu.SemaphoreType.DMA((len(arguments),))],
        in_specs=[in_place] * len(arguments),
    )(*arguments)
    sent = sent.reshape(devices, 1, SENT * LANES)
    sent = lax.all_to_all(sent, axes, 0, 0, tiled=True).reshape(devices * SENT, LANES)
    (back,) = on_device(
        functools.partial(middle_kernel, x_devices),
        [((devices * RETURNED, LANES), single)],
        [pltpu.VMEM((x_devices * x_rows, LANES), single)],
    )(sent, *prepared, split_table(y_table.T), split_table(y_table))
    back = back.reshape(devices, 1, RETURNED * LANES)
    back = lax.all_to_all(back, axes, 0, 0, tiled=True).reshape(devices * RETURNED, LANES)
    shapes = [velocity.shape, velocity.shape, (6, units), (1, units), (3, units)]
    new, grad, grad_in, grad_bias, grad_out = on_device(
        functools.partial(unpack_kernel, float(cells)), [(shape, single) for shape in shapes]
    )(back, velocity, cotangent, split_table(z_table))
    return (new, grad, grad_in, grad_bias[0], grad_out.T)


def local(velocity, cotangent, weight_in, bias_in, weight_out):
    chosen = local_kernels if fits(velocity, weight_in.shape[1]) else local_plain
    return chosen(velocity, cotangent, weight_in, bias_in, weight_out)


def solution(mesh):
    in_specs = (P(None, "gx", "gy", None), P(None, "gx", "gy", None), P(), P(), P())
    out_specs = (P(None, "gx", "gy", None), P(None, "gx", "gy", None), P(), P(), P())
    return jax.shard_map(local, mesh=mesh, in_specs=in_specs, out_specs=out_specs, check_vma=False)
```

```python
import functools

import jax
import jax.numpy as jnp
import ml_dtypes
import numpy as np
from jax import lax
from jax.experimental import pallas as pl
from jax.experimental.pallas import tpu as pltpu
from jax.sharding import PartitionSpec as P

FILTER_ALPHA = 0.499
FILTER_GAIN = 0.5 + FILTER_ALPHA
COMPACT_ALPHA = 1.0 / 3.0
STEP_SIZE = 0.5
PRECISE = lax.Precision.HIGHEST
LANES = 128
SENT = 9
RETURNED = 14
LEFT_PIECES = (0, 1, 0, 2, 1, 0)
RIGHT_PIECES = (0, 0, 1, 0, 1, 2)


def beside(length, offset):
    return np.eye(length, k=offset) + np.eye(length, k=-offset)


def smooth_table(length):
    left = np.eye(length) + FILTER_ALPHA * beside(length, 1)
    right = FILTER_GAIN * np.eye(length) + 0.5 * FILTER_GAIN * beside(length, 1)
    return np.linalg.solve(left, right)


def derivative_table(length):
    left = np.eye(length) + COMPACT_ALPHA * beside(length, 1)
    right = 7.0 / 9.0 * (np.eye(length, k=1) - np.eye(length, k=-1)) + 1.0 / 36.0 * (
        np.eye(length, k=2) - np.eye(length, k=-2)
    )
    return np.linalg.solve(left, right)


def table(values):
    return jnp.asarray(values.astype(np.float32))


def split_table(values):
    pieces = []
    rest = values.astype(np.float32)
    for _ in range(3):
        pieces.append(rest.astype(ml_dtypes.bfloat16))
        rest = rest - pieces[-1].astype(np.float32)
    return jnp.asarray(np.concatenate([pieces[turn] for turn in RIGHT_PIECES], axis=0))


def local_plain(velocity, cotangent, weight_in, bias_in, weight_out):
    axes = ("gx", "gy")
    x_devices, y_devices = lax.axis_size("gx"), lax.axis_size("gy")
    devices = x_devices * y_devices
    _, x_rows, y_rows, z_length = velocity.shape
    x_length, y_length = x_rows * x_devices, y_rows * y_devices
    units = weight_in.shape[1]
    z_rows = -(-z_length // devices)
    padding = z_rows * devices - z_length

    z_table = table(derivative_table(z_length))
    y_table = table(derivative_table(y_length))
    x_table = table(smooth_table(x_length))

    along_z = jnp.einsum("ab,kxyb->kxya", z_table, velocity, precision=PRECISE)
    fields = jnp.concatenate([velocity, along_z, cotangent], axis=0)
    fields = jnp.pad(fields, ((0, 0), (0, 0), (0, 0), (0, padding)))
    fields = fields.reshape(9, x_rows, y_rows, z_rows, devices)
    fields = fields.transpose(4, 0, 3, 1, 2).reshape(devices, 9, z_rows * x_rows * y_rows)
    fields = lax.all_to_all(fields, axes, 0, 0, tiled=True)
    fields = fields.reshape(x_devices, y_devices, 9, z_rows, x_rows, y_rows)
    fields = fields.transpose(2, 0, 4, 3, 1, 5).reshape(9, x_length, z_rows, y_length)

    smoothed = jnp.einsum("ab,kbzy->kazy", x_table, fields[:6], precision=PRECISE)
    along_y = jnp.einsum("ab,kxzb->kxza", y_table, smoothed[:3], precision=PRECISE)
    features = jnp.concatenate([along_y, smoothed[3:]], axis=0).reshape(6, -1)
    grad_out = STEP_SIZE * fields[6:].reshape(3, -1)

    hidden = jnp.tanh(jnp.dot(weight_in.T, features, precision=PRECISE) + bias_in[:, None])
    forcing = jnp.dot(weight_out.T, hidden, precision=PRECISE)
    grad_pre = jnp.dot(weight_out, grad_out, precision=PRECISE) * (1.0 - hidden * hidden)
    grad_features = jnp.dot(weight_in, grad_pre, precision=PRECISE)
    sum_in = jnp.dot(features, grad_pre.T, precision=PRECISE)
    sum_bias = jnp.sum(grad_pre, axis=1)
    sum_out = jnp.dot(grad_out, hidden.T, precision=PRECISE)

    grad_features = grad_features.reshape(6, x_length, z_rows, y_length)
    back_y = jnp.einsum("ba,kxzb->kxza", y_table, grad_features[:3], precision=PRECISE)
    back = jnp.concatenate([back_y, grad_features[3:]], axis=0)
    back = jnp.einsum("ab,kbzy->kazy", x_table, back, precision=PRECISE)
    back = jnp.concatenate([forcing.reshape(3, x_length, z_rows, y_length), back], axis=0)
    back = back.reshape(9, x_devices, x_rows, z_rows, y_devices, y_rows)
    back = back.transpose(1, 4, 0, 3, 2, 5).reshape(devices, -1)
    sums = jnp.concatenate([sum_in, sum_bias[None], sum_out], axis=0).reshape(1, -1)
    cells = back.shape[1]
    back = jnp.concatenate([back, jnp.broadcast_to(sums, (devices, 10 * units))], axis=1)
    back = lax.all_to_all(back, axes, 0, 0, tiled=True)

    sums = jnp.sum(back[:, cells:], axis=0).reshape(10, units)
    sums = sums / float(x_length * y_length * z_length)
    back = back[:, :cells].reshape(devices, 9, z_rows, x_rows, y_rows)
    back = back.transpose(1, 3, 4, 2, 0).reshape(9, x_rows, y_rows, -1)[..., :z_length]
    new_velocity = velocity + STEP_SIZE * back[:3]
    back_z = jnp.einsum("ba,kxyb->kxya", z_table, back[6:], precision=PRECISE)
    grad_velocity = cotangent + back[3:6] + back_z
    return (new_velocity, grad_velocity, sums[:6], sums[6], sums[7:].T)


def exchange(parts, width):
    parts = list(parts)
    lane = lax.broadcasted_iota(jnp.int32, parts[0].shape, 1)
    step = len(parts) // 2
    while step:
        shift = step * width
        upper = (lane & shift) != 0
        for low in range(len(parts)):
            if low & step == 0:
                first, second = parts[low], parts[low + step]
                parts[low] = jnp.where(upper, pltpu.roll(second, shift, 1), first)
                parts[low + step] = jnp.where(upper, second, pltpu.roll(first, LANES - shift, 1))
        step //= 2
    return parts


def smooth_rows(rows):
    length = len(rows)
    half = length // 2
    scales = []
    before = 0.0
    for _ in range(half):
        scales.append(1.0 / (1.0 - FILTER_ALPHA * FILTER_ALPHA * before))
        before = scales[-1]
    factors = [-FILTER_ALPHA * scale for scale in scales]
    forward = np.cumprod([1.0] + factors[1:])
    backward = np.cumprod([1.0] + factors[-2::-1])[::-1]
    own = 0.5 * FILTER_GAIN / FILTER_ALPHA

    sides = [list(range(half)), list(range(length - 1, half - 1, -1))]
    running = []
    for side in sides:
        sums = []
        for turn, row in enumerate(side):
            value = rows[row] * float(scales[turn] / forward[turn])
            sums.append(value if turn == 0 else sums[-1] + value)
        running.append(sums)
    middle = forward[-1] / (1.0 - factors[-1] * factors[-1])
    cross = middle * factors[-1]
    smoothed = [None] * length
    for side, sums, others in zip(sides, running, running[::-1]):
        value = float(middle) * sums[-1] + float(cross) * others[-1]
        for turn in reversed(range(half)):
            if turn < half - 1:
                value = value + float(forward[turn] / backward[turn]) * sums[turn]
            row = side[turn]
            smoothed[row] = own * rows[row] + float((FILTER_GAIN - own) * backward[turn]) * value
    return smoothed


def times(left, right, contract=(1, 0)):
    dims = (((contract[0],), (contract[1],)), ((), ()))
    return lax.dot_general(left, right, dims, preferred_element_type=jnp.float32)


def split(values, count):
    pieces = []
    for turn in range(count):
        pieces.append(values.astype(jnp.bfloat16))
        if turn + 1 < count:
            values = values - pieces[-1].astype(jnp.float32)
    return pieces


def times_table(values, wide_table):
    pieces = split(values, 3)
    return times(jnp.concatenate([pieces[turn] for turn in LEFT_PIECES], axis=1), wide_table)


def widened(square_table):
    pieces = split(square_table, 3)
    return jnp.concatenate([pieces[turn] for turn in RIGHT_PIECES], axis=0)


def by_parts(rows, wide_table):
    half = len(rows) // 2
    outs = []
    for start in (0, half):
        out = times_table(jnp.concatenate(rows[start : start + half], axis=0), wide_table)
        outs.extend(out[8 * turn : 8 * turn + 8] for turn in range(half))
    return outs


def pack_kernel(
    velocity_hbm,
    cotangent_hbm,
    z_hbm,
    weight_in_hbm,
    bias_hbm,
    weight_out_hbm,
    out_ref,
    before_ref,
    after_ref,
    velocity_ref,
    cotangent_ref,
    z_ref,
    weight_in_ref,
    bias_ref,
    weight_out_ref,
    arrived,
):
    pairs = [
        (weight_in_hbm, weight_in_ref),
        (bias_hbm, bias_ref),
        (weight_out_hbm, weight_out_ref),
        (velocity_hbm, velocity_ref),
        (cotangent_hbm, cotangent_ref),
        (z_hbm, z_ref),
    ]
    copies = [
        pltpu.make_async_copy(source, target, arrived.at[turn])
        for turn, (source, target) in enumerate(pairs)
    ]
    for copy in copies:
        copy.start()

    for copy in copies[:3]:
        copy.wait()
    weight_in = weight_in_ref[...]
    weight_out = weight_out_ref[...]
    units = weight_in.shape[1]
    zeros = functools.partial(jnp.zeros, dtype=jnp.float32)
    before = jnp.concatenate(
        [
            jnp.concatenate([weight_in, bias_ref[...], zeros((9, units))], axis=0),
            jnp.concatenate([zeros((13, units)), STEP_SIZE * weight_out], axis=0),
        ],
        axis=1,
    )
    after = jnp.concatenate(
        [
            jnp.concatenate([zeros((6, units)), weight_out, zeros((7, units))], axis=0),
            jnp.concatenate([weight_in, zeros((10, units))], axis=0),
        ],
        axis=1,
    )
    pieces = [piece.astype(jnp.float32) for piece in split(before, 3)]
    before = jnp.concatenate([pieces[turn] for turn in RIGHT_PIECES + (1, 2)], axis=0)
    before_ref[...] = before.T.astype(jnp.bfloat16)
    pieces = split(after, 3)
    after_ref[...] = jnp.concatenate(
        [
            jnp.concatenate([pieces[0], pieces[0]], axis=1),
            jnp.concatenate([pieces[1], pieces[1]], axis=1),
            jnp.concatenate([pieces[2], jnp.zeros_like(pieces[2])], axis=1),
        ],
        axis=0,
    )

    for copy in copies[3:]:
        copy.wait()
    _, x_rows, y_rows, z_length = velocity_ref.shape
    block = x_rows * y_rows
    groups = LANES // block
    devices = z_length // groups
    velocity = velocity_ref[...].reshape(3 * block, z_length)
    cotangent = cotangent_ref[...].reshape(3 * block, z_length)
    along_z = times_table(velocity, widened(z_ref[...]))
    fill = jnp.zeros(((-SENT % groups) * block, z_length), jnp.float32)
    rows = jnp.concatenate(
        [velocity, along_z, cotangent[block:], cotangent[:block], fill], axis=0
    )
    for start in range(0, SENT, groups):
        turned = rows[start * block : (start + groups) * block].T
        parts = [turned[group * devices : (group + 1) * devices] for group in range(groups)]
        parts = exchange(parts, block)
        for field in range(start, min(start + groups, SENT)):
            out_ref[pl.ds(field, devices, stride=SENT), :] = parts[field - start]


def middle_kernel(x_devices, in_ref, before_ref, after_ref, y_ref, y_back_ref, out_ref, tail_ref):
    y_devices = in_ref.shape[0] // SENT // x_devices
    x_rows = y_devices
    x_length = x_devices * x_rows
    units = before_ref.shape[0] // 2
    y_rows = LANES // y_devices // x_rows
    row8 = lax.broadcasted_iota(jnp.int32, (8, LANES), 0)

    planes = []
    for x_device in range(x_devices):
        places = [(turn * x_devices + x_device) * SENT for turn in range(y_devices)]
        parts = [in_ref[place : place + 8, :] for place in places]
        planes.extend(exchange(parts, y_rows))
    tails = [
        in_ref[pl.ds(turn * x_devices * SENT + 8, x_devices, stride=SENT), :]
        for turn in range(y_devices)
    ]
    tails = exchange(tails, y_rows)

    smoothed = smooth_rows(planes)
    along_y = by_parts(smoothed, y_ref[...])
    upper_rows = []
    lower_rows = []
    for x in range(x_length):
        features = jnp.where(row8 < 3, along_y[x], smoothed[x])
        features = jnp.where(row8 < 6, features, jnp.where(row8 == 6, 1.0, 0.0))
        last = tails[x % x_rows][x // x_rows : x // x_rows + 1]
        upper_rows.append(features)
        lower_rows.append(jnp.where(row8 == 5, last, planes[x]))

    before = before_ref[...]
    after = after_ref[...]
    at_once = 2
    sums = jnp.zeros((32, 4 * units), jnp.float32)
    results = []
    for start in range(0, x_length, at_once):
        stop = start + at_once
        cells = jnp.concatenate(
            [
                jnp.concatenate(upper_rows[start:stop], axis=1),
                jnp.concatenate(lower_rows[start:stop], axis=1),
            ],
            axis=0,
        )
        pieces = split(cells, 3)
        both = times(before, jnp.concatenate([pieces[turn] for turn in LEFT_PIECES + (2, 1)], axis=0))
        hidden = jnp.tanh(both[:units])
        grad_pre = both[units:] * (1.0 - hidden * hidden)
        both = jnp.concatenate([hidden, grad_pre], axis=0)
        both = jnp.concatenate(split(both, 2), axis=0)
        sums = sums + times(jnp.concatenate(pieces[:2], axis=0), both, (1, 1))
        result = times(after, both)
        result = result[:16] + result[16:32] + result[32:]
        for turn in range(at_once):
            results.append(result[:8, turn * LANES : (turn + 1) * LANES])
            x = start + turn
            place = (x % x_rows) * x_devices + x // x_rows
            tail_ref[place : place + 1, :] = result[8:9, turn * LANES : (turn + 1) * LANES]

    back_y = by_parts(results, y_back_ref[...])
    back = [jnp.where(row8 < 3, back_y[x], results[x]) for x in range(x_length)]
    back = smooth_rows(back)
    back = [jnp.where(row8 < 6, value, result) for value, result in zip(back, results)]
    for x_device in range(x_devices):
        first = x_device * x_rows
        parts = exchange(back[first : first + x_rows], y_rows)
        for turn in range(y_devices):
            place = (turn * x_devices + x_device) * RETURNED
            out_ref[place : place + 8, :] = parts[turn]
    tails = [tail_ref[x * x_devices : (x + 1) * x_devices, :] for x in range(x_rows)]
    tails = exchange(tails, y_rows)
    for turn in range(y_devices):
        place = turn * x_devices * RETURNED + 8
        out_ref[pl.ds(place, x_devices, stride=RETURNED), :] = tails[turn]

    sums = sums[:, : 2 * units] + sums[:, 2 * units :]
    sums = sums[:16] + sums[16:]
    moved = jnp.concatenate([sums[5:7, units:], STEP_SIZE * sums[13:16, :units]], axis=0)
    packed = jnp.concatenate([sums[:5, units:], moved], axis=1)
    for device in range(x_devices * y_devices):
        place = device * RETURNED + SENT
        out_ref[place : place + 5, :] = packed


def unpack_kernel(
    cells,
    in_ref,
    velocity_ref,
    cotangent_ref,
    z_ref,
    new_ref,
    grad_ref,
    in_grad_ref,
    bias_grad_ref,
    out_grad_ref,
):
    _, x_rows, y_rows, z_length = velocity_ref.shape
    block = x_rows * y_rows
    groups = LANES // block
    devices = z_length // groups
    units = in_grad_ref.shape[1]
    fields = []
    for start in range(0, SENT, groups):
        parts = [
            in_ref[pl.ds(min(field, SENT - 1), devices, stride=RETURNED), :]
            for field in range(start, start + groups)
        ]
        turned = jnp.concatenate(exchange(parts, block), axis=0).T
        fields.extend(turned[turn * block : (turn + 1) * block] for turn in range(groups))
    shape = (3, x_rows, y_rows, z_length)
    forcing = jnp.concatenate(fields[6:9], axis=0).reshape(shape)
    new_ref[...] = velocity_ref[...] + STEP_SIZE * forcing
    back_z = times_table(jnp.concatenate(fields[3:6], axis=0), z_ref[...])
    back = jnp.concatenate(fields[:3], axis=0) + back_z
    grad_ref[...] = cotangent_ref[...] + back.reshape(shape)

    sums = in_ref[SENT : SENT + 5, :]
    for device in range(1, devices):
        place = device * RETURNED + SENT
        sums = sums + in_ref[place : place + 5, :]
    sums = sums * (1.0 / cells)
    in_grad_ref[:5, :] = sums[:, :units]
    in_grad_ref[5:, :] = sums[:1, units:]
    bias_grad_ref[...] = sums[1:2, units:]
    out_grad_ref[...] = sums[2:, units:]


def on_device(kernel, shapes, scratch=(), **more):
    return pl.pallas_call(
        kernel,
        out_shape=[jax.ShapeDtypeStruct(shape, kind) for shape, kind in shapes],
        scratch_shapes=[*scratch],
        compiler_params=pltpu.CompilerParams(vmem_limit_bytes=32 * 1024 * 1024),
        **more,
    )


def fits(velocity, units):
    x_devices, y_devices = lax.axis_size("gx"), lax.axis_size("gy")
    _, x_rows, y_rows, z_length = velocity.shape
    return (
        z_length == LANES
        and x_rows * y_rows * LANES == LANES * LANES // 4
        and x_devices * y_devices * 4 == LANES
        and x_devices == 8
        and y_devices == x_rows
        and y_rows % 8 == 0
        and 2 * units == LANES
    )


def local_kernels(velocity, cotangent, weight_in, bias_in, weight_out):
    axes = ("gy", "gx")
    x_devices, y_devices = lax.axis_size("gx"), lax.axis_size("gy")
    devices = x_devices * y_devices
    _, x_rows, y_rows, z_length = velocity.shape
    units = weight_in.shape[1]
    cells = x_rows * x_devices * y_rows * y_devices * z_length
    z_table = derivative_table(z_length)
    y_table = np.kron(np.eye(z_length // devices), derivative_table(y_rows * y_devices))
    single, half = jnp.float32, jnp.bfloat16

    in_place = pl.BlockSpec(memory_space=pltpu.HBM)

    arguments = [
        velocity,
        cotangent,
        table(z_table.T),
        weight_in,
        bias_in[None],
        weight_out.T,
    ]
    arguments = [pltpu.with_memory_space_constraint(each, pltpu.HBM) for each in arguments]
    sent, *prepared = on_device(
        pack_kernel,
        [
            ((devices * SENT, LANES), single),
            ((2 * units, LANES), half),
            ((48, 4 * units), half),
        ],
        [pltpu.VMEM(values.shape, values.dtype) for values in arguments]
        + [pltpu.SemaphoreType.DMA((len(arguments),))],
        in_specs=[in_place] * len(arguments),
    )(*arguments)
    sent = sent.reshape(devices, 1, SENT * LANES)
    sent = lax.all_to_all(sent, axes, 0, 0, tiled=True).reshape(devices * SENT, LANES)
    (back,) = on_device(
        functools.partial(middle_kernel, x_devices),
        [((devices * RETURNED, LANES), single)],
        [pltpu.VMEM((x_devices * x_rows, LANES), single)],
    )(sent, *prepared, split_table(y_table.T), split_table(y_table))
    back = back.reshape(devices, 1, RETURNED * LANES)
    back = lax.all_to_all(back, axes, 0, 0, tiled=True).reshape(devices * RETURNED, LANES)
    shapes = [velocity.shape, velocity.shape, (6, units), (1, units), (3, units)]
    new, grad, grad_in, grad_bias, grad_out = on_device(
        functools.partial(unpack_kernel, float(cells)), [(shape, single) for shape in shapes]
    )(back, velocity, cotangent, split_table(z_table))
    return (new, grad, grad_in, grad_bias[0], grad_out.T)


def local(velocity, cotangent, weight_in, bias_in, weight_out):
    chosen = local_kernels if fits(velocity, weight_in.shape[1]) else local_plain
    return chosen(velocity, cotangent, weight_in, bias_in, weight_out)


def solution(mesh):
    in_specs = (P(None, "gx", "gy", None), P(None, "gx", "gy", None), P(), P(), P())
    out_specs = (P(None, "gx", "gy", None), P(None, "gx", "gy", None), P(), P(), P())
    return jax.shard_map(local, mesh=mesh, in_specs=in_specs, out_specs=out_specs, check_vma=False)
```

```python
import functools

import jax
import jax.numpy as jnp
import ml_dtypes
import numpy as np
from jax import lax
from jax.experimental import pallas as pl
from jax.experimental.pallas import tpu as pltpu
from jax.sharding import PartitionSpec as P

FILTER_ALPHA = 0.499
FILTER_GAIN = 0.5 + FILTER_ALPHA
COMPACT_ALPHA = 1.0 / 3.0
STEP_SIZE = 0.5
PRECISE = lax.Precision.HIGHEST
LANES = 128
SENT = 9
RETURNED = 14
LEFT_PIECES = (0, 1, 0, 2, 1, 0)
RIGHT_PIECES = (0, 0, 1, 0, 1, 2)


def beside(length, offset):
    return np.eye(length, k=offset) + np.eye(length, k=-offset)


def smooth_table(length):
    left = np.eye(length) + FILTER_ALPHA * beside(length, 1)
    right = FILTER_GAIN * np.eye(length) + 0.5 * FILTER_GAIN * beside(length, 1)
    return np.linalg.solve(left, right)


def derivative_table(length):
    left = np.eye(length) + COMPACT_ALPHA * beside(length, 1)
    right = 7.0 / 9.0 * (np.eye(length, k=1) - np.eye(length, k=-1)) + 1.0 / 36.0 * (
        np.eye(length, k=2) - np.eye(length, k=-2)
    )
    return np.linalg.solve(left, right)


def table(values):
    return jnp.asarray(values.astype(np.float32))


def split_table(values):
    pieces = []
    rest = values.astype(np.float32)
    for _ in range(3):
        pieces.append(rest.astype(ml_dtypes.bfloat16))
        rest = rest - pieces[-1].astype(np.float32)
    return jnp.asarray(np.concatenate([pieces[turn] for turn in RIGHT_PIECES], axis=0))


def local_plain(velocity, cotangent, weight_in, bias_in, weight_out):
    axes = ("gx", "gy")
    x_devices, y_devices = lax.axis_size("gx"), lax.axis_size("gy")
    devices = x_devices * y_devices
    _, x_rows, y_rows, z_length = velocity.shape
    x_length, y_length = x_rows * x_devices, y_rows * y_devices
    units = weight_in.shape[1]
    z_rows = -(-z_length // devices)
    padding = z_rows * devices - z_length

    z_table = table(derivative_table(z_length))
    y_table = table(derivative_table(y_length))
    x_table = table(smooth_table(x_length))

    along_z = jnp.einsum("ab,kxyb->kxya", z_table, velocity, precision=PRECISE)
    fields = jnp.concatenate([velocity, along_z, cotangent], axis=0)
    fields = jnp.pad(fields, ((0, 0), (0, 0), (0, 0), (0, padding)))
    fields = fields.reshape(9, x_rows, y_rows, z_rows, devices)
    fields = fields.transpose(4, 0, 3, 1, 2).reshape(devices, 9, z_rows * x_rows * y_rows)
    fields = lax.all_to_all(fields, axes, 0, 0, tiled=True)
    fields = fields.reshape(x_devices, y_devices, 9, z_rows, x_rows, y_rows)
    fields = fields.transpose(2, 0, 4, 3, 1, 5).reshape(9, x_length, z_rows, y_length)

    smoothed = jnp.einsum("ab,kbzy->kazy", x_table, fields[:6], precision=PRECISE)
    along_y = jnp.einsum("ab,kxzb->kxza", y_table, smoothed[:3], precision=PRECISE)
    features = jnp.concatenate([along_y, smoothed[3:]], axis=0).reshape(6, -1)
    grad_out = STEP_SIZE * fields[6:].reshape(3, -1)

    hidden = jnp.tanh(jnp.dot(weight_in.T, features, precision=PRECISE) + bias_in[:, None])
    forcing = jnp.dot(weight_out.T, hidden, precision=PRECISE)
    grad_pre = jnp.dot(weight_out, grad_out, precision=PRECISE) * (1.0 - hidden * hidden)
    grad_features = jnp.dot(weight_in, grad_pre, precision=PRECISE)
    sum_in = jnp.dot(features, grad_pre.T, precision=PRECISE)
    sum_bias = jnp.sum(grad_pre, axis=1)
    sum_out = jnp.dot(grad_out, hidden.T, precision=PRECISE)

    grad_features = grad_features.reshape(6, x_length, z_rows, y_length)
    back_y = jnp.einsum("ba,kxzb->kxza", y_table, grad_features[:3], precision=PRECISE)
    back = jnp.concatenate([back_y, grad_features[3:]], axis=0)
    back = jnp.einsum("ab,kbzy->kazy", x_table, back, precision=PRECISE)
    back = jnp.concatenate([forcing.reshape(3, x_length, z_rows, y_length), back], axis=0)
    back = back.reshape(9, x_devices, x_rows, z_rows, y_devices, y_rows)
    back = back.transpose(1, 4, 0, 3, 2, 5).reshape(devices, -1)
    sums = jnp.concatenate([sum_in, sum_bias[None], sum_out], axis=0).reshape(1, -1)
    cells = back.shape[1]
    back = jnp.concatenate([back, jnp.broadcast_to(sums, (devices, 10 * units))], axis=1)
    back = lax.all_to_all(back, axes, 0, 0, tiled=True)

    sums = jnp.sum(back[:, cells:], axis=0).reshape(10, units)
    sums = sums / float(x_length * y_length * z_length)
    back = back[:, :cells].reshape(devices, 9, z_rows, x_rows, y_rows)
    back = back.transpose(1, 3, 4, 2, 0).reshape(9, x_rows, y_rows, -1)[..., :z_length]
    new_velocity = velocity + STEP_SIZE * back[:3]
    back_z = jnp.einsum("ba,kxyb->kxya", z_table, back[6:], precision=PRECISE)
    grad_velocity = cotangent + back[3:6] + back_z
    return (new_velocity, grad_velocity, sums[:6], sums[6], sums[7:].T)


def exchange(parts, width):
    parts = list(parts)
    lane = lax.broadcasted_iota(jnp.int32, parts[0].shape, 1)
    step = len(parts) // 2
    while step:
        shift = step * width
        upper = (lane & shift) != 0
        for low in range(len(parts)):
            if low & step == 0:
                first, second = parts[low], parts[low + step]
                parts[low] = jnp.where(upper, pltpu.roll(second, shift, 1), first)
                parts[low + step] = jnp.where(upper, second, pltpu.roll(first, LANES - shift, 1))
        step //= 2
    return parts


def smooth_rows(rows):
    length = len(rows)
    half = length // 2
    scales = []
    before = 0.0
    for _ in range(half):
        scales.append(1.0 / (1.0 - FILTER_ALPHA * FILTER_ALPHA * before))
        before = scales[-1]
    factors = [-FILTER_ALPHA * scale for scale in scales]
    forward = np.cumprod([1.0] + factors[1:])
    backward = np.cumprod([1.0] + factors[-2::-1])[::-1]
    own = 0.5 * FILTER_GAIN / FILTER_ALPHA

    sides = [list(range(half)), list(range(length - 1, half - 1, -1))]
    running = []
    for side in sides:
        sums = []
        for turn, row in enumerate(side):
            value = rows[row] * float(scales[turn] / forward[turn])
            sums.append(value if turn == 0 else sums[-1] + value)
        running.append(sums)
    middle = forward[-1] / (1.0 - factors[-1] * factors[-1])
    cross = middle * factors[-1]
    smoothed = [None] * length
    for side, sums, others in zip(sides, running, running[::-1]):
        value = float(middle) * sums[-1] + float(cross) * others[-1]
        for turn in reversed(range(half)):
            if turn < half - 1:
                value = value + float(forward[turn] / backward[turn]) * sums[turn]
            row = side[turn]
            smoothed[row] = own * rows[row] + float((FILTER_GAIN - own) * backward[turn]) * value
    return smoothed


def times(left, right, contract=(1, 0)):
    dims = (((contract[0],), (contract[1],)), ((), ()))
    return lax.dot_general(left, right, dims, preferred_element_type=jnp.float32)


def split(values, count):
    pieces = []
    for turn in range(count):
        pieces.append(values.astype(jnp.bfloat16))
        if turn + 1 < count:
            values = values - pieces[-1].astype(jnp.float32)
    return pieces


def times_table(values, wide_table):
    pieces = split(values, 3)
    return times(jnp.concatenate([pieces[turn] for turn in LEFT_PIECES], axis=1), wide_table)


def widened(square_table):
    pieces = split(square_table, 3)
    return jnp.concatenate([pieces[turn] for turn in RIGHT_PIECES], axis=0)


def on_rows(rows, wide_table):
    out = times_table(jnp.concatenate(rows, axis=0), wide_table)
    return [out[8 * turn : 8 * turn + 8] for turn in range(len(rows))]


def pack_kernel(
    velocity_hbm,
    cotangent_hbm,
    z_hbm,
    weight_in_hbm,
    bias_hbm,
    weight_out_hbm,
    out_ref,
    before_ref,
    after_ref,
    velocity_ref,
    cotangent_ref,
    z_ref,
    weight_in_ref,
    bias_ref,
    weight_out_ref,
    arrived,
):
    pairs = [
        (weight_in_hbm, weight_in_ref),
        (bias_hbm, bias_ref),
        (weight_out_hbm, weight_out_ref),
        (velocity_hbm, velocity_ref),
        (cotangent_hbm, cotangent_ref),
        (z_hbm, z_ref),
    ]
    copies = [
        pltpu.make_async_copy(source, target, arrived.at[turn])
        for turn, (source, target) in enumerate(pairs)
    ]
    for copy in copies:
        copy.start()

    for copy in copies[:3]:
        copy.wait()
    weight_in = weight_in_ref[...]
    weight_out = weight_out_ref[...]
    units = weight_in.shape[1]
    zeros = functools.partial(jnp.zeros, dtype=jnp.float32)
    before = jnp.concatenate(
        [
            jnp.concatenate([weight_in, bias_ref[...], zeros((9, units))], axis=0),
            jnp.concatenate([zeros((13, units)), STEP_SIZE * weight_out], axis=0),
        ],
        axis=1,
    )
    after = jnp.concatenate(
        [
            jnp.concatenate([zeros((6, units)), weight_out, zeros((7, units))], axis=0),
            jnp.concatenate([weight_in, zeros((10, units))], axis=0),
        ],
        axis=1,
    )
    pieces = [piece.astype(jnp.float32) for piece in split(before, 3)]
    before = jnp.concatenate([pieces[turn] for turn in RIGHT_PIECES + (1, 2)], axis=0)
    before_ref[...] = before.T.astype(jnp.bfloat16)
    pieces = split(after, 3)
    after_ref[...] = jnp.concatenate(
        [
            jnp.concatenate([pieces[0], pieces[0]], axis=1),
            jnp.concatenate([pieces[1], pieces[1]], axis=1),
            jnp.concatenate([pieces[2], jnp.zeros_like(pieces[2])], axis=1),
        ],
        axis=0,
    )

    for copy in copies[3:]:
        copy.wait()
    _, x_rows, y_rows, z_length = velocity_ref.shape
    block = x_rows * y_rows
    groups = LANES // block
    devices = z_length // groups
    velocity = velocity_ref[...].reshape(3 * block, z_length)
    cotangent = cotangent_ref[...].reshape(3 * block, z_length)
    along_z = times_table(velocity, widened(z_ref[...]))
    fill = jnp.zeros(((-SENT % groups) * block, z_length), jnp.float32)
    rows = jnp.concatenate(
        [velocity, along_z, cotangent[block:], cotangent[:block], fill], axis=0
    )
    for start in range(0, SENT, groups):
        turned = rows[start * block : (start + groups) * block].T
        parts = [turned[group * devices : (group + 1) * devices] for group in range(groups)]
        parts = exchange(parts, block)
        for field in range(start, min(start + groups, SENT)):
            out_ref[pl.ds(field, devices, stride=SENT), :] = parts[field - start]


def middle_kernel(x_devices, in_ref, before_ref, after_ref, y_ref, y_back_ref, out_ref, tail_ref):
    y_devices = in_ref.shape[0] // SENT // x_devices
    x_rows = y_devices
    x_length = x_devices * x_rows
    units = before_ref.shape[0] // 2
    y_rows = LANES // y_devices // x_rows
    row8 = lax.broadcasted_iota(jnp.int32, (8, LANES), 0)

    planes = []
    for x_device in range(x_devices):
        places = [(turn * x_devices + x_device) * SENT for turn in range(y_devices)]
        parts = [in_ref[place : place + 8, :] for place in places]
        planes.extend(exchange(parts, y_rows))
    tails = [
        in_ref[pl.ds(turn * x_devices * SENT + 8, x_devices, stride=SENT), :]
        for turn in range(y_devices)
    ]
    tails = exchange(tails, y_rows)

    smoothed = smooth_rows(planes)
    along_y = on_rows(smoothed, y_ref[...])
    upper_rows = []
    lower_rows = []
    for x in range(x_length):
        features = jnp.where(row8 < 3, along_y[x], smoothed[x])
        features = jnp.where(row8 < 6, features, jnp.where(row8 == 6, 1.0, 0.0))
        last = tails[x % x_rows][x // x_rows : x // x_rows + 1]
        upper_rows.append(features)
        lower_rows.append(jnp.where(row8 == 5, last, planes[x]))

    before = before_ref[...]
    after = after_ref[...]
    at_once = x_length
    sums = jnp.zeros((32, 4 * units), jnp.float32)
    results = []
    for start in range(0, x_length, at_once):
        stop = start + at_once
        cells = jnp.concatenate(
            [
                jnp.concatenate(upper_rows[start:stop], axis=1),
                jnp.concatenate(lower_rows[start:stop], axis=1),
            ],
            axis=0,
        )
        pieces = split(cells, 3)
        both = times(before, jnp.concatenate([pieces[turn] for turn in LEFT_PIECES + (2, 1)], axis=0))
        hidden = jnp.tanh(both[:units])
        grad_pre = both[units:] * (1.0 - hidden * hidden)
        both = jnp.concatenate([hidden, grad_pre], axis=0)
        both = jnp.concatenate(split(both, 2), axis=0)
        sums = sums + times(jnp.concatenate(pieces[:2], axis=0), both, (1, 1))
        result = times(after, both)
        result = result[:16] + result[16:32] + result[32:]
        for turn in range(at_once):
            results.append(result[:8, turn * LANES : (turn + 1) * LANES])
            x = start + turn
            place = (x % x_rows) * x_devices + x // x_rows
            tail_ref[place : place + 1, :] = result[8:9, turn * LANES : (turn + 1) * LANES]

    back_y = on_rows(results, y_back_ref[...])
    back = [jnp.where(row8 < 3, back_y[x], results[x]) for x in range(x_length)]
    back = smooth_rows(back)
    back = [jnp.where(row8 < 6, value, result) for value, result in zip(back, results)]
    for x_device in range(x_devices):
        first = x_device * x_rows
        parts = exchange(back[first : first + x_rows], y_rows)
        for turn in range(y_devices):
            place = (turn * x_devices + x_device) * RETURNED
            out_ref[place : place + 8, :] = parts[turn]
    tails = [tail_ref[x * x_devices : (x + 1) * x_devices, :] for x in range(x_rows)]
    tails = exchange(tails, y_rows)
    for turn in range(y_devices):
        place = turn * x_devices * RETURNED + 8
        out_ref[pl.ds(place, x_devices, stride=RETURNED), :] = tails[turn]

    sums = sums[:, : 2 * units] + sums[:, 2 * units :]
    sums = sums[:16] + sums[16:]
    moved = jnp.concatenate([sums[5:7, units:], STEP_SIZE * sums[13:16, :units]], axis=0)
    packed = jnp.concatenate([sums[:5, units:], moved], axis=1)
    for device in range(x_devices * y_devices):
        place = device * RETURNED + SENT
        out_ref[place : place + 5, :] = packed


def unpack_kernel(
    cells,
    in_ref,
    velocity_ref,
    cotangent_ref,
    z_ref,
    new_ref,
    grad_ref,
    in_grad_ref,
    bias_grad_ref,
    out_grad_ref,
):
    _, x_rows, y_rows, z_length = velocity_ref.shape
    block = x_rows * y_rows
    groups = LANES // block
    devices = z_length // groups
    units = in_grad_ref.shape[1]
    fields = []
    for start in range(0, SENT, groups):
        parts = [
            in_ref[pl.ds(min(field, SENT - 1), devices, stride=RETURNED), :]
            for field in range(start, start + groups)
        ]
        turned = jnp.concatenate(exchange(parts, block), axis=0).T
        fields.extend(turned[turn * block : (turn + 1) * block] for turn in range(groups))
    shape = (3, x_rows, y_rows, z_length)
    forcing = jnp.concatenate(fields[6:9], axis=0).reshape(shape)
    new_ref[...] = velocity_ref[...] + STEP_SIZE * forcing
    back_z = times_table(jnp.concatenate(fields[3:6], axis=0), z_ref[...])
    back = jnp.concatenate(fields[:3], axis=0) + back_z
    grad_ref[...] = cotangent_ref[...] + back.reshape(shape)

    sums = in_ref[SENT : SENT + 5, :]
    for device in range(1, devices):
        place = device * RETURNED + SENT
        sums = sums + in_ref[place : place + 5, :]
    sums = sums * (1.0 / cells)
    in_grad_ref[:5, :] = sums[:, :units]
    in_grad_ref[5:, :] = sums[:1, units:]
    bias_grad_ref[...] = sums[1:2, units:]
    out_grad_ref[...] = sums[2:, units:]


def on_device(kernel, shapes, scratch=(), **more):
    return pl.pallas_call(
        kernel,
        out_shape=[jax.ShapeDtypeStruct(shape, kind) for shape, kind in shapes],
        scratch_shapes=[*scratch],
        compiler_params=pltpu.CompilerParams(vmem_limit_bytes=32 * 1024 * 1024),
        **more,
    )


def fits(velocity, units):
    x_devices, y_devices = lax.axis_size("gx"), lax.axis_size("gy")
    _, x_rows, y_rows, z_length = velocity.shape
    return (
        z_length == LANES
        and x_rows * y_rows * LANES == LANES * LANES // 4
        and x_devices * y_devices * 4 == LANES
        and x_devices == 8
        and y_devices == x_rows
        and y_rows % 8 == 0
        and 2 * units == LANES
    )


def local_kernels(velocity, cotangent, weight_in, bias_in, weight_out):
    axes = ("gy", "gx")
    x_devices, y_devices = lax.axis_size("gx"), lax.axis_size("gy")
    devices = x_devices * y_devices
    _, x_rows, y_rows, z_length = velocity.shape
    units = weight_in.shape[1]
    cells = x_rows * x_devices * y_rows * y_devices * z_length
    z_table = derivative_table(z_length)
    y_table = np.kron(np.eye(z_length // devices), derivative_table(y_rows * y_devices))
    single, half = jnp.float32, jnp.bfloat16

    in_place = pl.BlockSpec(memory_space=pltpu.HBM)

    arguments = [
        velocity,
        cotangent,
        table(z_table.T),
        weight_in,
        bias_in[None],
        weight_out.T,
    ]
    arguments = [pltpu.with_memory_space_constraint(each, pltpu.HBM) for each in arguments]
    sent, *prepared = on_device(
        pack_kernel,
        [
            ((devices * SENT, LANES), single),
            ((2 * units, LANES), half),
            ((48, 4 * units), half),
        ],
        [pltpu.VMEM(values.shape, values.dtype) for values in arguments]
        + [pltpu.SemaphoreType.DMA((len(arguments),))],
        in_specs=[in_place] * len(arguments),
    )(*arguments)
    sent = sent.reshape(devices, 1, SENT * LANES)
    sent = lax.all_to_all(sent, axes, 0, 0, tiled=True).reshape(devices * SENT, LANES)
    (back,) = on_device(
        functools.partial(middle_kernel, x_devices),
        [((devices * RETURNED, LANES), single)],
        [pltpu.VMEM((x_devices * x_rows, LANES), single)],
    )(sent, *prepared, split_table(y_table.T), split_table(y_table))
    back = back.reshape(devices, 1, RETURNED * LANES)
    back = lax.all_to_all(back, axes, 0, 0, tiled=True).reshape(devices * RETURNED, LANES)
    shapes = [velocity.shape, velocity.shape, (6, units), (1, units), (3, units)]
    new, grad, grad_in, grad_bias, grad_out = on_device(
        functools.partial(unpack_kernel, float(cells)), [(shape, single) for shape in shapes]
    )(back, velocity, cotangent, split_table(z_table))
    return (new, grad, grad_in, grad_bias[0], grad_out.T)


def local(velocity, cotangent, weight_in, bias_in, weight_out):
    chosen = local_kernels if fits(velocity, weight_in.shape[1]) else local_plain
    return chosen(velocity, cotangent, weight_in, bias_in, weight_out)


def solution(mesh):
    in_specs = (P(None, "gx", "gy", None), P(None, "gx", "gy", None), P(), P(), P())
    out_specs = (P(None, "gx", "gy", None), P(None, "gx", "gy", None), P(), P(), P())
    return jax.shard_map(local, mesh=mesh, in_specs=in_specs, out_specs=out_specs, check_vma=False)
```

```python
import functools

import jax
import jax.numpy as jnp
import ml_dtypes
import numpy as np
from jax import lax
from jax.experimental import pallas as pl
from jax.experimental.pallas import tpu as pltpu
from jax.sharding import PartitionSpec as P

FILTER_ALPHA = 0.499
FILTER_GAIN = 0.5 + FILTER_ALPHA
COMPACT_ALPHA = 1.0 / 3.0
STEP_SIZE = 0.5
PRECISE = lax.Precision.HIGHEST
LANES = 128
SENT = 9
RETURNED = 14
LEFT_PIECES = (0, 1, 0, 2, 1, 0)
RIGHT_PIECES = (0, 0, 1, 0, 1, 2)


def beside(length, offset):
    return np.eye(length, k=offset) + np.eye(length, k=-offset)


def smooth_table(length):
    left = np.eye(length) + FILTER_ALPHA * beside(length, 1)
    right = FILTER_GAIN * np.eye(length) + 0.5 * FILTER_GAIN * beside(length, 1)
    return np.linalg.solve(left, right)


def derivative_table(length):
    left = np.eye(length) + COMPACT_ALPHA * beside(length, 1)
    right = 7.0 / 9.0 * (np.eye(length, k=1) - np.eye(length, k=-1)) + 1.0 / 36.0 * (
        np.eye(length, k=2) - np.eye(length, k=-2)
    )
    return np.linalg.solve(left, right)


def table(values):
    return jnp.asarray(values.astype(np.float32))


def split_table(values):
    pieces = []
    rest = values.astype(np.float32)
    for _ in range(3):
        pieces.append(rest.astype(ml_dtypes.bfloat16))
        rest = rest - pieces[-1].astype(np.float32)
    return jnp.asarray(np.concatenate([pieces[turn] for turn in RIGHT_PIECES], axis=0))


def local_plain(velocity, cotangent, weight_in, bias_in, weight_out):
    axes = ("gx", "gy")
    x_devices, y_devices = lax.axis_size("gx"), lax.axis_size("gy")
    devices = x_devices * y_devices
    _, x_rows, y_rows, z_length = velocity.shape
    x_length, y_length = x_rows * x_devices, y_rows * y_devices
    units = weight_in.shape[1]
    z_rows = -(-z_length // devices)
    padding = z_rows * devices - z_length

    z_table = table(derivative_table(z_length))
    y_table = table(derivative_table(y_length))
    x_table = table(smooth_table(x_length))

    along_z = jnp.einsum("ab,kxyb->kxya", z_table, velocity, precision=PRECISE)
    fields = jnp.concatenate([velocity, along_z, cotangent], axis=0)
    fields = jnp.pad(fields, ((0, 0), (0, 0), (0, 0), (0, padding)))
    fields = fields.reshape(9, x_rows, y_rows, z_rows, devices)
    fields = fields.transpose(4, 0, 3, 1, 2).reshape(devices, 9, z_rows * x_rows * y_rows)
    fields = lax.all_to_all(fields, axes, 0, 0, tiled=True)
    fields = fields.reshape(x_devices, y_devices, 9, z_rows, x_rows, y_rows)
    fields = fields.transpose(2, 0, 4, 3, 1, 5).reshape(9, x_length, z_rows, y_length)

    smoothed = jnp.einsum("ab,kbzy->kazy", x_table, fields[:6], precision=PRECISE)
    along_y = jnp.einsum("ab,kxzb->kxza", y_table, smoothed[:3], precision=PRECISE)
    features = jnp.concatenate([along_y, smoothed[3:]], axis=0).reshape(6, -1)
    grad_out = STEP_SIZE * fields[6:].reshape(3, -1)

    hidden = jnp.tanh(jnp.dot(weight_in.T, features, precision=PRECISE) + bias_in[:, None])
    forcing = jnp.dot(weight_out.T, hidden, precision=PRECISE)
    grad_pre = jnp.dot(weight_out, grad_out, precision=PRECISE) * (1.0 - hidden * hidden)
    grad_features = jnp.dot(weight_in, grad_pre, precision=PRECISE)
    sum_in = jnp.dot(features, grad_pre.T, precision=PRECISE)
    sum_bias = jnp.sum(grad_pre, axis=1)
    sum_out = jnp.dot(grad_out, hidden.T, precision=PRECISE)

    grad_features = grad_features.reshape(6, x_length, z_rows, y_length)
    back_y = jnp.einsum("ba,kxzb->kxza", y_table, grad_features[:3], precision=PRECISE)
    back = jnp.concatenate([back_y, grad_features[3:]], axis=0)
    back = jnp.einsum("ab,kbzy->kazy", x_table, back, precision=PRECISE)
    back = jnp.concatenate([forcing.reshape(3, x_length, z_rows, y_length), back], axis=0)
    back = back.reshape(9, x_devices, x_rows, z_rows, y_devices, y_rows)
    back = back.transpose(1, 4, 0, 3, 2, 5).reshape(devices, -1)
    sums = jnp.concatenate([sum_in, sum_bias[None], sum_out], axis=0).reshape(1, -1)
    cells = back.shape[1]
    back = jnp.concatenate([back, jnp.broadcast_to(sums, (devices, 10 * units))], axis=1)
    back = lax.all_to_all(back, axes, 0, 0, tiled=True)

    sums = jnp.sum(back[:, cells:], axis=0).reshape(10, units)
    sums = sums / float(x_length * y_length * z_length)
    back = back[:, :cells].reshape(devices, 9, z_rows, x_rows, y_rows)
    back = back.transpose(1, 3, 4, 2, 0).reshape(9, x_rows, y_rows, -1)[..., :z_length]
    new_velocity = velocity + STEP_SIZE * back[:3]
    back_z = jnp.einsum("ba,kxyb->kxya", z_table, back[6:], precision=PRECISE)
    grad_velocity = cotangent + back[3:6] + back_z
    return (new_velocity, grad_velocity, sums[:6], sums[6], sums[7:].T)


def exchange(parts, width):
    parts = list(parts)
    lane = lax.broadcasted_iota(jnp.int32, parts[0].shape, 1)
    step = len(parts) // 2
    while step:
        shift = step * width
        upper = (lane & shift) != 0
        for low in range(len(parts)):
            if low & step == 0:
                first, second = parts[low], parts[low + step]
                parts[low] = jnp.where(upper, pltpu.roll(second, shift, 1), first)
                parts[low + step] = jnp.where(upper, second, pltpu.roll(first, LANES - shift, 1))
        step //= 2
    return parts


def smooth_rows(rows):
    length = len(rows)
    half = length // 2
    scales = []
    before = 0.0
    for _ in range(half):
        scales.append(1.0 / (1.0 - FILTER_ALPHA * FILTER_ALPHA * before))
        before = scales[-1]
    factors = [-FILTER_ALPHA * scale for scale in scales]
    forward = np.cumprod([1.0] + factors[1:])
    backward = np.cumprod([1.0] + factors[-2::-1])[::-1]
    own = 0.5 * FILTER_GAIN / FILTER_ALPHA

    sides = [list(range(half)), list(range(length - 1, half - 1, -1))]
    running = []
    for side in sides:
        sums = []
        for turn, row in enumerate(side):
            value = rows[row] * float(scales[turn] / forward[turn])
            sums.append(value if turn == 0 else sums[-1] + value)
        running.append(sums)
    middle = forward[-1] / (1.0 - factors[-1] * factors[-1])
    cross = middle * factors[-1]
    smoothed = [None] * length
    for side, sums, others in zip(sides, running, running[::-1]):
        value = float(middle) * sums[-1] + float(cross) * others[-1]
        for turn in reversed(range(half)):
            if turn < half - 1:
                value = value + float(forward[turn] / backward[turn]) * sums[turn]
            row = side[turn]
            smoothed[row] = own * rows[row] + float((FILTER_GAIN - own) * backward[turn]) * value
    return smoothed


def times(left, right, contract=(1, 0)):
    dims = (((contract[0],), (contract[1],)), ((), ()))
    return lax.dot_general(left, right, dims, preferred_element_type=jnp.float32)


def split(values, count):
    pieces = []
    for turn in range(count):
        pieces.append(values.astype(jnp.bfloat16))
        if turn + 1 < count:
            values = values - pieces[-1].astype(jnp.float32)
    return pieces


def times_table(values, wide_table):
    pieces = split(values, 3)
    return times(jnp.concatenate([pieces[turn] for turn in LEFT_PIECES], axis=1), wide_table)


def widened(square_table):
    pieces = split(square_table, 3)
    return jnp.concatenate([pieces[turn] for turn in RIGHT_PIECES], axis=0)


def on_rows(rows, wide_table):
    out = times_table(jnp.concatenate(rows, axis=0), wide_table)
    return [out[8 * turn : 8 * turn + 8] for turn in range(len(rows))]


def pack_kernel(
    velocity_hbm,
    cotangent_hbm,
    z_hbm,
    weight_in_hbm,
    bias_hbm,
    weight_out_hbm,
    out_ref,
    before_ref,
    after_ref,
    velocity_ref,
    cotangent_ref,
    z_ref,
    weight_in_ref,
    bias_ref,
    weight_out_ref,
    arrived,
):
    pairs = [
        (weight_in_hbm, weight_in_ref),
        (bias_hbm, bias_ref),
        (weight_out_hbm, weight_out_ref),
        (velocity_hbm, velocity_ref),
        (cotangent_hbm, cotangent_ref),
        (z_hbm, z_ref),
    ]
    copies = [
        pltpu.make_async_copy(source, target, arrived.at[turn])
        for turn, (source, target) in enumerate(pairs)
    ]
    for copy in copies:
        copy.start()

    for copy in copies[:3]:
        copy.wait()
    weight_in = weight_in_ref[...]
    weight_out = weight_out_ref[...]
    units = weight_in.shape[1]
    zeros = functools.partial(jnp.zeros, dtype=jnp.float32)
    before = jnp.concatenate(
        [
            jnp.concatenate([weight_in, bias_ref[...], zeros((9, units))], axis=0),
            jnp.concatenate([zeros((13, units)), STEP_SIZE * weight_out], axis=0),
        ],
        axis=1,
    )
    after = jnp.concatenate(
        [
            jnp.concatenate([zeros((6, units)), weight_out, zeros((7, units))], axis=0),
            jnp.concatenate([weight_in, zeros((10, units))], axis=0),
        ],
        axis=1,
    )
    pieces = [piece.astype(jnp.float32) for piece in split(before, 3)]
    before = jnp.concatenate([pieces[turn] for turn in RIGHT_PIECES + (0, 0)], axis=0)
    before_ref[...] = before.T.astype(jnp.bfloat16)
    pieces = split(after, 3)
    after_ref[...] = jnp.concatenate(
        [
            jnp.concatenate([pieces[0], pieces[0]], axis=1),
            jnp.concatenate([pieces[1], pieces[1]], axis=1),
            jnp.concatenate([pieces[2], jnp.zeros_like(pieces[2])], axis=1),
        ],
        axis=0,
    )

    for copy in copies[3:]:
        copy.wait()
    _, x_rows, y_rows, z_length = velocity_ref.shape
    block = x_rows * y_rows
    groups = LANES // block
    devices = z_length // groups
    velocity = velocity_ref[...].reshape(3 * block, z_length)
    cotangent = cotangent_ref[...].reshape(3 * block, z_length)
    along_z = times_table(velocity, widened(z_ref[...]))
    fill = jnp.zeros(((-SENT % groups) * block, z_length), jnp.float32)
    rows = jnp.concatenate(
        [velocity, along_z, cotangent[block:], cotangent[:block], fill], axis=0
    )
    for start in range(0, SENT, groups):
        turned = rows[start * block : (start + groups) * block].T
        parts = [turned[group * devices : (group + 1) * devices] for group in range(groups)]
        parts = exchange(parts, block)
        for field in range(start, min(start + groups, SENT)):
            out_ref[pl.ds(field, devices, stride=SENT), :] = parts[field - start]


def middle_kernel(x_devices, in_ref, before_ref, after_ref, y_ref, y_back_ref, out_ref, tail_ref):
    y_devices = in_ref.shape[0] // SENT // x_devices
    x_rows = y_devices
    x_length = x_devices * x_rows
    units = before_ref.shape[0] // 2
    y_rows = LANES // y_devices // x_rows
    row8 = lax.broadcasted_iota(jnp.int32, (8, LANES), 0)

    planes = []
    for x_device in range(x_devices):
        places = [(turn * x_devices + x_device) * SENT for turn in range(y_devices)]
        parts = [in_ref[place : place + 8, :] for place in places]
        planes.extend(exchange(parts, y_rows))
    tails = [
        in_ref[pl.ds(turn * x_devices * SENT + 8, x_devices, stride=SENT), :]
        for turn in range(y_devices)
    ]
    tails = exchange(tails, y_rows)

    smoothed = smooth_rows(planes)
    along_y = on_rows(smoothed, y_ref[...])
    upper_rows = []
    lower_rows = []
    for x in range(x_length):
        features = jnp.where(row8 < 3, along_y[x], smoothed[x])
        features = jnp.where(row8 < 6, features, jnp.where(row8 == 6, 1.0, 0.0))
        last = tails[x % x_rows][x // x_rows : x // x_rows + 1]
        upper_rows.append(features)
        lower_rows.append(jnp.where(row8 == 5, last, planes[x]))

    before = before_ref[:, : 16 * len(LEFT_PIECES)]
    after = after_ref[...]
    at_once = x_length
    sums = jnp.zeros((4 * units, 32), jnp.float32)
    results = []
    for start in range(0, x_length, at_once):
        stop = start + at_once
        cells = jnp.concatenate(
            [
                jnp.concatenate(upper_rows[start:stop], axis=1),
                jnp.concatenate(lower_rows[start:stop], axis=1),
            ],
            axis=0,
        )
        pieces = split(cells, 3)
        both = times(before, jnp.concatenate([pieces[turn] for turn in LEFT_PIECES], axis=0))
        hidden = jnp.tanh(both[:units])
        grad_pre = both[units:] * (1.0 - hidden * hidden)
        both = jnp.concatenate([hidden, grad_pre], axis=0)
        both = jnp.concatenate(split(both, 2), axis=0)
        sums = sums + times(both, jnp.concatenate(pieces[:2], axis=0), (1, 1))
        result = times(after, both)
        result = result[:16] + result[16:32] + result[32:]
        for turn in range(at_once):
            results.append(result[:8, turn * LANES : (turn + 1) * LANES])
            x = start + turn
            place = (x % x_rows) * x_devices + x // x_rows
            tail_ref[place : place + 1, :] = result[8:9, turn * LANES : (turn + 1) * LANES]

    back_y = on_rows(results, y_back_ref[...])
    back = [jnp.where(row8 < 3, back_y[x], results[x]) for x in range(x_length)]
    back = smooth_rows(back)
    back = [jnp.where(row8 < 6, value, result) for value, result in zip(back, results)]
    for x_device in range(x_devices):
        first = x_device * x_rows
        parts = exchange(back[first : first + x_rows], y_rows)
        for turn in range(y_devices):
            place = (turn * x_devices + x_device) * RETURNED
            out_ref[place : place + 8, :] = parts[turn]
    tails = [tail_ref[x * x_devices : (x + 1) * x_devices, :] for x in range(x_rows)]
    tails = exchange(tails, y_rows)
    for turn in range(y_devices):
        place = turn * x_devices * RETURNED + 8
        out_ref[pl.ds(place, x_devices, stride=RETURNED), :] = tails[turn]

    sums = sums[: 2 * units] + sums[2 * units :]
    fill = jnp.zeros((2 * units, LANES - 32), jnp.float32)
    sums = jnp.concatenate([sums, fill], axis=1).T
    sums = sums[:16] + sums[16:32]
    moved = jnp.concatenate([sums[5:7, units:], STEP_SIZE * sums[13:16, :units]], axis=0)
    packed = jnp.concatenate([sums[:5, units:], moved], axis=1)
    for device in range(x_devices * y_devices):
        place = device * RETURNED + SENT
        out_ref[place : place + 5, :] = packed


def unpack_kernel(
    cells,
    in_ref,
    velocity_ref,
    cotangent_ref,
    z_ref,
    new_ref,
    grad_ref,
    in_grad_ref,
    bias_grad_ref,
    out_grad_ref,
):
    _, x_rows, y_rows, z_length = velocity_ref.shape
    block = x_rows * y_rows
    groups = LANES // block
    devices = z_length // groups
    units = in_grad_ref.shape[1]
    fields = []
    for start in range(0, SENT, groups):
        parts = [
            in_ref[pl.ds(min(field, SENT - 1), devices, stride=RETURNED), :]
            for field in range(start, start + groups)
        ]
        turned = jnp.concatenate(exchange(parts, block), axis=0).T
        fields.extend(turned[turn * block : (turn + 1) * block] for turn in range(groups))
    shape = (3, x_rows, y_rows, z_length)
    forcing = jnp.concatenate(fields[6:9], axis=0).reshape(shape)
    new_ref[...] = velocity_ref[...] + STEP_SIZE * forcing
    back_z = times_table(jnp.concatenate(fields[3:6], axis=0), z_ref[...])
    back = jnp.concatenate(fields[:3], axis=0) + back_z
    grad_ref[...] = cotangent_ref[...] + back.reshape(shape)

    sums = in_ref[SENT : SENT + 5, :]
    for device in range(1, devices):
        place = device * RETURNED + SENT
        sums = sums + in_ref[place : place + 5, :]
    sums = sums * (1.0 / cells)
    in_grad_ref[:5, :] = sums[:, :units]
    in_grad_ref[5:, :] = sums[:1, units:]
    bias_grad_ref[...] = sums[1:2, units:]
    out_grad_ref[...] = sums[2:, units:]


def on_device(kernel, shapes, scratch=(), **more):
    return pl.pallas_call(
        kernel,
        out_shape=[jax.ShapeDtypeStruct(shape, kind) for shape, kind in shapes],
        scratch_shapes=[*scratch],
        compiler_params=pltpu.CompilerParams(vmem_limit_bytes=32 * 1024 * 1024),
        **more,
    )


def fits(velocity, units):
    x_devices, y_devices = lax.axis_size("gx"), lax.axis_size("gy")
    _, x_rows, y_rows, z_length = velocity.shape
    return (
        z_length == LANES
        and x_rows * y_rows * LANES == LANES * LANES // 4
        and x_devices * y_devices * 4 == LANES
        and x_devices == 8
        and y_devices == x_rows
        and y_rows % 8 == 0
        and 2 * units == LANES
    )


def local_kernels(velocity, cotangent, weight_in, bias_in, weight_out):
    axes = ("gy", "gx")
    x_devices, y_devices = lax.axis_size("gx"), lax.axis_size("gy")
    devices = x_devices * y_devices
    _, x_rows, y_rows, z_length = velocity.shape
    units = weight_in.shape[1]
    cells = x_rows * x_devices * y_rows * y_devices * z_length
    z_table = derivative_table(z_length)
    y_table = np.kron(np.eye(z_length // devices), derivative_table(y_rows * y_devices))
    single, half = jnp.float32, jnp.bfloat16

    in_place = pl.BlockSpec(memory_space=pltpu.HBM)

    arguments = [
        velocity,
        cotangent,
        table(z_table.T),
        weight_in,
        bias_in[None],
        weight_out.T,
    ]
    arguments = [pltpu.with_memory_space_constraint(each, pltpu.HBM) for each in arguments]
    sent, *prepared = on_device(
        pack_kernel,
        [
            ((devices * SENT, LANES), single),
            ((2 * units, LANES), half),
            ((48, 4 * units), half),
        ],
        [pltpu.VMEM(values.shape, values.dtype) for values in arguments]
        + [pltpu.SemaphoreType.DMA((len(arguments),))],
        in_specs=[in_place] * len(arguments),
    )(*arguments)
    sent = sent.reshape(devices, 1, SENT * LANES)
    sent = lax.all_to_all(sent, axes, 0, 0, tiled=True).reshape(devices * SENT, LANES)
    (back,) = on_device(
        functools.partial(middle_kernel, x_devices),
        [((devices * RETURNED, LANES), single)],
        [pltpu.VMEM((x_devices * x_rows, LANES), single)],
    )(sent, *prepared, split_table(y_table.T), split_table(y_table))
    back = back.reshape(devices, 1, RETURNED * LANES)
    back = lax.all_to_all(back, axes, 0, 0, tiled=True).reshape(devices * RETURNED, LANES)
    shapes = [velocity.shape, velocity.shape, (6, units), (1, units), (3, units)]
    new, grad, grad_in, grad_bias, grad_out = on_device(
        functools.partial(unpack_kernel, float(cells)), [(shape, single) for shape in shapes]
    )(back, velocity, cotangent, split_table(z_table))
    return (new, grad, grad_in, grad_bias[0], grad_out.T)


def local(velocity, cotangent, weight_in, bias_in, weight_out):
    chosen = local_kernels if fits(velocity, weight_in.shape[1]) else local_plain
    return chosen(velocity, cotangent, weight_in, bias_in, weight_out)


def solution(mesh):
    in_specs = (P(None, "gx", "gy", None), P(None, "gx", "gy", None), P(), P(), P())
    out_specs = (P(None, "gx", "gy", None), P(None, "gx", "gy", None), P(), P(), P())
    return jax.shard_map(local, mesh=mesh, in_specs=in_specs, out_specs=out_specs, check_vma=False)
```

```python
import functools

import jax
import jax.numpy as jnp
import ml_dtypes
import numpy as np
from jax import lax
from jax.experimental import pallas as pl
from jax.experimental.pallas import tpu as pltpu
from jax.sharding import PartitionSpec as P

FILTER_ALPHA = 0.499
FILTER_GAIN = 0.5 + FILTER_ALPHA
COMPACT_ALPHA = 1.0 / 3.0
STEP_SIZE = 0.5
PRECISE = lax.Precision.HIGHEST
LANES = 128
SENT = 9
RETURNED = 14
LEFT_PIECES = (0, 1, 0, 2, 1, 0)
RIGHT_PIECES = (0, 0, 1, 0, 1, 2)


def beside(length, offset):
    return np.eye(length, k=offset) + np.eye(length, k=-offset)


def smooth_table(length):
    left = np.eye(length) + FILTER_ALPHA * beside(length, 1)
    right = FILTER_GAIN * np.eye(length) + 0.5 * FILTER_GAIN * beside(length, 1)
    return np.linalg.solve(left, right)


def derivative_table(length):
    left = np.eye(length) + COMPACT_ALPHA * beside(length, 1)
    right = 7.0 / 9.0 * (np.eye(length, k=1) - np.eye(length, k=-1)) + 1.0 / 36.0 * (
        np.eye(length, k=2) - np.eye(length, k=-2)
    )
    return np.linalg.solve(left, right)


def table(values):
    return jnp.asarray(values.astype(np.float32))


def split_table(values):
    pieces = []
    rest = values.astype(np.float32)
    for _ in range(3):
        pieces.append(rest.astype(ml_dtypes.bfloat16))
        rest = rest - pieces[-1].astype(np.float32)
    return jnp.asarray(np.concatenate([pieces[turn] for turn in RIGHT_PIECES], axis=0))


def local_plain(velocity, cotangent, weight_in, bias_in, weight_out):
    axes = ("gx", "gy")
    x_devices, y_devices = lax.axis_size("gx"), lax.axis_size("gy")
    devices = x_devices * y_devices
    _, x_rows, y_rows, z_length = velocity.shape
    x_length, y_length = x_rows * x_devices, y_rows * y_devices
    units = weight_in.shape[1]
    z_rows = -(-z_length // devices)
    padding = z_rows * devices - z_length

    z_table = table(derivative_table(z_length))
    y_table = table(derivative_table(y_length))
    x_table = table(smooth_table(x_length))

    along_z = jnp.einsum("ab,kxyb->kxya", z_table, velocity, precision=PRECISE)
    fields = jnp.concatenate([velocity, along_z, cotangent], axis=0)
    fields = jnp.pad(fields, ((0, 0), (0, 0), (0, 0), (0, padding)))
    fields = fields.reshape(9, x_rows, y_rows, z_rows, devices)
    fields = fields.transpose(4, 0, 3, 1, 2).reshape(devices, 9, z_rows * x_rows * y_rows)
    fields = lax.all_to_all(fields, axes, 0, 0, tiled=True)
    fields = fields.reshape(x_devices, y_devices, 9, z_rows, x_rows, y_rows)
    fields = fields.transpose(2, 0, 4, 3, 1, 5).reshape(9, x_length, z_rows, y_length)

    smoothed = jnp.einsum("ab,kbzy->kazy", x_table, fields[:6], precision=PRECISE)
    along_y = jnp.einsum("ab,kxzb->kxza", y_table, smoothed[:3], precision=PRECISE)
    features = jnp.concatenate([along_y, smoothed[3:]], axis=0).reshape(6, -1)
    grad_out = STEP_SIZE * fields[6:].reshape(3, -1)

    hidden = jnp.tanh(jnp.dot(weight_in.T, features, precision=PRECISE) + bias_in[:, None])
    forcing = jnp.dot(weight_out.T, hidden, precision=PRECISE)
    grad_pre = jnp.dot(weight_out, grad_out, precision=PRECISE) * (1.0 - hidden * hidden)
    grad_features = jnp.dot(weight_in, grad_pre, precision=PRECISE)
    sum_in = jnp.dot(features, grad_pre.T, precision=PRECISE)
    sum_bias = jnp.sum(grad_pre, axis=1)
    sum_out = jnp.dot(grad_out, hidden.T, precision=PRECISE)

    grad_features = grad_features.reshape(6, x_length, z_rows, y_length)
    back_y = jnp.einsum("ba,kxzb->kxza", y_table, grad_features[:3], precision=PRECISE)
    back = jnp.concatenate([back_y, grad_features[3:]], axis=0)
    back = jnp.einsum("ab,kbzy->kazy", x_table, back, precision=PRECISE)
    back = jnp.concatenate([forcing.reshape(3, x_length, z_rows, y_length), back], axis=0)
    back = back.reshape(9, x_devices, x_rows, z_rows, y_devices, y_rows)
    back = back.transpose(1, 4, 0, 3, 2, 5).reshape(devices, -1)
    sums = jnp.concatenate([sum_in, sum_bias[None], sum_out], axis=0).reshape(1, -1)
    cells = back.shape[1]
    back = jnp.concatenate([back, jnp.broadcast_to(sums, (devices, 10 * units))], axis=1)
    back = lax.all_to_all(back, axes, 0, 0, tiled=True)

    sums = jnp.sum(back[:, cells:], axis=0).reshape(10, units)
    sums = sums / float(x_length * y_length * z_length)
    back = back[:, :cells].reshape(devices, 9, z_rows, x_rows, y_rows)
    back = back.transpose(1, 3, 4, 2, 0).reshape(9, x_rows, y_rows, -1)[..., :z_length]
    new_velocity = velocity + STEP_SIZE * back[:3]
    back_z = jnp.einsum("ba,kxyb->kxya", z_table, back[6:], precision=PRECISE)
    grad_velocity = cotangent + back[3:6] + back_z
    return (new_velocity, grad_velocity, sums[:6], sums[6], sums[7:].T)


def exchange(parts, width):
    parts = list(parts)
    lane = lax.broadcasted_iota(jnp.int32, parts[0].shape, 1)
    step = len(parts) // 2
    while step:
        shift = step * width
        upper = (lane & shift) != 0
        for low in range(len(parts)):
            if low & step == 0:
                first, second = parts[low], parts[low + step]
                parts[low] = jnp.where(upper, pltpu.roll(second, shift, 1), first)
                parts[low + step] = jnp.where(upper, second, pltpu.roll(first, LANES - shift, 1))
        step //= 2
    return parts


def smooth_rows(rows):
    length = len(rows)
    half = length // 2
    scales = []
    before = 0.0
    for _ in range(half):
        scales.append(1.0 / (1.0 - FILTER_ALPHA * FILTER_ALPHA * before))
        before = scales[-1]
    factors = [-FILTER_ALPHA * scale for scale in scales]
    forward = np.cumprod([1.0] + factors[1:])
    backward = np.cumprod([1.0] + factors[-2::-1])[::-1]
    own = 0.5 * FILTER_GAIN / FILTER_ALPHA

    sides = [list(range(half)), list(range(length - 1, half - 1, -1))]
    running = []
    for side in sides:
        sums = []
        for turn, row in enumerate(side):
            value = rows[row] * float(scales[turn] / forward[turn])
            sums.append(value if turn == 0 else sums[-1] + value)
        running.append(sums)
    middle = forward[-1] / (1.0 - factors[-1] * factors[-1])
    cross = middle * factors[-1]
    smoothed = [None] * length
    for side, sums, others in zip(sides, running, running[::-1]):
        value = float(middle) * sums[-1] + float(cross) * others[-1]
        for turn in reversed(range(half)):
            if turn < half - 1:
                value = value + float(forward[turn] / backward[turn]) * sums[turn]
            row = side[turn]
            smoothed[row] = own * rows[row] + float((FILTER_GAIN - own) * backward[turn]) * value
    return smoothed


def times(left, right, contract=(1, 0)):
    dims = (((contract[0],), (contract[1],)), ((), ()))
    return lax.dot_general(left, right, dims, preferred_element_type=jnp.float32)


def split(values, count):
    pieces = []
    for turn in range(count):
        pieces.append(values.astype(jnp.bfloat16))
        if turn + 1 < count:
            values = values - pieces[-1].astype(jnp.float32)
    return pieces


def times_table(values, wide_table):
    pieces = split(values, 3)
    return times(jnp.concatenate([pieces[turn] for turn in LEFT_PIECES], axis=1), wide_table)


def widened(square_table):
    pieces = split(square_table, 3)
    return jnp.concatenate([pieces[turn] for turn in RIGHT_PIECES], axis=0)


def on_rows(rows, wide_table):
    out = times_table(jnp.concatenate(rows, axis=0), wide_table)
    return [out[8 * turn : 8 * turn + 8] for turn in range(len(rows))]


def pack_kernel(
    velocity_hbm,
    cotangent_hbm,
    z_hbm,
    weight_in_hbm,
    bias_hbm,
    weight_out_hbm,
    out_ref,
    before_ref,
    after_ref,
    velocity_ref,
    cotangent_ref,
    z_ref,
    weight_in_ref,
    bias_ref,
    weight_out_ref,
    arrived,
):
    pairs = [
        (weight_in_hbm, weight_in_ref),
        (bias_hbm, bias_ref),
        (weight_out_hbm, weight_out_ref),
        (velocity_hbm, velocity_ref),
        (cotangent_hbm, cotangent_ref),
        (z_hbm, z_ref),
    ]
    copies = [
        pltpu.make_async_copy(source, target, arrived.at[turn])
        for turn, (source, target) in enumerate(pairs)
    ]
    for copy in copies:
        copy.start()

    for copy in copies[:3]:
        copy.wait()
    weight_in = weight_in_ref[...]
    weight_out = weight_out_ref[...]
    units = weight_in.shape[1]
    zeros = functools.partial(jnp.zeros, dtype=jnp.float32)
    before = jnp.concatenate(
        [
            jnp.concatenate([weight_in, bias_ref[...], zeros((9, units))], axis=0),
            jnp.concatenate([zeros((13, units)), STEP_SIZE * weight_out], axis=0),
        ],
        axis=1,
    )
    after = jnp.concatenate(
        [
            jnp.concatenate([zeros((6, units)), weight_out, zeros((7, units))], axis=0),
            jnp.concatenate([weight_in, zeros((10, units))], axis=0),
        ],
        axis=1,
    )
    pieces = [piece.astype(jnp.float32) for piece in split(before, 3)]
    before = jnp.concatenate([pieces[turn] for turn in RIGHT_PIECES + (1, 2)], axis=0)
    before_ref[...] = before.T.astype(jnp.bfloat16)
    pieces = split(after, 3)
    after_ref[...] = jnp.concatenate(
        [
            jnp.concatenate([pieces[0], pieces[0]], axis=1),
            jnp.concatenate([pieces[1], pieces[1]], axis=1),
            jnp.concatenate([pieces[2], jnp.zeros_like(pieces[2])], axis=1),
        ],
        axis=0,
    )

    for copy in copies[3:]:
        copy.wait()
    _, x_rows, y_rows, z_length = velocity_ref.shape
    block = x_rows * y_rows
    groups = LANES // block
    devices = z_length // groups
    velocity = velocity_ref[...].reshape(3 * block, z_length)
    cotangent = cotangent_ref[...].reshape(3 * block, z_length)
    along_z = times_table(velocity, widened(z_ref[...]))
    fill = jnp.zeros(((-SENT % groups) * block, z_length), jnp.float32)
    rows = jnp.concatenate(
        [velocity, along_z, cotangent[block:], cotangent[:block], fill], axis=0
    )
    for start in range(0, SENT, groups):
        turned = rows[start * block : (start + groups) * block].T
        parts = [turned[group * devices : (group + 1) * devices] for group in range(groups)]
        parts = exchange(parts, block)
        for field in range(start, min(start + groups, SENT)):
            out_ref[pl.ds(field, devices, stride=SENT), :] = parts[field - start]


def middle_kernel(x_devices, in_ref, before_ref, after_ref, y_ref, y_back_ref, out_ref, tail_ref):
    y_devices = in_ref.shape[0] // SENT // x_devices
    x_rows = y_devices
    x_length = x_devices * x_rows
    units = before_ref.shape[0] // 2
    y_rows = LANES // y_devices // x_rows
    row8 = lax.broadcasted_iota(jnp.int32, (8, LANES), 0)

    planes = []
    for x_device in range(x_devices):
        places = [(turn * x_devices + x_device) * SENT for turn in range(y_devices)]
        parts = [in_ref[place : place + 8, :] for place in places]
        planes.extend(exchange(parts, y_rows))
    tails = [
        in_ref[pl.ds(turn * x_devices * SENT + 8, x_devices, stride=SENT), :]
        for turn in range(y_devices)
    ]
    tails = exchange(tails, y_rows)

    smoothed = smooth_rows(planes)
    along_y = on_rows(smoothed, y_ref[...])
    upper_rows = []
    lower_rows = []
    for x in range(x_length):
        features = jnp.where(row8 < 3, along_y[x], smoothed[x])
        features = jnp.where(row8 < 6, features, jnp.where(row8 == 6, 1.0, 0.0))
        last = tails[x % x_rows][x // x_rows : x // x_rows + 1]
        upper_rows.append(features)
        lower_rows.append(jnp.where(row8 == 5, last, planes[x]))

    before = before_ref[...]
    after = after_ref[...]
    at_once = x_length
    sums = jnp.zeros((32, 4 * units), jnp.float32)
    results = []
    for start in range(0, x_length, at_once):
        stop = start + at_once
        cells = jnp.concatenate(
            [
                jnp.concatenate(upper_rows[start:stop], axis=1),
                jnp.concatenate(lower_rows[start:stop], axis=1),
            ],
            axis=0,
        )
        pieces = split(cells, 3)
        both = times(before, jnp.concatenate([pieces[turn] for turn in LEFT_PIECES + (2, 1)], axis=0))
        hidden = jnp.tanh(both[:units])
        grad_pre = both[units:] * (1.0 - hidden * hidden)
        both = jnp.concatenate([hidden, grad_pre], axis=0)
        both = jnp.concatenate(split(both, 2), axis=0)
        sums = sums + times(jnp.concatenate(pieces[:2], axis=0), both, (1, 1))
        result = times(after, both)
        result = result[:16] + result[16:32] + result[32:]
        for turn in range(at_once):
            results.append(result[:8, turn * LANES : (turn + 1) * LANES])
            x = start + turn
            place = (x % x_rows) * x_devices + x // x_rows
            tail_ref[place : place + 1, :] = result[8:9, turn * LANES : (turn + 1) * LANES]

    back_y = on_rows(results, y_back_ref[...])
    back = [jnp.where(row8 < 3, back_y[x], results[x]) for x in range(x_length)]
    back = smooth_rows(back)
    back = [jnp.where(row8 < 6, value, result) for value, result in zip(back, results)]
    for x_device in range(x_devices):
        first = x_device * x_rows
        parts = exchange(back[first : first + x_rows], y_rows)
        for turn in range(y_devices):
            place = (x_device * y_devices + turn) * RETURNED
            out_ref[place : place + 8, :] = parts[turn]
    tails = [tail_ref[x * x_devices : (x + 1) * x_devices, :] for x in range(x_rows)]
    tails = exchange(tails, y_rows)
    for turn in range(y_devices):
        place = turn * RETURNED + 8
        out_ref[pl.ds(place, x_devices, stride=y_devices * RETURNED), :] = tails[turn]

    sums = sums[:, : 2 * units] + sums[:, 2 * units :]
    sums = sums[:16] + sums[16:]
    moved = jnp.concatenate([sums[5:7, units:], STEP_SIZE * sums[13:16, :units]], axis=0)
    packed = jnp.concatenate([sums[:5, units:], moved], axis=1)
    for device in range(x_devices * y_devices):
        place = device * RETURNED + SENT
        out_ref[place : place + 5, :] = packed


def unpack_kernel(
    x_devices,
    cells,
    in_ref,
    velocity_ref,
    cotangent_ref,
    z_ref,
    new_ref,
    grad_ref,
    in_grad_ref,
    bias_grad_ref,
    out_grad_ref,
):
    _, x_rows, y_rows, z_length = velocity_ref.shape
    block = x_rows * y_rows
    groups = LANES // block
    devices = z_length // groups
    units = in_grad_ref.shape[1]
    stride = devices // x_devices * RETURNED
    fields = []
    for start in range(0, SENT, groups):
        parts = []
        for field in range(start, start + groups):
            rows = [
                in_ref[pl.ds(place + min(field, SENT - 1), x_devices, stride=stride), :]
                for place in range(0, stride, RETURNED)
            ]
            parts.append(jnp.concatenate(rows, axis=0))
        turned = jnp.concatenate(exchange(parts, block), axis=0).T
        fields.extend(turned[turn * block : (turn + 1) * block] for turn in range(groups))
    shape = (3, x_rows, y_rows, z_length)
    forcing = jnp.concatenate(fields[6:9], axis=0).reshape(shape)
    new_ref[...] = velocity_ref[...] + STEP_SIZE * forcing
    back_z = times_table(jnp.concatenate(fields[3:6], axis=0), z_ref[...])
    back = jnp.concatenate(fields[:3], axis=0) + back_z
    grad_ref[...] = cotangent_ref[...] + back.reshape(shape)

    sums = in_ref[SENT : SENT + 5, :]
    for device in range(1, devices):
        place = device * RETURNED + SENT
        sums = sums + in_ref[place : place + 5, :]
    sums = sums * (1.0 / cells)
    in_grad_ref[:5, :] = sums[:, :units]
    in_grad_ref[5:, :] = sums[:1, units:]
    bias_grad_ref[...] = sums[1:2, units:]
    out_grad_ref[...] = sums[2:, units:]


def on_device(kernel, shapes, scratch=(), **more):
    return pl.pallas_call(
        kernel,
        out_shape=[jax.ShapeDtypeStruct(shape, kind) for shape, kind in shapes],
        scratch_shapes=[*scratch],
        compiler_params=pltpu.CompilerParams(vmem_limit_bytes=32 * 1024 * 1024),
        **more,
    )


def fits(velocity, units):
    x_devices, y_devices = lax.axis_size("gx"), lax.axis_size("gy")
    _, x_rows, y_rows, z_length = velocity.shape
    return (
        z_length == LANES
        and x_rows * y_rows * LANES == LANES * LANES // 4
        and x_devices * y_devices * 4 == LANES
        and x_devices == 8
        and y_devices == x_rows
        and y_rows % 8 == 0
        and 2 * units == LANES
    )


def local_kernels(velocity, cotangent, weight_in, bias_in, weight_out):
    x_devices, y_devices = lax.axis_size("gx"), lax.axis_size("gy")
    devices = x_devices * y_devices
    _, x_rows, y_rows, z_length = velocity.shape
    units = weight_in.shape[1]
    cells = x_rows * x_devices * y_rows * y_devices * z_length
    z_table = derivative_table(z_length)
    y_table = np.kron(np.eye(z_length // devices), derivative_table(y_rows * y_devices))
    single, half = jnp.float32, jnp.bfloat16

    in_place = pl.BlockSpec(memory_space=pltpu.HBM)

    arguments = [
        velocity,
        cotangent,
        table(z_table.T),
        weight_in,
        bias_in[None],
        weight_out.T,
    ]
    arguments = [pltpu.with_memory_space_constraint(each, pltpu.HBM) for each in arguments]
    sent, *prepared = on_device(
        pack_kernel,
        [
            ((devices * SENT, LANES), single),
            ((2 * units, LANES), half),
            ((48, 4 * units), half),
        ],
        [pltpu.VMEM(values.shape, values.dtype) for values in arguments]
        + [pltpu.SemaphoreType.DMA((len(arguments),))],
        in_specs=[in_place] * len(arguments),
    )(*arguments)
    sent = sent.reshape(devices, 1, SENT * LANES)
    sent = lax.all_to_all(sent, ("gy", "gx"), 0, 0, tiled=True)
    sent = sent.reshape(devices * SENT, LANES)
    (back,) = on_device(
        functools.partial(middle_kernel, x_devices),
        [((devices * RETURNED, LANES), single)],
        [pltpu.VMEM((x_devices * x_rows, LANES), single)],
    )(sent, *prepared, split_table(y_table.T), split_table(y_table))
    back = back.reshape(devices, 1, RETURNED * LANES)
    back = lax.all_to_all(back, ("gx", "gy"), 0, 0, tiled=True)
    back = back.reshape(devices * RETURNED, LANES)
    shapes = [velocity.shape, velocity.shape, (6, units), (1, units), (3, units)]
    new, grad, grad_in, grad_bias, grad_out = on_device(
        functools.partial(unpack_kernel, x_devices, float(cells)), [(shape, single) for shape in shapes]
    )(back, velocity, cotangent, split_table(z_table))
    return (new, grad, grad_in, grad_bias[0], grad_out.T)


def local(velocity, cotangent, weight_in, bias_in, weight_out):
    chosen = local_kernels if fits(velocity, weight_in.shape[1]) else local_plain
    return chosen(velocity, cotangent, weight_in, bias_in, weight_out)


def solution(mesh):
    in_specs = (P(None, "gx", "gy", None), P(None, "gx", "gy", None), P(), P(), P())
    out_specs = (P(None, "gx", "gy", None), P(None, "gx", "gy", None), P(), P(), P())
    return jax.shard_map(local, mesh=mesh, in_specs=in_specs, out_specs=out_specs, check_vma=False)
```

```python
import functools

import jax
import jax.numpy as jnp
import ml_dtypes
import numpy as np
from jax import lax
from jax.experimental import pallas as pl
from jax.experimental.pallas import tpu as pltpu
from jax.sharding import PartitionSpec as P

FILTER_ALPHA = 0.499
FILTER_GAIN = 0.5 + FILTER_ALPHA
COMPACT_ALPHA = 1.0 / 3.0
STEP_SIZE = 0.5
PRECISE = lax.Precision.HIGHEST
LANES = 128
SENT = 9
RETURNED = 14
LEFT_PIECES = (0, 1, 0, 2, 1, 0)
RIGHT_PIECES = (0, 0, 1, 0, 1, 2)


def beside(length, offset):
    return np.eye(length, k=offset) + np.eye(length, k=-offset)


def smooth_table(length):
    left = np.eye(length) + FILTER_ALPHA * beside(length, 1)
    right = FILTER_GAIN * np.eye(length) + 0.5 * FILTER_GAIN * beside(length, 1)
    return np.linalg.solve(left, right)


def derivative_table(length):
    left = np.eye(length) + COMPACT_ALPHA * beside(length, 1)
    right = 7.0 / 9.0 * (np.eye(length, k=1) - np.eye(length, k=-1)) + 1.0 / 36.0 * (
        np.eye(length, k=2) - np.eye(length, k=-2)
    )
    return np.linalg.solve(left, right)


def table(values):
    return jnp.asarray(values.astype(np.float32))


def split_table(values):
    pieces = []
    rest = values.astype(np.float32)
    for _ in range(3):
        pieces.append(rest.astype(ml_dtypes.bfloat16))
        rest = rest - pieces[-1].astype(np.float32)
    return jnp.asarray(np.concatenate([pieces[turn] for turn in RIGHT_PIECES], axis=0))


def local_plain(velocity, cotangent, weight_in, bias_in, weight_out):
    axes = ("gx", "gy")
    x_devices, y_devices = lax.axis_size("gx"), lax.axis_size("gy")
    devices = x_devices * y_devices
    _, x_rows, y_rows, z_length = velocity.shape
    x_length, y_length = x_rows * x_devices, y_rows * y_devices
    units = weight_in.shape[1]
    z_rows = -(-z_length // devices)
    padding = z_rows * devices - z_length

    z_table = table(derivative_table(z_length))
    y_table = table(derivative_table(y_length))
    x_table = table(smooth_table(x_length))

    along_z = jnp.einsum("ab,kxyb->kxya", z_table, velocity, precision=PRECISE)
    fields = jnp.concatenate([velocity, along_z, cotangent], axis=0)
    fields = jnp.pad(fields, ((0, 0), (0, 0), (0, 0), (0, padding)))
    fields = fields.reshape(9, x_rows, y_rows, z_rows, devices)
    fields = fields.transpose(4, 0, 3, 1, 2).reshape(devices, 9, z_rows * x_rows * y_rows)
    fields = lax.all_to_all(fields, axes, 0, 0, tiled=True)
    fields = fields.reshape(x_devices, y_devices, 9, z_rows, x_rows, y_rows)
    fields = fields.transpose(2, 0, 4, 3, 1, 5).reshape(9, x_length, z_rows, y_length)

    smoothed = jnp.einsum("ab,kbzy->kazy", x_table, fields[:6], precision=PRECISE)
    along_y = jnp.einsum("ab,kxzb->kxza", y_table, smoothed[:3], precision=PRECISE)
    features = jnp.concatenate([along_y, smoothed[3:]], axis=0).reshape(6, -1)
    grad_out = STEP_SIZE * fields[6:].reshape(3, -1)

    hidden = jnp.tanh(jnp.dot(weight_in.T, features, precision=PRECISE) + bias_in[:, None])
    forcing = jnp.dot(weight_out.T, hidden, precision=PRECISE)
    grad_pre = jnp.dot(weight_out, grad_out, precision=PRECISE) * (1.0 - hidden * hidden)
    grad_features = jnp.dot(weight_in, grad_pre, precision=PRECISE)
    sum_in = jnp.dot(features, grad_pre.T, precision=PRECISE)
    sum_bias = jnp.sum(grad_pre, axis=1)
    sum_out = jnp.dot(grad_out, hidden.T, precision=PRECISE)

    grad_features = grad_features.reshape(6, x_length, z_rows, y_length)
    back_y = jnp.einsum("ba,kxzb->kxza", y_table, grad_features[:3], precision=PRECISE)
    back = jnp.concatenate([back_y, grad_features[3:]], axis=0)
    back = jnp.einsum("ab,kbzy->kazy", x_table, back, precision=PRECISE)
    back = jnp.concatenate([forcing.reshape(3, x_length, z_rows, y_length), back], axis=0)
    back = back.reshape(9, x_devices, x_rows, z_rows, y_devices, y_rows)
    back = back.transpose(1, 4, 0, 3, 2, 5).reshape(devices, -1)
    sums = jnp.concatenate([sum_in, sum_bias[None], sum_out], axis=0).reshape(1, -1)
    cells = back.shape[1]
    back = jnp.concatenate([back, jnp.broadcast_to(sums, (devices, 10 * units))], axis=1)
    back = lax.all_to_all(back, axes, 0, 0, tiled=True)

    sums = jnp.sum(back[:, cells:], axis=0).reshape(10, units)
    sums = sums / float(x_length * y_length * z_length)
    back = back[:, :cells].reshape(devices, 9, z_rows, x_rows, y_rows)
    back = back.transpose(1, 3, 4, 2, 0).reshape(9, x_rows, y_rows, -1)[..., :z_length]
    new_velocity = velocity + STEP_SIZE * back[:3]
    back_z = jnp.einsum("ba,kxyb->kxya", z_table, back[6:], precision=PRECISE)
    grad_velocity = cotangent + back[3:6] + back_z
    return (new_velocity, grad_velocity, sums[:6], sums[6], sums[7:].T)


def exchange(parts, width):
    parts = list(parts)
    lane = lax.broadcasted_iota(jnp.int32, parts[0].shape, 1)
    step = len(parts) // 2
    while step:
        shift = step * width
        upper = (lane & shift) != 0
        for low in range(len(parts)):
            if low & step == 0:
                first, second = parts[low], parts[low + step]
                parts[low] = jnp.where(upper, pltpu.roll(second, shift, 1), first)
                parts[low + step] = jnp.where(upper, second, pltpu.roll(first, LANES - shift, 1))
        step //= 2
    return parts


def smooth_rows(rows):
    length = len(rows)
    half = length // 2
    scales = []
    before = 0.0
    for _ in range(half):
        scales.append(1.0 / (1.0 - FILTER_ALPHA * FILTER_ALPHA * before))
        before = scales[-1]
    factors = [-FILTER_ALPHA * scale for scale in scales]
    forward = np.cumprod([1.0] + factors[1:])
    backward = np.cumprod([1.0] + factors[-2::-1])[::-1]
    own = 0.5 * FILTER_GAIN / FILTER_ALPHA

    sides = [list(range(half)), list(range(length - 1, half - 1, -1))]
    running = []
    for side in sides:
        sums = []
        for turn, row in enumerate(side):
            value = rows[row] * float(scales[turn] / forward[turn])
            sums.append(value if turn == 0 else sums[-1] + value)
        running.append(sums)
    middle = forward[-1] / (1.0 - factors[-1] * factors[-1])
    cross = middle * factors[-1]
    smoothed = [None] * length
    for side, sums, others in zip(sides, running, running[::-1]):
        value = float(middle) * sums[-1] + float(cross) * others[-1]
        for turn in reversed(range(half)):
            if turn < half - 1:
                value = value + float(forward[turn] / backward[turn]) * sums[turn]
            row = side[turn]
            smoothed[row] = own * rows[row] + float((FILTER_GAIN - own) * backward[turn]) * value
    return smoothed


def times(left, right, contract=(1, 0)):
    dims = (((contract[0],), (contract[1],)), ((), ()))
    return lax.dot_general(left, right, dims, preferred_element_type=jnp.float32)


def split(values, count):
    pieces = []
    for turn in range(count):
        pieces.append(values.astype(jnp.bfloat16))
        if turn + 1 < count:
            values = values - pieces[-1].astype(jnp.float32)
    return pieces


def times_table(values, wide_table):
    pieces = split(values, 3)
    return times(jnp.concatenate([pieces[turn] for turn in LEFT_PIECES], axis=1), wide_table)


def widened(square_table):
    pieces = split(square_table, 3)
    return jnp.concatenate([pieces[turn] for turn in RIGHT_PIECES], axis=0)


def on_rows(rows, wide_table):
    out = times_table(jnp.concatenate(rows, axis=0), wide_table)
    return [out[8 * turn : 8 * turn + 8] for turn in range(len(rows))]


def pack_kernel(
    velocity_hbm,
    cotangent_hbm,
    z_hbm,
    weight_in_hbm,
    bias_hbm,
    weight_out_hbm,
    out_ref,
    before_ref,
    after_ref,
    velocity_ref,
    cotangent_ref,
    z_ref,
    weight_in_ref,
    bias_ref,
    weight_out_ref,
    arrived,
):
    pairs = [
        (weight_in_hbm, weight_in_ref),
        (bias_hbm, bias_ref),
        (weight_out_hbm, weight_out_ref),
    ]
    pairs += [
        (whole.at[part], held.at[part])
        for whole, held in ((velocity_hbm, velocity_ref), (cotangent_hbm, cotangent_ref))
        for part in range(3)
    ]
    half = z_ref.shape[0] // 2
    pairs += [(z_hbm.at[part], z_ref.at[part]) for part in (pl.ds(0, half), pl.ds(half, half))]
    copies = [
        pltpu.make_async_copy(source, target, arrived.at[turn])
        for turn, (source, target) in enumerate(pairs)
    ]
    for copy in copies:
        copy.start()

    for copy in copies[:3]:
        copy.wait()
    weight_in = weight_in_ref[...]
    weight_out = weight_out_ref[...]
    units = weight_in.shape[1]
    zeros = functools.partial(jnp.zeros, dtype=jnp.float32)
    before = jnp.concatenate(
        [
            jnp.concatenate([weight_in, bias_ref[...], zeros((9, units))], axis=0),
            jnp.concatenate([zeros((13, units)), STEP_SIZE * weight_out], axis=0),
        ],
        axis=1,
    )
    after = jnp.concatenate(
        [
            jnp.concatenate([zeros((6, units)), weight_out, zeros((7, units))], axis=0),
            jnp.concatenate([weight_in, zeros((10, units))], axis=0),
        ],
        axis=1,
    )
    pieces = [piece.astype(jnp.float32) for piece in split(before, 3)]
    before = jnp.concatenate([pieces[turn] for turn in RIGHT_PIECES + (1, 2)], axis=0)
    before_ref[...] = before.T.astype(jnp.bfloat16)
    pieces = split(after, 3)
    after_ref[...] = jnp.concatenate(
        [
            jnp.concatenate([pieces[0], pieces[0]], axis=1),
            jnp.concatenate([pieces[1], pieces[1]], axis=1),
            jnp.concatenate([pieces[2], jnp.zeros_like(pieces[2])], axis=1),
        ],
        axis=0,
    )

    for copy in copies[3:]:
        copy.wait()
    _, x_rows, y_rows, z_length = velocity_ref.shape
    block = x_rows * y_rows
    groups = LANES // block
    devices = z_length // groups
    velocity = velocity_ref[...].reshape(3 * block, z_length)
    cotangent = cotangent_ref[...].reshape(3 * block, z_length)
    along_z = times_table(velocity, widened(z_ref[...]))
    fill = jnp.zeros(((-SENT % groups) * block, z_length), jnp.float32)
    rows = jnp.concatenate(
        [velocity, along_z, cotangent[block:], cotangent[:block], fill], axis=0
    )
    for start in range(0, SENT, groups):
        turned = rows[start * block : (start + groups) * block].T
        parts = [turned[group * devices : (group + 1) * devices] for group in range(groups)]
        parts = exchange(parts, block)
        for field in range(start, min(start + groups, SENT)):
            out_ref[pl.ds(field, devices, stride=SENT), :] = parts[field - start]


def middle_kernel(x_devices, in_ref, before_ref, after_ref, y_ref, y_back_ref, out_ref, tail_ref):
    y_devices = in_ref.shape[0] // SENT // x_devices
    x_rows = y_devices
    x_length = x_devices * x_rows
    units = before_ref.shape[0] // 2
    y_rows = LANES // y_devices // x_rows
    row8 = lax.broadcasted_iota(jnp.int32, (8, LANES), 0)

    planes = []
    for x_device in range(x_devices):
        places = [(turn * x_devices + x_device) * SENT for turn in range(y_devices)]
        parts = [in_ref[place : place + 8, :] for place in places]
        planes.extend(exchange(parts, y_rows))
    tails = [
        in_ref[pl.ds(turn * x_devices * SENT + 8, x_devices, stride=SENT), :]
        for turn in range(y_devices)
    ]
    tails = exchange(tails, y_rows)

    smoothed = smooth_rows(planes)
    along_y = on_rows(smoothed, y_ref[...])
    upper_rows = []
    lower_rows = []
    for x in range(x_length):
        features = jnp.where(row8 < 3, along_y[x], smoothed[x])
        features = jnp.where(row8 < 6, features, jnp.where(row8 == 6, 1.0, 0.0))
        last = tails[x % x_rows][x // x_rows : x // x_rows + 1]
        upper_rows.append(features)
        lower_rows.append(jnp.where(row8 == 5, last, planes[x]))

    before = before_ref[...]
    after = after_ref[...]
    at_once = 2 * x_rows
    sums = jnp.zeros((32, 4 * units), jnp.float32)
    results = []

    def first_layer(chunk):
        planes_in = slice(chunk * at_once, (chunk + 1) * at_once)
        upper = jnp.concatenate(upper_rows[planes_in], axis=1)
        lower = jnp.concatenate(lower_rows[planes_in], axis=1)
        pieces = split(jnp.concatenate([upper, lower], axis=0), 3)
        wide = jnp.concatenate([pieces[turn] for turn in LEFT_PIECES + (2, 1)], axis=0)
        return jnp.concatenate(pieces[:2], axis=0), times(before, wide)

    def activation(both):
        hidden = jnp.tanh(both[:units])
        grad_pre = both[units:] * (1.0 - hidden * hidden)
        return jnp.concatenate(split(jnp.concatenate([hidden, grad_pre], axis=0), 2), axis=0)

    chunks = x_length // at_once
    staged = {}
    for step in range(chunks + 2):
        if step < chunks:
            staged[step] = first_layer(step)
        if 0 <= step - 1 < chunks:
            cells, both = staged[step - 1]
            staged[step - 1] = (cells, activation(both))
        if 0 <= step - 2:
            cells, both = staged.pop(step - 2)
            result = times(after, both)
            result = result[:16] + result[16:32] + result[32:]
            sums = sums + times(cells, both, (1, 1))
            for turn in range(at_once):
                part = result[:, turn * LANES : (turn + 1) * LANES]
                results.append(part[:8])
                x = (step - 2) * at_once + turn
                place = (x % x_rows) * x_devices + x // x_rows
                tail_ref[place : place + 1, :] = part[8:9]

    back_y = on_rows(results, y_back_ref[...])
    back = [jnp.where(row8 < 3, back_y[x], results[x]) for x in range(x_length)]
    back = smooth_rows(back)
    back = [jnp.where(row8 < 6, value, result) for value, result in zip(back, results)]
    for x_device in range(x_devices):
        first = x_device * x_rows
        parts = exchange(back[first : first + x_rows], y_rows)
        for turn in range(y_devices):
            place = (turn * x_devices + x_device) * RETURNED
            out_ref[place : place + 8, :] = parts[turn]
    tails = [tail_ref[x * x_devices : (x + 1) * x_devices, :] for x in range(x_rows)]
    tails = exchange(tails, y_rows)
    for turn in range(y_devices):
        place = turn * x_devices * RETURNED + 8
        out_ref[pl.ds(place, x_devices, stride=RETURNED), :] = tails[turn]

    sums = sums[:, : 2 * units] + sums[:, 2 * units :]
    sums = sums[:16] + sums[16:]
    moved = jnp.concatenate([sums[5:7, units:], STEP_SIZE * sums[13:16, :units]], axis=0)
    packed = jnp.concatenate([sums[:5, units:], moved], axis=1)
    for device in range(x_devices * y_devices):
        place = device * RETURNED + SENT
        out_ref[place : place + 5, :] = packed


def unpack_kernel(
    cells,
    in_ref,
    velocity_ref,
    cotangent_ref,
    z_ref,
    new_ref,
    grad_ref,
    in_grad_ref,
    bias_grad_ref,
    out_grad_ref,
):
    _, x_rows, y_rows, z_length = velocity_ref.shape
    block = x_rows * y_rows
    groups = LANES // block
    devices = z_length // groups
    units = in_grad_ref.shape[1]
    fields = []
    for start in range(0, SENT, groups):
        parts = [
            in_ref[pl.ds(min(field, SENT - 1), devices, stride=RETURNED), :]
            for field in range(start, start + groups)
        ]
        turned = jnp.concatenate(exchange(parts, block), axis=0).T
        fields.extend(turned[turn * block : (turn + 1) * block] for turn in range(groups))
    shape = (3, x_rows, y_rows, z_length)
    forcing = jnp.concatenate(fields[6:9], axis=0).reshape(shape)
    new_ref[...] = velocity_ref[...] + STEP_SIZE * forcing
    back_z = times_table(jnp.concatenate(fields[3:6], axis=0), z_ref[...])
    back = jnp.concatenate(fields[:3], axis=0) + back_z
    grad_ref[...] = cotangent_ref[...] + back.reshape(shape)

    sums = in_ref[SENT : SENT + 5, :]
    for device in range(1, devices):
        place = device * RETURNED + SENT
        sums = sums + in_ref[place : place + 5, :]
    sums = sums * (1.0 / cells)
    in_grad_ref[:5, :] = sums[:, :units]
    in_grad_ref[5:, :] = sums[:1, units:]
    bias_grad_ref[...] = sums[1:2, units:]
    out_grad_ref[...] = sums[2:, units:]


def on_device(kernel, shapes, scratch=(), **more):
    return pl.pallas_call(
        kernel,
        out_shape=[jax.ShapeDtypeStruct(shape, kind) for shape, kind in shapes],
        scratch_shapes=[*scratch],
        compiler_params=pltpu.CompilerParams(vmem_limit_bytes=32 * 1024 * 1024),
        **more,
    )


def fits(velocity, units):
    x_devices, y_devices = lax.axis_size("gx"), lax.axis_size("gy")
    _, x_rows, y_rows, z_length = velocity.shape
    return (
        z_length == LANES
        and x_rows * y_rows * LANES == LANES * LANES // 4
        and x_devices * y_devices * 4 == LANES
        and x_devices == 8
        and y_devices == x_rows
        and y_rows % 8 == 0
        and 2 * units == LANES
    )


def local_kernels(velocity, cotangent, weight_in, bias_in, weight_out):
    axes = ("gy", "gx")
    x_devices, y_devices = lax.axis_size("gx"), lax.axis_size("gy")
    devices = x_devices * y_devices
    _, x_rows, y_rows, z_length = velocity.shape
    units = weight_in.shape[1]
    cells = x_rows * x_devices * y_rows * y_devices * z_length
    z_table = derivative_table(z_length)
    y_table = np.kron(np.eye(z_length // devices), derivative_table(y_rows * y_devices))
    single, half = jnp.float32, jnp.bfloat16

    in_place = pl.BlockSpec(memory_space=pltpu.HBM)

    arguments = [
        velocity,
        cotangent,
        table(z_table.T),
        weight_in,
        bias_in[None],
        weight_out.T,
    ]
    arguments = [pltpu.with_memory_space_constraint(each, pltpu.HBM) for each in arguments]
    sent, *prepared = on_device(
        pack_kernel,
        [
            ((devices * SENT, LANES), single),
            ((2 * units, LANES), half),
            ((48, 4 * units), half),
        ],
        [pltpu.VMEM(values.shape, values.dtype) for values in arguments]
        + [pltpu.SemaphoreType.DMA((11,))],
        in_specs=[in_place] * len(arguments),
    )(*arguments)
    sent = sent.reshape(devices, 1, SENT * LANES)
    sent = lax.all_to_all(sent, axes, 0, 0, tiled=True).reshape(devices * SENT, LANES)
    (back,) = on_device(
        functools.partial(middle_kernel, x_devices),
        [((devices * RETURNED, LANES), single)],
        [pltpu.VMEM((x_devices * x_rows, LANES), single)],
    )(sent, *prepared, split_table(y_table.T), split_table(y_table))
    back = back.reshape(devices, 1, RETURNED * LANES)
    back = lax.all_to_all(back, axes, 0, 0, tiled=True).reshape(devices * RETURNED, LANES)
    shapes = [velocity.shape, velocity.shape, (6, units), (1, units), (3, units)]
    new, grad, grad_in, grad_bias, grad_out = on_device(
        functools.partial(unpack_kernel, float(cells)), [(shape, single) for shape in shapes]
    )(back, velocity, cotangent, split_table(z_table))
    return (new, grad, grad_in, grad_bias[0], grad_out.T)


def local(velocity, cotangent, weight_in, bias_in, weight_out):
    chosen = local_kernels if fits(velocity, weight_in.shape[1]) else local_plain
    return chosen(velocity, cotangent, weight_in, bias_in, weight_out)


def solution(mesh):
    in_specs = (P(None, "gx", "gy", None), P(None, "gx", "gy", None), P(), P(), P())
    out_specs = (P(None, "gx", "gy", None), P(None, "gx", "gy", None), P(), P(), P())
    return jax.shard_map(local, mesh=mesh, in_specs=in_specs, out_specs=out_specs, check_vma=False)
```

```python
import functools

import jax
import jax.numpy as jnp
import ml_dtypes
import numpy as np
from jax import lax
from jax.experimental import pallas as pl
from jax.experimental.pallas import tpu as pltpu
from jax.sharding import PartitionSpec as P

FILTER_ALPHA = 0.499
FILTER_GAIN = 0.5 + FILTER_ALPHA
COMPACT_ALPHA = 1.0 / 3.0
STEP_SIZE = 0.5
PRECISE = lax.Precision.HIGHEST
LANES = 128
SENT = 9
RETURNED = 14
LEFT_PIECES = (0, 1, 0, 2, 1, 0)
RIGHT_PIECES = (0, 0, 1, 0, 1, 2)


def beside(length, offset):
    return np.eye(length, k=offset) + np.eye(length, k=-offset)


def smooth_table(length):
    left = np.eye(length) + FILTER_ALPHA * beside(length, 1)
    right = FILTER_GAIN * np.eye(length) + 0.5 * FILTER_GAIN * beside(length, 1)
    return np.linalg.solve(left, right)


def derivative_table(length):
    left = np.eye(length) + COMPACT_ALPHA * beside(length, 1)
    right = 7.0 / 9.0 * (np.eye(length, k=1) - np.eye(length, k=-1)) + 1.0 / 36.0 * (
        np.eye(length, k=2) - np.eye(length, k=-2)
    )
    return np.linalg.solve(left, right)


def table(values):
    return jnp.asarray(values.astype(np.float32))


def split_table(values):
    pieces = []
    rest = values.astype(np.float32)
    for _ in range(3):
        pieces.append(rest.astype(ml_dtypes.bfloat16))
        rest = rest - pieces[-1].astype(np.float32)
    return jnp.asarray(np.concatenate([pieces[turn] for turn in RIGHT_PIECES], axis=0))


def local_plain(velocity, cotangent, weight_in, bias_in, weight_out):
    axes = ("gx", "gy")
    x_devices, y_devices = lax.axis_size("gx"), lax.axis_size("gy")
    devices = x_devices * y_devices
    _, x_rows, y_rows, z_length = velocity.shape
    x_length, y_length = x_rows * x_devices, y_rows * y_devices
    units = weight_in.shape[1]
    z_rows = -(-z_length // devices)
    padding = z_rows * devices - z_length

    z_table = table(derivative_table(z_length))
    y_table = table(derivative_table(y_length))
    x_table = table(smooth_table(x_length))

    along_z = jnp.einsum("ab,kxyb->kxya", z_table, velocity, precision=PRECISE)
    fields = jnp.concatenate([velocity, along_z, cotangent], axis=0)
    fields = jnp.pad(fields, ((0, 0), (0, 0), (0, 0), (0, padding)))
    fields = fields.reshape(9, x_rows, y_rows, z_rows, devices)
    fields = fields.transpose(4, 0, 3, 1, 2).reshape(devices, 9, z_rows * x_rows * y_rows)
    fields = lax.all_to_all(fields, axes, 0, 0, tiled=True)
    fields = fields.reshape(x_devices, y_devices, 9, z_rows, x_rows, y_rows)
    fields = fields.transpose(2, 0, 4, 3, 1, 5).reshape(9, x_length, z_rows, y_length)

    smoothed = jnp.einsum("ab,kbzy->kazy", x_table, fields[:6], precision=PRECISE)
    along_y = jnp.einsum("ab,kxzb->kxza", y_table, smoothed[:3], precision=PRECISE)
    features = jnp.concatenate([along_y, smoothed[3:]], axis=0).reshape(6, -1)
    grad_out = STEP_SIZE * fields[6:].reshape(3, -1)

    hidden = jnp.tanh(jnp.dot(weight_in.T, features, precision=PRECISE) + bias_in[:, None])
    forcing = jnp.dot(weight_out.T, hidden, precision=PRECISE)
    grad_pre = jnp.dot(weight_out, grad_out, precision=PRECISE) * (1.0 - hidden * hidden)
    grad_features = jnp.dot(weight_in, grad_pre, precision=PRECISE)
    sum_in = jnp.dot(features, grad_pre.T, precision=PRECISE)
    sum_bias = jnp.sum(grad_pre, axis=1)
    sum_out = jnp.dot(grad_out, hidden.T, precision=PRECISE)

    grad_features = grad_features.reshape(6, x_length, z_rows, y_length)
    back_y = jnp.einsum("ba,kxzb->kxza", y_table, grad_features[:3], precision=PRECISE)
    back = jnp.concatenate([back_y, grad_features[3:]], axis=0)
    back = jnp.einsum("ab,kbzy->kazy", x_table, back, precision=PRECISE)
    back = jnp.concatenate([forcing.reshape(3, x_length, z_rows, y_length), back], axis=0)
    back = back.reshape(9, x_devices, x_rows, z_rows, y_devices, y_rows)
    back = back.transpose(1, 4, 0, 3, 2, 5).reshape(devices, -1)
    sums = jnp.concatenate([sum_in, sum_bias[None], sum_out], axis=0).reshape(1, -1)
    cells = back.shape[1]
    back = jnp.concatenate([back, jnp.broadcast_to(sums, (devices, 10 * units))], axis=1)
    back = lax.all_to_all(back, axes, 0, 0, tiled=True)

    sums = jnp.sum(back[:, cells:], axis=0).reshape(10, units)
    sums = sums / float(x_length * y_length * z_length)
    back = back[:, :cells].reshape(devices, 9, z_rows, x_rows, y_rows)
    back = back.transpose(1, 3, 4, 2, 0).reshape(9, x_rows, y_rows, -1)[..., :z_length]
    new_velocity = velocity + STEP_SIZE * back[:3]
    back_z = jnp.einsum("ba,kxyb->kxya", z_table, back[6:], precision=PRECISE)
    grad_velocity = cotangent + back[3:6] + back_z
    return (new_velocity, grad_velocity, sums[:6], sums[6], sums[7:].T)


def exchange(parts, width):
    parts = list(parts)
    lane = lax.broadcasted_iota(jnp.int32, parts[0].shape, 1)
    step = len(parts) // 2
    while step:
        shift = step * width
        upper = (lane & shift) != 0
        for low in range(len(parts)):
            if low & step == 0:
                first, second = parts[low], parts[low + step]
                parts[low] = jnp.where(upper, pltpu.roll(second, shift, 1), first)
                parts[low + step] = jnp.where(upper, second, pltpu.roll(first, LANES - shift, 1))
        step //= 2
    return parts


def smooth_rows(rows):
    length = len(rows)
    half = length // 2
    scales = []
    before = 0.0
    for _ in range(half):
        scales.append(1.0 / (1.0 - FILTER_ALPHA * FILTER_ALPHA * before))
        before = scales[-1]
    factors = [-FILTER_ALPHA * scale for scale in scales]
    forward = np.cumprod([1.0] + factors[1:])
    backward = np.cumprod([1.0] + factors[-2::-1])[::-1]
    own = 0.5 * FILTER_GAIN / FILTER_ALPHA

    sides = [list(range(half)), list(range(length - 1, half - 1, -1))]
    running = []
    for side in sides:
        sums = []
        for turn, row in enumerate(side):
            value = rows[row] * float(scales[turn] / forward[turn])
            sums.append(value if turn == 0 else sums[-1] + value)
        running.append(sums)
    middle = forward[-1] / (1.0 - factors[-1] * factors[-1])
    cross = middle * factors[-1]
    smoothed = [None] * length
    for side, sums, others in zip(sides, running, running[::-1]):
        value = float(middle) * sums[-1] + float(cross) * others[-1]
        for turn in reversed(range(half)):
            if turn < half - 1:
                value = value + float(forward[turn] / backward[turn]) * sums[turn]
            row = side[turn]
            smoothed[row] = own * rows[row] + float((FILTER_GAIN - own) * backward[turn]) * value
    return smoothed


def times(left, right, contract=(1, 0)):
    dims = (((contract[0],), (contract[1],)), ((), ()))
    return lax.dot_general(left, right, dims, preferred_element_type=jnp.float32)


def split(values, count):
    pieces = []
    for turn in range(count):
        pieces.append(values.astype(jnp.bfloat16))
        if turn + 1 < count:
            values = values - pieces[-1].astype(jnp.float32)
    return pieces


def times_table(values, wide_table):
    pieces = split(values, 3)
    return times(jnp.concatenate([pieces[turn] for turn in LEFT_PIECES], axis=1), wide_table)


def widened(square_table):
    pieces = split(square_table, 3)
    return jnp.concatenate([pieces[turn] for turn in RIGHT_PIECES], axis=0)


def on_rows(rows, wide_table):
    out = times_table(jnp.concatenate(rows, axis=0), wide_table)
    return [out[8 * turn : 8 * turn + 8] for turn in range(len(rows))]


def pack_kernel(
    velocity_hbm,
    cotangent_hbm,
    z_hbm,
    weight_in_hbm,
    bias_hbm,
    weight_out_hbm,
    out_ref,
    before_ref,
    after_ref,
    velocity_ref,
    cotangent_ref,
    z_ref,
    weight_in_ref,
    bias_ref,
    weight_out_ref,
    arrived,
):
    pairs = [
        (weight_in_hbm, weight_in_ref),
        (bias_hbm, bias_ref),
        (weight_out_hbm, weight_out_ref),
        (velocity_hbm, velocity_ref),
        (cotangent_hbm, cotangent_ref),
        (z_hbm, z_ref),
    ]
    copies = [
        pltpu.make_async_copy(source, target, arrived.at[turn])
        for turn, (source, target) in enumerate(pairs)
    ]
    for copy in copies:
        copy.start()

    for copy in copies[:3]:
        copy.wait()
    weight_in = weight_in_ref[...]
    weight_out = weight_out_ref[...]
    units = weight_in.shape[1]
    zeros = functools.partial(jnp.zeros, dtype=jnp.float32)
    before = jnp.concatenate(
        [
            jnp.concatenate([weight_in, bias_ref[...], zeros((9, units))], axis=0),
            jnp.concatenate([zeros((13, units)), STEP_SIZE * weight_out], axis=0),
        ],
        axis=1,
    )
    after = jnp.concatenate(
        [
            jnp.concatenate([zeros((6, units)), weight_out, zeros((7, units))], axis=0),
            jnp.concatenate([weight_in, zeros((10, units))], axis=0),
        ],
        axis=1,
    )
    pieces = [piece.astype(jnp.float32) for piece in split(before, 2)]
    before = jnp.concatenate([pieces[turn] for turn in (0, 0, 1, 1)] + [zeros((64, LANES))], axis=0)
    before_ref[...] = before.T.astype(jnp.bfloat16)
    pieces = split(after, 2)
    pieces = [jnp.concatenate([piece, piece], axis=1) for piece in pieces]
    after_ref[...] = jnp.concatenate(pieces, axis=0)

    for copy in copies[3:]:
        copy.wait()
    _, x_rows, y_rows, z_length = velocity_ref.shape
    block = x_rows * y_rows
    groups = LANES // block
    devices = z_length // groups
    velocity = velocity_ref[...].reshape(3 * block, z_length)
    cotangent = cotangent_ref[...].reshape(3 * block, z_length)
    along_z = times_table(velocity, widened(z_ref[...]))
    fill = jnp.zeros(((-SENT % groups) * block, z_length), jnp.float32)
    rows = jnp.concatenate(
        [velocity, along_z, cotangent[block:], cotangent[:block], fill], axis=0
    )
    for start in range(0, SENT, groups):
        turned = rows[start * block : (start + groups) * block].T
        parts = [turned[group * devices : (group + 1) * devices] for group in range(groups)]
        parts = exchange(parts, block)
        for field in range(start, min(start + groups, SENT)):
            out_ref[pl.ds(field, devices, stride=SENT), :] = parts[field - start]


def middle_kernel(x_devices, in_ref, before_ref, after_ref, y_ref, y_back_ref, out_ref, tail_ref):
    y_devices = in_ref.shape[0] // SENT // x_devices
    x_rows = y_devices
    x_length = x_devices * x_rows
    units = before_ref.shape[0] // 2
    y_rows = LANES // y_devices // x_rows
    row8 = lax.broadcasted_iota(jnp.int32, (8, LANES), 0)

    planes = []
    for x_device in range(x_devices):
        places = [(turn * x_devices + x_device) * SENT for turn in range(y_devices)]
        parts = [in_ref[place : place + 8, :] for place in places]
        planes.extend(exchange(parts, y_rows))
    tails = [
        in_ref[pl.ds(turn * x_devices * SENT + 8, x_devices, stride=SENT), :]
        for turn in range(y_devices)
    ]
    tails = exchange(tails, y_rows)

    smoothed = smooth_rows(planes)
    along_y = on_rows(smoothed, y_ref[...])
    upper_rows = []
    lower_rows = []
    for x in range(x_length):
        features = jnp.where(row8 < 3, along_y[x], smoothed[x])
        features = jnp.where(row8 < 6, features, jnp.where(row8 == 6, 1.0, 0.0))
        last = tails[x % x_rows][x // x_rows : x // x_rows + 1]
        upper_rows.append(features)
        lower_rows.append(jnp.where(row8 == 5, last, planes[x]))

    before = before_ref[:, :64]
    after = after_ref[...]
    at_once = x_length
    sums = jnp.zeros((32, 4 * units), jnp.float32)
    results = []
    for start in range(0, x_length, at_once):
        stop = start + at_once
        cells = jnp.concatenate(
            [
                jnp.concatenate(upper_rows[start:stop], axis=1),
                jnp.concatenate(lower_rows[start:stop], axis=1),
            ],
            axis=0,
        )
        pieces = split(cells, 2)
        both = times(before, jnp.concatenate(pieces + pieces, axis=0))
        hidden = jnp.tanh(both[:units])
        grad_pre = both[units:] * (1.0 - hidden * hidden)
        both = jnp.concatenate([hidden, grad_pre], axis=0)
        both = jnp.concatenate(split(both, 2), axis=0)
        sums = sums + times(jnp.concatenate(pieces, axis=0), both, (1, 1))
        result = times(after, both)
        result = result[:16] + result[16:]
        for turn in range(at_once):
            results.append(result[:8, turn * LANES : (turn + 1) * LANES])
            x = start + turn
            place = (x % x_rows) * x_devices + x // x_rows
            tail_ref[place : place + 1, :] = result[8:9, turn * LANES : (turn + 1) * LANES]

    back_y = on_rows(results, y_back_ref[...])
    back = [jnp.where(row8 < 3, back_y[x], results[x]) for x in range(x_length)]
    back = smooth_rows(back)
    back = [jnp.where(row8 < 6, value, result) for value, result in zip(back, results)]
    for x_device in range(x_devices):
        first = x_device * x_rows
        parts = exchange(back[first : first + x_rows], y_rows)
        for turn in range(y_devices):
            place = (turn * x_devices + x_device) * RETURNED
            out_ref[place : place + 8, :] = parts[turn]
    tails = [tail_ref[x * x_devices : (x + 1) * x_devices, :] for x in range(x_rows)]
    tails = exchange(tails, y_rows)
    for turn in range(y_devices):
        place = turn * x_devices * RETURNED + 8
        out_ref[pl.ds(place, x_devices, stride=RETURNED), :] = tails[turn]

    sums = sums[:, : 2 * units] + sums[:, 2 * units :]
    sums = sums[:16] + sums[16:]
    moved = jnp.concatenate([sums[5:7, units:], STEP_SIZE * sums[13:16, :units]], axis=0)
    packed = jnp.concatenate([sums[:5, units:], moved], axis=1)
    for device in range(x_devices * y_devices):
        place = device * RETURNED + SENT
        out_ref[place : place + 5, :] = packed


def unpack_kernel(
    cells,
    in_ref,
    velocity_ref,
    cotangent_ref,
    z_ref,
    new_ref,
    grad_ref,
    in_grad_ref,
    bias_grad_ref,
    out_grad_ref,
):
    _, x_rows, y_rows, z_length = velocity_ref.shape
    block = x_rows * y_rows
    groups = LANES // block
    devices = z_length // groups
    units = in_grad_ref.shape[1]
    fields = []
    for start in range(0, SENT, groups):
        parts = [
            in_ref[pl.ds(min(field, SENT - 1), devices, stride=RETURNED), :]
            for field in range(start, start + groups)
        ]
        turned = jnp.concatenate(exchange(parts, block), axis=0).T
        fields.extend(turned[turn * block : (turn + 1) * block] for turn in range(groups))
    shape = (3, x_rows, y_rows, z_length)
    forcing = jnp.concatenate(fields[6:9], axis=0).reshape(shape)
    new_ref[...] = velocity_ref[...] + STEP_SIZE * forcing
    back_z = times_table(jnp.concatenate(fields[3:6], axis=0), z_ref[...])
    back = jnp.concatenate(fields[:3], axis=0) + back_z
    grad_ref[...] = cotangent_ref[...] + back.reshape(shape)

    sums = in_ref[SENT : SENT + 5, :]
    for device in range(1, devices):
        place = device * RETURNED + SENT
        sums = sums + in_ref[place : place + 5, :]
    sums = sums * (1.0 / cells)
    in_grad_ref[:5, :] = sums[:, :units]
    in_grad_ref[5:, :] = sums[:1, units:]
    bias_grad_ref[...] = sums[1:2, units:]
    out_grad_ref[...] = sums[2:, units:]


def on_device(kernel, shapes, scratch=(), **more):
    return pl.pallas_call(
        kernel,
        out_shape=[jax.ShapeDtypeStruct(shape, kind) for shape, kind in shapes],
        scratch_shapes=[*scratch],
        compiler_params=pltpu.CompilerParams(vmem_limit_bytes=32 * 1024 * 1024),
        **more,
    )


def fits(velocity, units):
    x_devices, y_devices = lax.axis_size("gx"), lax.axis_size("gy")
    _, x_rows, y_rows, z_length = velocity.shape
    return (
        z_length == LANES
        and x_rows * y_rows * LANES == LANES * LANES // 4
        and x_devices * y_devices * 4 == LANES
        and x_devices == 8
        and y_devices == x_rows
        and y_rows % 8 == 0
        and 2 * units == LANES
    )


def local_kernels(velocity, cotangent, weight_in, bias_in, weight_out):
    axes = ("gy", "gx")
    x_devices, y_devices = lax.axis_size("gx"), lax.axis_size("gy")
    devices = x_devices * y_devices
    _, x_rows, y_rows, z_length = velocity.shape
    units = weight_in.shape[1]
    cells = x_rows * x_devices * y_rows * y_devices * z_length
    z_table = derivative_table(z_length)
    y_table = np.kron(np.eye(z_length // devices), derivative_table(y_rows * y_devices))
    single, half = jnp.float32, jnp.bfloat16

    in_place = pl.BlockSpec(memory_space=pltpu.HBM)

    arguments = [
        velocity,
        cotangent,
        table(z_table.T),
        weight_in,
        bias_in[None],
        weight_out.T,
    ]
    arguments = [pltpu.with_memory_space_constraint(each, pltpu.HBM) for each in arguments]
    sent, *prepared = on_device(
        pack_kernel,
        [
            ((devices * SENT, LANES), single),
            ((2 * units, LANES), half),
            ((32, 4 * units), half),
        ],
        [pltpu.VMEM(values.shape, values.dtype) for values in arguments]
        + [pltpu.SemaphoreType.DMA((len(arguments),))],
        in_specs=[in_place] * len(arguments),
    )(*arguments)
    sent = sent.reshape(devices, 1, SENT * LANES)
    sent = lax.all_to_all(sent, axes, 0, 0, tiled=True).reshape(devices * SENT, LANES)
    (back,) = on_device(
        functools.partial(middle_kernel, x_devices),
        [((devices * RETURNED, LANES), single)],
        [pltpu.VMEM((x_devices * x_rows, LANES), single)],
    )(sent, *prepared, split_table(y_table.T), split_table(y_table))
    back = back.reshape(devices, 1, RETURNED * LANES)
    back = lax.all_to_all(back, axes, 0, 0, tiled=True).reshape(devices * RETURNED, LANES)
    shapes = [velocity.shape, velocity.shape, (6, units), (1, units), (3, units)]
    new, grad, grad_in, grad_bias, grad_out = on_device(
        functools.partial(unpack_kernel, float(cells)), [(shape, single) for shape in shapes]
    )(back, velocity, cotangent, split_table(z_table))
    return (new, grad, grad_in, grad_bias[0], grad_out.T)


def local(velocity, cotangent, weight_in, bias_in, weight_out):
    chosen = local_kernels if fits(velocity, weight_in.shape[1]) else local_plain
    return chosen(velocity, cotangent, weight_in, bias_in, weight_out)


def solution(mesh):
    in_specs = (P(None, "gx", "gy", None), P(None, "gx", "gy", None), P(), P(), P())
    out_specs = (P(None, "gx", "gy", None), P(None, "gx", "gy", None), P(), P(), P())
    return jax.shard_map(local, mesh=mesh, in_specs=in_specs, out_specs=out_specs, check_vma=False)
```

```python
import functools

import jax
import jax.numpy as jnp
import ml_dtypes
import numpy as np
from jax import lax
from jax.experimental import pallas as pl
from jax.experimental.pallas import tpu as pltpu
from jax.sharding import PartitionSpec as P

FILTER_ALPHA = 0.499
FILTER_GAIN = 0.5 + FILTER_ALPHA
COMPACT_ALPHA = 1.0 / 3.0
STEP_SIZE = 0.5
PRECISE = lax.Precision.HIGHEST
LANES = 128
SENT = 9
RETURNED = 14
LEFT_PIECES = (0, 1, 0, 2, 1, 0)
RIGHT_PIECES = (0, 0, 1, 0, 1, 2)


def beside(length, offset):
    return np.eye(length, k=offset) + np.eye(length, k=-offset)


def smooth_table(length):
    left = np.eye(length) + FILTER_ALPHA * beside(length, 1)
    right = FILTER_GAIN * np.eye(length) + 0.5 * FILTER_GAIN * beside(length, 1)
    return np.linalg.solve(left, right)


def derivative_table(length):
    left = np.eye(length) + COMPACT_ALPHA * beside(length, 1)
    right = 7.0 / 9.0 * (np.eye(length, k=1) - np.eye(length, k=-1)) + 1.0 / 36.0 * (
        np.eye(length, k=2) - np.eye(length, k=-2)
    )
    return np.linalg.solve(left, right)


def table(values):
    return jnp.asarray(values.astype(np.float32))


def split_table(values):
    pieces = []
    rest = values.astype(np.float32)
    for _ in range(3):
        pieces.append(rest.astype(ml_dtypes.bfloat16))
        rest = rest - pieces[-1].astype(np.float32)
    return jnp.asarray(np.concatenate([pieces[turn] for turn in RIGHT_PIECES], axis=0))


def local_plain(velocity, cotangent, weight_in, bias_in, weight_out):
    axes = ("gx", "gy")
    x_devices, y_devices = lax.axis_size("gx"), lax.axis_size("gy")
    devices = x_devices * y_devices
    _, x_rows, y_rows, z_length = velocity.shape
    x_length, y_length = x_rows * x_devices, y_rows * y_devices
    units = weight_in.shape[1]
    z_rows = -(-z_length // devices)
    padding = z_rows * devices - z_length

    z_table = table(derivative_table(z_length))
    y_table = table(derivative_table(y_length))
    x_table = table(smooth_table(x_length))

    along_z = jnp.einsum("ab,kxyb->kxya", z_table, velocity, precision=PRECISE)
    fields = jnp.concatenate([velocity, along_z, cotangent], axis=0)
    fields = jnp.pad(fields, ((0, 0), (0, 0), (0, 0), (0, padding)))
    fields = fields.reshape(9, x_rows, y_rows, z_rows, devices)
    fields = fields.transpose(4, 0, 3, 1, 2).reshape(devices, 9, z_rows * x_rows * y_rows)
    fields = lax.all_to_all(fields, axes, 0, 0, tiled=True)
    fields = fields.reshape(x_devices, y_devices, 9, z_rows, x_rows, y_rows)
    fields = fields.transpose(2, 0, 4, 3, 1, 5).reshape(9, x_length, z_rows, y_length)

    smoothed = jnp.einsum("ab,kbzy->kazy", x_table, fields[:6], precision=PRECISE)
    along_y = jnp.einsum("ab,kxzb->kxza", y_table, smoothed[:3], precision=PRECISE)
    features = jnp.concatenate([along_y, smoothed[3:]], axis=0).reshape(6, -1)
    grad_out = STEP_SIZE * fields[6:].reshape(3, -1)

    hidden = jnp.tanh(jnp.dot(weight_in.T, features, precision=PRECISE) + bias_in[:, None])
    forcing = jnp.dot(weight_out.T, hidden, precision=PRECISE)
    grad_pre = jnp.dot(weight_out, grad_out, precision=PRECISE) * (1.0 - hidden * hidden)
    grad_features = jnp.dot(weight_in, grad_pre, precision=PRECISE)
    sum_in = jnp.dot(features, grad_pre.T, precision=PRECISE)
    sum_bias = jnp.sum(grad_pre, axis=1)
    sum_out = jnp.dot(grad_out, hidden.T, precision=PRECISE)

    grad_features = grad_features.reshape(6, x_length, z_rows, y_length)
    back_y = jnp.einsum("ba,kxzb->kxza", y_table, grad_features[:3], precision=PRECISE)
    back = jnp.concatenate([back_y, grad_features[3:]], axis=0)
    back = jnp.einsum("ab,kbzy->kazy", x_table, back, precision=PRECISE)
    back = jnp.concatenate([forcing.reshape(3, x_length, z_rows, y_length), back], axis=0)
    back = back.reshape(9, x_devices, x_rows, z_rows, y_devices, y_rows)
    back = back.transpose(1, 4, 0, 3, 2, 5).reshape(devices, -1)
    sums = jnp.concatenate([sum_in, sum_bias[None], sum_out], axis=0).reshape(1, -1)
    cells = back.shape[1]
    back = jnp.concatenate([back, jnp.broadcast_to(sums, (devices, 10 * units))], axis=1)
    back = lax.all_to_all(back, axes, 0, 0, tiled=True)

    sums = jnp.sum(back[:, cells:], axis=0).reshape(10, units)
    sums = sums / float(x_length * y_length * z_length)
    back = back[:, :cells].reshape(devices, 9, z_rows, x_rows, y_rows)
    back = back.transpose(1, 3, 4, 2, 0).reshape(9, x_rows, y_rows, -1)[..., :z_length]
    new_velocity = velocity + STEP_SIZE * back[:3]
    back_z = jnp.einsum("ba,kxyb->kxya", z_table, back[6:], precision=PRECISE)
    grad_velocity = cotangent + back[3:6] + back_z
    return (new_velocity, grad_velocity, sums[:6], sums[6], sums[7:].T)


def exchange(parts, width):
    parts = list(parts)
    lane = lax.broadcasted_iota(jnp.int32, parts[0].shape, 1)
    step = len(parts) // 2
    while step:
        shift = step * width
        upper = (lane & shift) != 0
        for low in range(len(parts)):
            if low & step == 0:
                first, second = parts[low], parts[low + step]
                parts[low] = jnp.where(upper, pltpu.roll(second, shift, 1), first)
                parts[low + step] = jnp.where(upper, second, pltpu.roll(first, LANES - shift, 1))
        step //= 2
    return parts


def smooth_rows(rows):
    length = len(rows)
    half = length // 2
    scales = []
    before = 0.0
    for _ in range(half):
        scales.append(1.0 / (1.0 - FILTER_ALPHA * FILTER_ALPHA * before))
        before = scales[-1]
    factors = [-FILTER_ALPHA * scale for scale in scales]
    forward = np.cumprod([1.0] + factors[1:])
    backward = np.cumprod([1.0] + factors[-2::-1])[::-1]
    own = 0.5 * FILTER_GAIN / FILTER_ALPHA

    sides = [list(range(half)), list(range(length - 1, half - 1, -1))]
    running = []
    for side in sides:
        sums = []
        for turn, row in enumerate(side):
            value = rows[row] * float(scales[turn] / forward[turn])
            sums.append(value if turn == 0 else sums[-1] + value)
        running.append(sums)
    middle = forward[-1] / (1.0 - factors[-1] * factors[-1])
    cross = middle * factors[-1]
    smoothed = [None] * length
    for side, sums, others in zip(sides, running, running[::-1]):
        value = float(middle) * sums[-1] + float(cross) * others[-1]
        for turn in reversed(range(half)):
            if turn < half - 1:
                value = value + float(forward[turn] / backward[turn]) * sums[turn]
            row = side[turn]
            smoothed[row] = own * rows[row] + float((FILTER_GAIN - own) * backward[turn]) * value
    return smoothed


def times(left, right, contract=(1, 0)):
    dims = (((contract[0],), (contract[1],)), ((), ()))
    return lax.dot_general(left, right, dims, preferred_element_type=jnp.float32)


def split(values, count):
    pieces = []
    for turn in range(count):
        pieces.append(values.astype(jnp.bfloat16))
        if turn + 1 < count:
            values = values - pieces[-1].astype(jnp.float32)
    return pieces


def times_table(values, wide_table):
    pieces = split(values, 3)
    return times(jnp.concatenate([pieces[turn] for turn in LEFT_PIECES], axis=1), wide_table)


def widened(square_table):
    pieces = split(square_table, 3)
    return jnp.concatenate([pieces[turn] for turn in RIGHT_PIECES], axis=0)


def on_rows(rows, wide_table):
    out = times_table(jnp.concatenate(rows, axis=0), wide_table)
    return [out[8 * turn : 8 * turn + 8] for turn in range(len(rows))]


def pack_kernel(
    velocity_hbm,
    cotangent_hbm,
    z_hbm,
    weight_in_hbm,
    bias_hbm,
    weight_out_hbm,
    out_ref,
    weight_in_ref,
    bias_ref,
    weight_out_ref,
    velocity_ref,
    cotangent_ref,
    z_ref,
    arrived,
):
    pairs = [
        (weight_in_hbm, weight_in_ref),
        (bias_hbm, bias_ref),
        (weight_out_hbm, weight_out_ref),
        (velocity_hbm, velocity_ref),
        (cotangent_hbm, cotangent_ref),
        (z_hbm, z_ref),
    ]
    copies = [
        pltpu.make_async_copy(source, target, arrived.at[turn])
        for turn, (source, target) in enumerate(pairs)
    ]
    for copy in copies:
        copy.start()

    for copy in copies[3:]:
        copy.wait()
    _, x_rows, y_rows, z_length = velocity_ref.shape
    block = x_rows * y_rows
    groups = LANES // block
    devices = z_length // groups
    velocity = velocity_ref[...].reshape(3 * block, z_length)
    cotangent = cotangent_ref[...].reshape(3 * block, z_length)
    along_z = times_table(velocity, widened(z_ref[...]))
    fill = jnp.zeros(((-SENT % groups) * block, z_length), jnp.float32)
    rows = jnp.concatenate(
        [velocity, along_z, cotangent[block:], cotangent[:block], fill], axis=0
    )
    for start in range(0, SENT, groups):
        turned = rows[start * block : (start + groups) * block].T
        parts = [turned[group * devices : (group + 1) * devices] for group in range(groups)]
        parts = exchange(parts, block)
        for field in range(start, min(start + groups, SENT)):
            out_ref[pl.ds(field, devices, stride=SENT), :] = parts[field - start]
    for copy in copies[:3]:
        copy.wait()


def network_matrices(weight_in_ref, bias_ref, weight_out_ref):
    weight_in = weight_in_ref[...]
    weight_out = weight_out_ref[...]
    units = weight_in.shape[1]
    zeros = functools.partial(jnp.zeros, dtype=jnp.float32)
    before = jnp.concatenate(
        [
            jnp.concatenate([weight_in, bias_ref[...], zeros((9, units))], axis=0),
            jnp.concatenate([zeros((13, units)), STEP_SIZE * weight_out], axis=0),
        ],
        axis=1,
    )
    after = jnp.concatenate(
        [
            jnp.concatenate([zeros((6, units)), weight_out, zeros((7, units))], axis=0),
            jnp.concatenate([weight_in, zeros((10, units))], axis=0),
        ],
        axis=1,
    )
    pieces = [piece.astype(jnp.float32) for piece in split(before, 3)]
    before = jnp.concatenate([pieces[turn] for turn in RIGHT_PIECES + (1, 2)], axis=0)
    before = before.T.astype(jnp.bfloat16)
    pieces = split(after, 3)
    after = jnp.concatenate(
        [
            jnp.concatenate([pieces[0], pieces[0]], axis=1),
            jnp.concatenate([pieces[1], pieces[1]], axis=1),
            jnp.concatenate([pieces[2], jnp.zeros_like(pieces[2])], axis=1),
        ],
        axis=0,
    )
    return before, after


def middle_kernel(
    x_devices,
    in_ref,
    weight_in_ref,
    bias_ref,
    weight_out_ref,
    y_ref,
    y_back_ref,
    out_ref,
    tail_ref,
):
    y_devices = in_ref.shape[0] // SENT // x_devices
    x_rows = y_devices
    x_length = x_devices * x_rows
    units = weight_in_ref.shape[1]
    y_rows = LANES // y_devices // x_rows
    row8 = lax.broadcasted_iota(jnp.int32, (8, LANES), 0)

    planes = []
    for x_device in range(x_devices):
        places = [(turn * x_devices + x_device) * SENT for turn in range(y_devices)]
        parts = [in_ref[place : place + 8, :] for place in places]
        planes.extend(exchange(parts, y_rows))
    tails = [
        in_ref[pl.ds(turn * x_devices * SENT + 8, x_devices, stride=SENT), :]
        for turn in range(y_devices)
    ]
    tails = exchange(tails, y_rows)

    smoothed = smooth_rows(planes)
    along_y = on_rows(smoothed, y_ref[...])
    upper_rows = []
    lower_rows = []
    for x in range(x_length):
        features = jnp.where(row8 < 3, along_y[x], smoothed[x])
        features = jnp.where(row8 < 6, features, jnp.where(row8 == 6, 1.0, 0.0))
        last = tails[x % x_rows][x // x_rows : x // x_rows + 1]
        upper_rows.append(features)
        lower_rows.append(jnp.where(row8 == 5, last, planes[x]))

    before, after = network_matrices(weight_in_ref, bias_ref, weight_out_ref)
    at_once = x_length
    sums = jnp.zeros((32, 4 * units), jnp.float32)
    results = []
    for start in range(0, x_length, at_once):
        stop = start + at_once
        cells = jnp.concatenate(
            [
                jnp.concatenate(upper_rows[start:stop], axis=1),
                jnp.concatenate(lower_rows[start:stop], axis=1),
            ],
            axis=0,
        )
        pieces = split(cells, 3)
        both = times(before, jnp.concatenate([pieces[turn] for turn in LEFT_PIECES + (2, 1)], axis=0))
        hidden = jnp.tanh(both[:units])
        grad_pre = both[units:] * (1.0 - hidden * hidden)
        both = jnp.concatenate([hidden, grad_pre], axis=0)
        both = jnp.concatenate(split(both, 2), axis=0)
        sums = sums + times(jnp.concatenate(pieces[:2], axis=0), both, (1, 1))
        result = times(after, both)
        result = result[:16] + result[16:32] + result[32:]
        for turn in range(at_once):
            results.append(result[:8, turn * LANES : (turn + 1) * LANES])
            x = start + turn
            place = (x % x_rows) * x_devices + x // x_rows
            tail_ref[place : place + 1, :] = result[8:9, turn * LANES : (turn + 1) * LANES]

    back_y = on_rows(results, y_back_ref[...])
    back = [jnp.where(row8 < 3, back_y[x], results[x]) for x in range(x_length)]
    back = smooth_rows(back)
    back = [jnp.where(row8 < 6, value, result) for value, result in zip(back, results)]
    for x_device in range(x_devices):
        first = x_device * x_rows
        parts = exchange(back[first : first + x_rows], y_rows)
        for turn in range(y_devices):
            place = (turn * x_devices + x_device) * RETURNED
            out_ref[place : place + 8, :] = parts[turn]
    tails = [tail_ref[x * x_devices : (x + 1) * x_devices, :] for x in range(x_rows)]
    tails = exchange(tails, y_rows)
    for turn in range(y_devices):
        place = turn * x_devices * RETURNED + 8
        out_ref[pl.ds(place, x_devices, stride=RETURNED), :] = tails[turn]

    sums = sums[:, : 2 * units] + sums[:, 2 * units :]
    sums = sums[:16] + sums[16:]
    moved = jnp.concatenate([sums[5:7, units:], STEP_SIZE * sums[13:16, :units]], axis=0)
    packed = jnp.concatenate([sums[:5, units:], moved], axis=1)
    for device in range(x_devices * y_devices):
        place = device * RETURNED + SENT
        out_ref[place : place + 5, :] = packed


def unpack_kernel(
    cells,
    in_ref,
    velocity_ref,
    cotangent_ref,
    z_ref,
    new_ref,
    grad_ref,
    in_grad_ref,
    bias_grad_ref,
    out_grad_ref,
):
    _, x_rows, y_rows, z_length = velocity_ref.shape
    block = x_rows * y_rows
    groups = LANES // block
    devices = z_length // groups
    units = in_grad_ref.shape[1]
    fields = []
    for start in range(0, SENT, groups):
        parts = [
            in_ref[pl.ds(min(field, SENT - 1), devices, stride=RETURNED), :]
            for field in range(start, start + groups)
        ]
        turned = jnp.concatenate(exchange(parts, block), axis=0).T
        fields.extend(turned[turn * block : (turn + 1) * block] for turn in range(groups))
    shape = (3, x_rows, y_rows, z_length)
    forcing = jnp.concatenate(fields[6:9], axis=0).reshape(shape)
    new_ref[...] = velocity_ref[...] + STEP_SIZE * forcing
    back_z = times_table(jnp.concatenate(fields[3:6], axis=0), z_ref[...])
    back = jnp.concatenate(fields[:3], axis=0) + back_z
    grad_ref[...] = cotangent_ref[...] + back.reshape(shape)

    sums = in_ref[SENT : SENT + 5, :]
    for device in range(1, devices):
        place = device * RETURNED + SENT
        sums = sums + in_ref[place : place + 5, :]
    sums = sums * (1.0 / cells)
    in_grad_ref[:5, :] = sums[:, :units]
    in_grad_ref[5:, :] = sums[:1, units:]
    bias_grad_ref[...] = sums[1:2, units:]
    out_grad_ref[...] = sums[2:, units:]


def on_device(kernel, shapes, scratch=(), **more):
    return pl.pallas_call(
        kernel,
        out_shape=[jax.ShapeDtypeStruct(shape, kind) for shape, kind in shapes],
        scratch_shapes=[*scratch],
        compiler_params=pltpu.CompilerParams(vmem_limit_bytes=32 * 1024 * 1024),
        **more,
    )


def fits(velocity, units):
    x_devices, y_devices = lax.axis_size("gx"), lax.axis_size("gy")
    _, x_rows, y_rows, z_length = velocity.shape
    return (
        z_length == LANES
        and x_rows * y_rows * LANES == LANES * LANES // 4
        and x_devices * y_devices * 4 == LANES
        and x_devices == 8
        and y_devices == x_rows
        and y_rows % 8 == 0
        and 2 * units == LANES
    )


def local_kernels(velocity, cotangent, weight_in, bias_in, weight_out):
    axes = ("gy", "gx")
    x_devices, y_devices = lax.axis_size("gx"), lax.axis_size("gy")
    devices = x_devices * y_devices
    _, x_rows, y_rows, z_length = velocity.shape
    units = weight_in.shape[1]
    cells = x_rows * x_devices * y_rows * y_devices * z_length
    z_table = derivative_table(z_length)
    y_table = np.kron(np.eye(z_length // devices), derivative_table(y_rows * y_devices))
    single = jnp.float32

    in_place = pl.BlockSpec(memory_space=pltpu.HBM)

    arguments = [
        velocity,
        cotangent,
        table(z_table.T),
        weight_in,
        bias_in[None],
        weight_out.T,
    ]
    arguments = [pltpu.with_memory_space_constraint(each, pltpu.HBM) for each in arguments]
    sent, *prepared = on_device(
        pack_kernel,
        [
            ((devices * SENT, LANES), single),
            *((values.shape, single) for values in arguments[3:]),
        ],
        [pltpu.VMEM(values.shape, values.dtype) for values in arguments[:3]]
        + [pltpu.SemaphoreType.DMA((len(arguments),))],
        in_specs=[in_place] * len(arguments),
    )(*arguments)
    sent = sent.reshape(devices, 1, SENT * LANES)
    sent = lax.all_to_all(sent, axes, 0, 0, tiled=True).reshape(devices * SENT, LANES)
    (back,) = on_device(
        functools.partial(middle_kernel, x_devices),
        [((devices * RETURNED, LANES), single)],
        [pltpu.VMEM((x_devices * x_rows, LANES), single)],
    )(sent, *prepared, split_table(y_table.T), split_table(y_table))
    back = back.reshape(devices, 1, RETURNED * LANES)
    back = lax.all_to_all(back, axes, 0, 0, tiled=True).reshape(devices * RETURNED, LANES)
    shapes = [velocity.shape, velocity.shape, (6, units), (1, units), (3, units)]
    new, grad, grad_in, grad_bias, grad_out = on_device(
        functools.partial(unpack_kernel, float(cells)), [(shape, single) for shape in shapes]
    )(back, velocity, cotangent, split_table(z_table))
    return (new, grad, grad_in, grad_bias[0], grad_out.T)


def local(velocity, cotangent, weight_in, bias_in, weight_out):
    chosen = local_kernels if fits(velocity, weight_in.shape[1]) else local_plain
    return chosen(velocity, cotangent, weight_in, bias_in, weight_out)


def solution(mesh):
    in_specs = (P(None, "gx", "gy", None), P(None, "gx", "gy", None), P(), P(), P())
    out_specs = (P(None, "gx", "gy", None), P(None, "gx", "gy", None), P(), P(), P())
    return jax.shard_map(local, mesh=mesh, in_specs=in_specs, out_specs=out_specs, check_vma=False)
```

```python
import functools

import jax
import jax.numpy as jnp
import ml_dtypes
import numpy as np
from jax import lax
from jax.experimental import pallas as pl
from jax.experimental.pallas import tpu as pltpu
from jax.sharding import PartitionSpec as P

FILTER_ALPHA = 0.499
FILTER_GAIN = 0.5 + FILTER_ALPHA
COMPACT_ALPHA = 1.0 / 3.0
STEP_SIZE = 0.5
PRECISE = lax.Precision.HIGHEST
LANES = 128
SENT = 9
RETURNED = 14
LEFT_PIECES = (0, 1, 0, 2, 1, 0)
RIGHT_PIECES = (0, 0, 1, 0, 1, 2)


def beside(length, offset):
    return np.eye(length, k=offset) + np.eye(length, k=-offset)


def smooth_table(length):
    left = np.eye(length) + FILTER_ALPHA * beside(length, 1)
    right = FILTER_GAIN * np.eye(length) + 0.5 * FILTER_GAIN * beside(length, 1)
    return np.linalg.solve(left, right)


def derivative_table(length):
    left = np.eye(length) + COMPACT_ALPHA * beside(length, 1)
    right = 7.0 / 9.0 * (np.eye(length, k=1) - np.eye(length, k=-1)) + 1.0 / 36.0 * (
        np.eye(length, k=2) - np.eye(length, k=-2)
    )
    return np.linalg.solve(left, right)


def table(values):
    return jnp.asarray(values.astype(np.float32))


def split_table(values):
    pieces = []
    rest = values.astype(np.float32)
    for _ in range(3):
        pieces.append(rest.astype(ml_dtypes.bfloat16))
        rest = rest - pieces[-1].astype(np.float32)
    return jnp.asarray(np.concatenate([pieces[turn] for turn in RIGHT_PIECES], axis=0))


def local_plain(velocity, cotangent, weight_in, bias_in, weight_out):
    axes = ("gx", "gy")
    x_devices, y_devices = lax.axis_size("gx"), lax.axis_size("gy")
    devices = x_devices * y_devices
    _, x_rows, y_rows, z_length = velocity.shape
    x_length, y_length = x_rows * x_devices, y_rows * y_devices
    units = weight_in.shape[1]
    z_rows = -(-z_length // devices)
    padding = z_rows * devices - z_length

    z_table = table(derivative_table(z_length))
    y_table = table(derivative_table(y_length))
    x_table = table(smooth_table(x_length))

    along_z = jnp.einsum("ab,kxyb->kxya", z_table, velocity, precision=PRECISE)
    fields = jnp.concatenate([velocity, along_z, cotangent], axis=0)
    fields = jnp.pad(fields, ((0, 0), (0, 0), (0, 0), (0, padding)))
    fields = fields.reshape(9, x_rows, y_rows, z_rows, devices)
    fields = fields.transpose(4, 0, 3, 1, 2).reshape(devices, 9, z_rows * x_rows * y_rows)
    fields = lax.all_to_all(fields, axes, 0, 0, tiled=True)
    fields = fields.reshape(x_devices, y_devices, 9, z_rows, x_rows, y_rows)
    fields = fields.transpose(2, 0, 4, 3, 1, 5).reshape(9, x_length, z_rows, y_length)

    smoothed = jnp.einsum("ab,kbzy->kazy", x_table, fields[:6], precision=PRECISE)
    along_y = jnp.einsum("ab,kxzb->kxza", y_table, smoothed[:3], precision=PRECISE)
    features = jnp.concatenate([along_y, smoothed[3:]], axis=0).reshape(6, -1)
    grad_out = STEP_SIZE * fields[6:].reshape(3, -1)

    hidden = jnp.tanh(jnp.dot(weight_in.T, features, precision=PRECISE) + bias_in[:, None])
    forcing = jnp.dot(weight_out.T, hidden, precision=PRECISE)
    grad_pre = jnp.dot(weight_out, grad_out, precision=PRECISE) * (1.0 - hidden * hidden)
    grad_features = jnp.dot(weight_in, grad_pre, precision=PRECISE)
    sum_in = jnp.dot(features, grad_pre.T, precision=PRECISE)
    sum_bias = jnp.sum(grad_pre, axis=1)
    sum_out = jnp.dot(grad_out, hidden.T, precision=PRECISE)

    grad_features = grad_features.reshape(6, x_length, z_rows, y_length)
    back_y = jnp.einsum("ba,kxzb->kxza", y_table, grad_features[:3], precision=PRECISE)
    back = jnp.concatenate([back_y, grad_features[3:]], axis=0)
    back = jnp.einsum("ab,kbzy->kazy", x_table, back, precision=PRECISE)
    back = jnp.concatenate([forcing.reshape(3, x_length, z_rows, y_length), back], axis=0)
    back = back.reshape(9, x_devices, x_rows, z_rows, y_devices, y_rows)
    back = back.transpose(1, 4, 0, 3, 2, 5).reshape(devices, -1)
    sums = jnp.concatenate([sum_in, sum_bias[None], sum_out], axis=0).reshape(1, -1)
    cells = back.shape[1]
    back = jnp.concatenate([back, jnp.broadcast_to(sums, (devices, 10 * units))], axis=1)
    back = lax.all_to_all(back, axes, 0, 0, tiled=True)

    sums = jnp.sum(back[:, cells:], axis=0).reshape(10, units)
    sums = sums / float(x_length * y_length * z_length)
    back = back[:, :cells].reshape(devices, 9, z_rows, x_rows, y_rows)
    back = back.transpose(1, 3, 4, 2, 0).reshape(9, x_rows, y_rows, -1)[..., :z_length]
    new_velocity = velocity + STEP_SIZE * back[:3]
    back_z = jnp.einsum("ba,kxyb->kxya", z_table, back[6:], precision=PRECISE)
    grad_velocity = cotangent + back[3:6] + back_z
    return (new_velocity, grad_velocity, sums[:6], sums[6], sums[7:].T)


def exchange(parts, width):
    parts = list(parts)
    lane = lax.broadcasted_iota(jnp.int32, parts[0].shape, 1)
    step = len(parts) // 2
    while step:
        shift = step * width
        upper = (lane & shift) != 0
        for low in range(len(parts)):
            if low & step == 0:
                first, second = parts[low], parts[low + step]
                parts[low] = jnp.where(upper, pltpu.roll(second, shift, 1), first)
                parts[low + step] = jnp.where(upper, second, pltpu.roll(first, LANES - shift, 1))
        step //= 2
    return parts


def smooth_rows(rows):
    length = len(rows)
    half = length // 2
    scales = []
    before = 0.0
    for _ in range(half):
        scales.append(1.0 / (1.0 - FILTER_ALPHA * FILTER_ALPHA * before))
        before = scales[-1]
    factors = [-FILTER_ALPHA * scale for scale in scales]
    forward = np.cumprod([1.0] + factors[1:])
    backward = np.cumprod([1.0] + factors[-2::-1])[::-1]
    own = 0.5 * FILTER_GAIN / FILTER_ALPHA

    sides = [list(range(half)), list(range(length - 1, half - 1, -1))]
    running = []
    for side in sides:
        sums = []
        for turn, row in enumerate(side):
            value = rows[row] * float(scales[turn] / forward[turn])
            sums.append(value if turn == 0 else sums[-1] + value)
        running.append(sums)
    middle = forward[-1] / (1.0 - factors[-1] * factors[-1])
    cross = middle * factors[-1]
    smoothed = [None] * length
    for side, sums, others in zip(sides, running, running[::-1]):
        value = float(middle) * sums[-1] + float(cross) * others[-1]
        for turn in reversed(range(half)):
            if turn < half - 1:
                value = value + float(forward[turn] / backward[turn]) * sums[turn]
            row = side[turn]
            smoothed[row] = own * rows[row] + float((FILTER_GAIN - own) * backward[turn]) * value
    return smoothed


def times(left, right, contract=(1, 0)):
    dims = (((contract[0],), (contract[1],)), ((), ()))
    return lax.dot_general(left, right, dims, preferred_element_type=jnp.float32)


def split(values, count):
    pieces = []
    for turn in range(count):
        pieces.append(values.astype(jnp.bfloat16))
        if turn + 1 < count:
            values = values - pieces[-1].astype(jnp.float32)
    return pieces


def times_table(values, wide_table):
    pieces = split(values, 3)
    return times(jnp.concatenate([pieces[turn] for turn in LEFT_PIECES], axis=1), wide_table)


def widened(square_table):
    pieces = split(square_table, 3)
    return jnp.concatenate([pieces[turn] for turn in RIGHT_PIECES], axis=0)


def on_rows(rows, wide_table):
    row8 = lax.broadcasted_iota(jnp.int32, rows[0].shape, 0)
    pairs = [
        jnp.where(row8 < 3, even, pltpu.roll(odd, 3, 0)) for even, odd in zip(rows[::2], rows[1::2])
    ]
    out = times_table(jnp.concatenate(pairs, axis=0), wide_table)
    outs = []
    for turn in range(len(pairs)):
        part = out[8 * turn : 8 * turn + 8]
        outs.extend([part, pltpu.roll(part, 5, 0)])
    return outs


def pack_kernel(
    velocity_hbm,
    cotangent_hbm,
    z_hbm,
    weight_in_hbm,
    bias_hbm,
    weight_out_hbm,
    out_ref,
    weight_in_ref,
    bias_ref,
    weight_out_ref,
    velocity_ref,
    cotangent_ref,
    z_ref,
    arrived,
):
    pairs = [
        (weight_in_hbm, weight_in_ref),
        (bias_hbm, bias_ref),
        (weight_out_hbm, weight_out_ref),
        (velocity_hbm, velocity_ref),
        (cotangent_hbm, cotangent_ref),
        (z_hbm, z_ref),
    ]
    copies = [
        pltpu.make_async_copy(source, target, arrived.at[turn])
        for turn, (source, target) in enumerate(pairs)
    ]
    for copy in copies:
        copy.start()

    _, x_rows, y_rows, z_length = velocity_ref.shape
    block = x_rows * y_rows
    groups = LANES // block
    devices = z_length // groups

    def store(fields, places):
        fill = [jnp.zeros_like(fields[0])] * (groups - len(fields))
        turned = jnp.concatenate([*fields, *fill], axis=0).T
        parts = [turned[group * devices : (group + 1) * devices] for group in range(groups)]
        for part, place in zip(exchange(parts, block), places):
            out_ref[pl.ds(place, devices, stride=SENT), :] = part

    for copy in copies[3:5]:
        copy.wait()
    velocity = [velocity_ref[part].reshape(block, z_length) for part in range(3)]
    cotangent = [cotangent_ref[part].reshape(block, z_length) for part in range(3)]
    store([*velocity, cotangent[1]], (0, 1, 2, 6))
    store([cotangent[2], cotangent[0]], (7, 8))
    copies[5].wait()
    along_z = times_table(jnp.concatenate(velocity, axis=0), widened(z_ref[...]))
    store([along_z[part * block : (part + 1) * block] for part in range(3)], (3, 4, 5))
    for copy in copies[:3]:
        copy.wait()


def network_matrices(weight_in_ref, bias_ref, weight_out_ref):
    weight_in = weight_in_ref[...]
    weight_out = weight_out_ref[...]
    units = weight_in.shape[1]
    zeros = functools.partial(jnp.zeros, dtype=jnp.float32)
    before = jnp.concatenate(
        [
            jnp.concatenate([weight_in, bias_ref[...], zeros((9, units))], axis=0),
            jnp.concatenate([zeros((13, units)), STEP_SIZE * weight_out], axis=0),
        ],
        axis=1,
    )
    after = jnp.concatenate(
        [
            jnp.concatenate([zeros((6, units)), weight_out, zeros((7, units))], axis=0),
            jnp.concatenate([weight_in, zeros((10, units))], axis=0),
        ],
        axis=1,
    )
    pieces = [piece.astype(jnp.float32) for piece in split(before, 3)]
    before = jnp.concatenate([pieces[turn] for turn in RIGHT_PIECES + (1, 2)], axis=0)
    before = before.T.astype(jnp.bfloat16)
    pieces = split(after, 3)
    after = jnp.concatenate(
        [
            jnp.concatenate([pieces[0], pieces[0]], axis=1),
            jnp.concatenate([pieces[1], pieces[1]], axis=1),
            jnp.concatenate([pieces[2], jnp.zeros_like(pieces[2])], axis=1),
        ],
        axis=0,
    )
    return before, after


def middle_kernel(
    x_devices,
    in_ref,
    weight_in_ref,
    bias_ref,
    weight_out_ref,
    y_ref,
    y_back_ref,
    out_ref,
    tail_ref,
):
    y_devices = in_ref.shape[0] // SENT // x_devices
    x_rows = y_devices
    x_length = x_devices * x_rows
    units = weight_in_ref.shape[1]
    y_rows = LANES // y_devices // x_rows
    row8 = lax.broadcasted_iota(jnp.int32, (8, LANES), 0)

    planes = []
    for x_device in range(x_devices):
        places = [(turn * x_devices + x_device) * SENT for turn in range(y_devices)]
        parts = [in_ref[place : place + 8, :] for place in places]
        planes.extend(exchange(parts, y_rows))
    tails = [
        in_ref[pl.ds(turn * x_devices * SENT + 8, x_devices, stride=SENT), :]
        for turn in range(y_devices)
    ]
    tails = exchange(tails, y_rows)

    smoothed = smooth_rows(planes)
    along_y = on_rows(smoothed, y_ref[...])
    upper_rows = []
    lower_rows = []
    for x in range(x_length):
        features = jnp.where(row8 < 3, along_y[x], smoothed[x])
        features = jnp.where(row8 < 6, features, jnp.where(row8 == 6, 1.0, 0.0))
        last = tails[x % x_rows][x // x_rows : x // x_rows + 1]
        upper_rows.append(features)
        lower_rows.append(jnp.where(row8 == 5, last, planes[x]))

    before, after = network_matrices(weight_in_ref, bias_ref, weight_out_ref)
    at_once = x_length
    sums = jnp.zeros((32, 4 * units), jnp.float32)
    results = []
    for start in range(0, x_length, at_once):
        stop = start + at_once
        cells = jnp.concatenate(
            [
                jnp.concatenate(upper_rows[start:stop], axis=1),
                jnp.concatenate(lower_rows[start:stop], axis=1),
            ],
            axis=0,
        )
        pieces = split(cells, 3)
        both = times(before, jnp.concatenate([pieces[turn] for turn in LEFT_PIECES + (2, 1)], axis=0))
        hidden = jnp.tanh(both[:units])
        grad_pre = both[units:] * (1.0 - hidden * hidden)
        both = jnp.concatenate([hidden, grad_pre], axis=0)
        both = jnp.concatenate(split(both, 2), axis=0)
        sums = sums + times(jnp.concatenate(pieces[:2], axis=0), both, (1, 1))
        result = times(after, both)
        result = result[:16] + result[16:32] + result[32:]
        for turn in range(at_once):
            results.append(result[:8, turn * LANES : (turn + 1) * LANES])
            x = start + turn
            place = (x % x_rows) * x_devices + x // x_rows
            tail_ref[place : place + 1, :] = result[8:9, turn * LANES : (turn + 1) * LANES]

    back_y = on_rows(results, y_back_ref[...])
    back = [jnp.where(row8 < 3, back_y[x], results[x]) for x in range(x_length)]
    back = smooth_rows(back)
    back = [jnp.where(row8 < 6, value, result) for value, result in zip(back, results)]
    for x_device in range(x_devices):
        first = x_device * x_rows
        parts = exchange(back[first : first + x_rows], y_rows)
        for turn in range(y_devices):
            place = (turn * x_devices + x_device) * RETURNED
            out_ref[place : place + 8, :] = parts[turn]
    tails = [tail_ref[x * x_devices : (x + 1) * x_devices, :] for x in range(x_rows)]
    tails = exchange(tails, y_rows)
    for turn in range(y_devices):
        place = turn * x_devices * RETURNED + 8
        out_ref[pl.ds(place, x_devices, stride=RETURNED), :] = tails[turn]

    sums = sums[:, : 2 * units] + sums[:, 2 * units :]
    sums = sums[:16] + sums[16:]
    moved = jnp.concatenate([sums[5:7, units:], STEP_SIZE * sums[13:16, :units]], axis=0)
    packed = jnp.concatenate([sums[:5, units:], moved], axis=1)
    for device in range(x_devices * y_devices):
        place = device * RETURNED + SENT
        out_ref[place : place + 5, :] = packed


def unpack_kernel(
    cells,
    in_ref,
    velocity_ref,
    cotangent_ref,
    z_ref,
    new_ref,
    grad_ref,
    in_grad_ref,
    bias_grad_ref,
    out_grad_ref,
):
    _, x_rows, y_rows, z_length = velocity_ref.shape
    block = x_rows * y_rows
    groups = LANES // block
    devices = z_length // groups
    units = in_grad_ref.shape[1]
    fields = []
    for start in range(0, SENT, groups):
        parts = [
            in_ref[pl.ds(min(field, SENT - 1), devices, stride=RETURNED), :]
            for field in range(start, start + groups)
        ]
        turned = jnp.concatenate(exchange(parts, block), axis=0).T
        fields.extend(turned[turn * block : (turn + 1) * block] for turn in range(groups))
    shape = (3, x_rows, y_rows, z_length)
    forcing = jnp.concatenate(fields[6:9], axis=0).reshape(shape)
    new_ref[...] = velocity_ref[...] + STEP_SIZE * forcing
    back_z = times_table(jnp.concatenate(fields[3:6], axis=0), z_ref[...])
    back = jnp.concatenate(fields[:3], axis=0) + back_z
    grad_ref[...] = cotangent_ref[...] + back.reshape(shape)

    sums = in_ref[SENT : SENT + 5, :]
    for device in range(1, devices):
        place = device * RETURNED + SENT
        sums = sums + in_ref[place : place + 5, :]
    sums = sums * (1.0 / cells)
    in_grad_ref[:5, :] = sums[:, :units]
    in_grad_ref[5:, :] = sums[:1, units:]
    bias_grad_ref[...] = sums[1:2, units:]
    out_grad_ref[...] = sums[2:, units:]


def on_device(kernel, shapes, scratch=(), **more):
    return pl.pallas_call(
        kernel,
        out_shape=[jax.ShapeDtypeStruct(shape, kind) for shape, kind in shapes],
        scratch_shapes=[*scratch],
        compiler_params=pltpu.CompilerParams(vmem_limit_bytes=32 * 1024 * 1024),
        **more,
    )


def fits(velocity, units):
    x_devices, y_devices = lax.axis_size("gx"), lax.axis_size("gy")
    _, x_rows, y_rows, z_length = velocity.shape
    return (
        z_length == LANES
        and x_rows * y_rows * LANES == LANES * LANES // 4
        and x_devices * y_devices * 4 == LANES
        and x_devices == 8
        and y_devices == x_rows
        and y_rows % 8 == 0
        and 2 * units == LANES
    )


def local_kernels(velocity, cotangent, weight_in, bias_in, weight_out):
    axes = ("gy", "gx")
    x_devices, y_devices = lax.axis_size("gx"), lax.axis_size("gy")
    devices = x_devices * y_devices
    _, x_rows, y_rows, z_length = velocity.shape
    units = weight_in.shape[1]
    cells = x_rows * x_devices * y_rows * y_devices * z_length
    z_table = derivative_table(z_length)
    y_table = np.kron(np.eye(z_length // devices), derivative_table(y_rows * y_devices))
    single = jnp.float32

    in_place = pl.BlockSpec(memory_space=pltpu.HBM)

    arguments = [
        velocity,
        cotangent,
        table(z_table.T),
        weight_in,
        bias_in[None],
        weight_out.T,
    ]
    arguments = [pltpu.with_memory_space_constraint(each, pltpu.HBM) for each in arguments]
    sent, *prepared = on_device(
        pack_kernel,
        [
            ((devices * SENT, LANES), single),
            *((values.shape, single) for values in arguments[3:]),
        ],
        [pltpu.VMEM(values.shape, values.dtype) for values in arguments[:3]]
        + [pltpu.SemaphoreType.DMA((len(arguments),))],
        in_specs=[in_place] * len(arguments),
    )(*arguments)
    sent = sent.reshape(devices, 1, SENT * LANES)
    sent = lax.all_to_all(sent, axes, 0, 0, tiled=True).reshape(devices * SENT, LANES)
    (back,) = on_device(
        functools.partial(middle_kernel, x_devices),
        [((devices * RETURNED, LANES), single)],
        [pltpu.VMEM((x_devices * x_rows, LANES), single)],
    )(sent, *prepared, split_table(y_table.T), split_table(y_table))
    back = back.reshape(devices, 1, RETURNED * LANES)
    back = lax.all_to_all(back, axes, 0, 0, tiled=True).reshape(devices * RETURNED, LANES)
    shapes = [velocity.shape, velocity.shape, (6, units), (1, units), (3, units)]
    new, grad, grad_in, grad_bias, grad_out = on_device(
        functools.partial(unpack_kernel, float(cells)), [(shape, single) for shape in shapes]
    )(back, velocity, cotangent, split_table(z_table))
    return (new, grad, grad_in, grad_bias[0], grad_out.T)


def local(velocity, cotangent, weight_in, bias_in, weight_out):
    chosen = local_kernels if fits(velocity, weight_in.shape[1]) else local_plain
    return chosen(velocity, cotangent, weight_in, bias_in, weight_out)


def solution(mesh):
    in_specs = (P(None, "gx", "gy", None), P(None, "gx", "gy", None), P(), P(), P())
    out_specs = (P(None, "gx", "gy", None), P(None, "gx", "gy", None), P(), P(), P())
    return jax.shard_map(local, mesh=mesh, in_specs=in_specs, out_specs=out_specs, check_vma=False)
```

```python
import functools

import jax
import jax.numpy as jnp
import ml_dtypes
import numpy as np
from jax import lax
from jax.experimental import pallas as pl
from jax.experimental.pallas import tpu as pltpu
from jax.sharding import PartitionSpec as P

FILTER_ALPHA = 0.499
FILTER_GAIN = 0.5 + FILTER_ALPHA
COMPACT_ALPHA = 1.0 / 3.0
STEP_SIZE = 0.5
PRECISE = lax.Precision.HIGHEST
LANES = 128
SENT = 9
RETURNED = 14
LEFT_PIECES = (0, 1, 0, 2, 1, 0)
RIGHT_PIECES = (0, 0, 1, 0, 1, 2)


def beside(length, offset):
    return np.eye(length, k=offset) + np.eye(length, k=-offset)


def smooth_table(length):
    left = np.eye(length) + FILTER_ALPHA * beside(length, 1)
    right = FILTER_GAIN * np.eye(length) + 0.5 * FILTER_GAIN * beside(length, 1)
    return np.linalg.solve(left, right)


def derivative_table(length):
    left = np.eye(length) + COMPACT_ALPHA * beside(length, 1)
    right = 7.0 / 9.0 * (np.eye(length, k=1) - np.eye(length, k=-1)) + 1.0 / 36.0 * (
        np.eye(length, k=2) - np.eye(length, k=-2)
    )
    return np.linalg.solve(left, right)


def table(values):
    return jnp.asarray(values.astype(np.float32))


def split_table(values):
    pieces = []
    rest = values.astype(np.float32)
    for _ in range(3):
        pieces.append(rest.astype(ml_dtypes.bfloat16))
        rest = rest - pieces[-1].astype(np.float32)
    return jnp.asarray(np.concatenate([pieces[turn] for turn in RIGHT_PIECES], axis=0))


def local_plain(velocity, cotangent, weight_in, bias_in, weight_out):
    axes = ("gx", "gy")
    x_devices, y_devices = lax.axis_size("gx"), lax.axis_size("gy")
    devices = x_devices * y_devices
    _, x_rows, y_rows, z_length = velocity.shape
    x_length, y_length = x_rows * x_devices, y_rows * y_devices
    units = weight_in.shape[1]
    z_rows = -(-z_length // devices)
    padding = z_rows * devices - z_length

    z_table = table(derivative_table(z_length))
    y_table = table(derivative_table(y_length))
    x_table = table(smooth_table(x_length))

    along_z = jnp.einsum("ab,kxyb->kxya", z_table, velocity, precision=PRECISE)
    fields = jnp.concatenate([velocity, along_z, cotangent], axis=0)
    fields = jnp.pad(fields, ((0, 0), (0, 0), (0, 0), (0, padding)))
    fields = fields.reshape(9, x_rows, y_rows, z_rows, devices)
    fields = fields.transpose(4, 0, 3, 1, 2).reshape(devices, 9, z_rows * x_rows * y_rows)
    fields = lax.all_to_all(fields, axes, 0, 0, tiled=True)
    fields = fields.reshape(x_devices, y_devices, 9, z_rows, x_rows, y_rows)
    fields = fields.transpose(2, 0, 4, 3, 1, 5).reshape(9, x_length, z_rows, y_length)

    smoothed = jnp.einsum("ab,kbzy->kazy", x_table, fields[:6], precision=PRECISE)
    along_y = jnp.einsum("ab,kxzb->kxza", y_table, smoothed[:3], precision=PRECISE)
    features = jnp.concatenate([along_y, smoothed[3:]], axis=0).reshape(6, -1)
    grad_out = STEP_SIZE * fields[6:].reshape(3, -1)

    hidden = jnp.tanh(jnp.dot(weight_in.T, features, precision=PRECISE) + bias_in[:, None])
    forcing = jnp.dot(weight_out.T, hidden, precision=PRECISE)
    grad_pre = jnp.dot(weight_out, grad_out, precision=PRECISE) * (1.0 - hidden * hidden)
    grad_features = jnp.dot(weight_in, grad_pre, precision=PRECISE)
    sum_in = jnp.dot(features, grad_pre.T, precision=PRECISE)
    sum_bias = jnp.sum(grad_pre, axis=1)
    sum_out = jnp.dot(grad_out, hidden.T, precision=PRECISE)

    grad_features = grad_features.reshape(6, x_length, z_rows, y_length)
    back_y = jnp.einsum("ba,kxzb->kxza", y_table, grad_features[:3], precision=PRECISE)
    back = jnp.concatenate([back_y, grad_features[3:]], axis=0)
    back = jnp.einsum("ab,kbzy->kazy", x_table, back, precision=PRECISE)
    back = jnp.concatenate([forcing.reshape(3, x_length, z_rows, y_length), back], axis=0)
    back = back.reshape(9, x_devices, x_rows, z_rows, y_devices, y_rows)
    back = back.transpose(1, 4, 0, 3, 2, 5).reshape(devices, -1)
    sums = jnp.concatenate([sum_in, sum_bias[None], sum_out], axis=0).reshape(1, -1)
    cells = back.shape[1]
    back = jnp.concatenate([back, jnp.broadcast_to(sums, (devices, 10 * units))], axis=1)
    back = lax.all_to_all(back, axes, 0, 0, tiled=True)

    sums = jnp.sum(back[:, cells:], axis=0).reshape(10, units)
    sums = sums / float(x_length * y_length * z_length)
    back = back[:, :cells].reshape(devices, 9, z_rows, x_rows, y_rows)
    back = back.transpose(1, 3, 4, 2, 0).reshape(9, x_rows, y_rows, -1)[..., :z_length]
    new_velocity = velocity + STEP_SIZE * back[:3]
    back_z = jnp.einsum("ba,kxyb->kxya", z_table, back[6:], precision=PRECISE)
    grad_velocity = cotangent + back[3:6] + back_z
    return (new_velocity, grad_velocity, sums[:6], sums[6], sums[7:].T)


def exchange(parts, width):
    parts = list(parts)
    lane = lax.broadcasted_iota(jnp.int32, parts[0].shape, 1)
    step = len(parts) // 2
    while step:
        shift = step * width
        upper = (lane & shift) != 0
        for low in range(len(parts)):
            if low & step == 0:
                first, second = parts[low], parts[low + step]
                parts[low] = jnp.where(upper, pltpu.roll(second, shift, 1), first)
                parts[low + step] = jnp.where(upper, second, pltpu.roll(first, LANES - shift, 1))
        step //= 2
    return parts


def smooth_rows(rows):
    length = len(rows)
    half = length // 2
    scales = []
    before = 0.0
    for _ in range(half):
        scales.append(1.0 / (1.0 - FILTER_ALPHA * FILTER_ALPHA * before))
        before = scales[-1]
    factors = [-FILTER_ALPHA * scale for scale in scales]
    forward = np.cumprod([1.0] + factors[1:])
    backward = np.cumprod([1.0] + factors[-2::-1])[::-1]
    own = 0.5 * FILTER_GAIN / FILTER_ALPHA

    sides = [list(range(half)), list(range(length - 1, half - 1, -1))]
    running = []
    for side in sides:
        sums = []
        for turn, row in enumerate(side):
            value = rows[row] * float(scales[turn] / forward[turn])
            sums.append(value if turn == 0 else sums[-1] + value)
        running.append(sums)
    middle = forward[-1] / (1.0 - factors[-1] * factors[-1])
    cross = middle * factors[-1]
    smoothed = [None] * length
    for side, sums, others in zip(sides, running, running[::-1]):
        value = float(middle) * sums[-1] + float(cross) * others[-1]
        for turn in reversed(range(half)):
            if turn < half - 1:
                value = value + float(forward[turn] / backward[turn]) * sums[turn]
            row = side[turn]
            smoothed[row] = own * rows[row] + float((FILTER_GAIN - own) * backward[turn]) * value
    return smoothed


def times(left, right, contract=(1, 0)):
    dims = (((contract[0],), (contract[1],)), ((), ()))
    return lax.dot_general(left, right, dims, preferred_element_type=jnp.float32)


def split(values, count):
    pieces = []
    for turn in range(count):
        pieces.append(values.astype(jnp.bfloat16))
        if turn + 1 < count:
            values = values - pieces[-1].astype(jnp.float32)
    return pieces


def times_table(values, wide_table):
    pieces = split(values, 3)
    return times(jnp.concatenate([pieces[turn] for turn in LEFT_PIECES], axis=1), wide_table)


def on_rows(rows, wide_table):
    out = times_table(jnp.concatenate(rows, axis=0), wide_table)
    return [out[8 * turn : 8 * turn + 8] for turn in range(len(rows))]


def pack_kernel(
    velocity_hbm,
    cotangent_hbm,
    z_hbm,
    weight_in_hbm,
    bias_hbm,
    weight_out_hbm,
    out_ref,
    weight_in_ref,
    bias_ref,
    weight_out_ref,
    velocity_ref,
    cotangent_ref,
    z_ref,
    arrived,
):
    pairs = [
        (weight_in_hbm, weight_in_ref),
        (bias_hbm, bias_ref),
        (weight_out_hbm, weight_out_ref),
        (velocity_hbm, velocity_ref),
        (cotangent_hbm, cotangent_ref),
        (z_hbm, z_ref),
    ]
    copies = [
        pltpu.make_async_copy(source, target, arrived.at[turn])
        for turn, (source, target) in enumerate(pairs)
    ]
    for copy in copies:
        copy.start()

    for copy in copies[3:]:
        copy.wait()
    _, x_rows, y_rows, z_length = velocity_ref.shape
    block = x_rows * y_rows
    groups = LANES // block
    devices = z_length // groups
    velocity = [velocity_ref[part].reshape(block, z_length) for part in range(3)]
    cotangent = [cotangent_ref[part].reshape(block, z_length) for part in range(3)]

    table_pieces = split(z_ref[...], 3)
    pieces = split(jnp.concatenate([*velocity, velocity[0]], axis=0), 3)
    along_z = times(
        jnp.concatenate([table_pieces[turn] for turn in RIGHT_PIECES], axis=1),
        jnp.concatenate([pieces[turn] for turn in LEFT_PIECES], axis=1),
        (1, 1),
    )
    fill = jnp.zeros_like(velocity[0])
    turned = [
        (jnp.concatenate([*velocity, cotangent[1]], axis=0).T, (0, 1, 2, 6)),
        (jnp.concatenate([cotangent[2], cotangent[0], fill, fill], axis=0).T, (7, 8)),
        (along_z, (3, 4, 5)),
    ]
    for fields, places in turned:
        parts = [fields[group * devices : (group + 1) * devices] for group in range(groups)]
        for part, place in zip(exchange(parts, block), places):
            out_ref[pl.ds(place, devices, stride=SENT), :] = part
    for copy in copies[:3]:
        copy.wait()


def network_matrices(weight_in_ref, bias_ref, weight_out_ref):
    weight_in = weight_in_ref[...]
    weight_out = weight_out_ref[...]
    units = weight_in.shape[1]
    zeros = functools.partial(jnp.zeros, dtype=jnp.float32)
    before = jnp.concatenate(
        [
            jnp.concatenate([weight_in, bias_ref[...], zeros((9, units))], axis=0),
            jnp.concatenate([zeros((13, units)), STEP_SIZE * weight_out], axis=0),
        ],
        axis=1,
    )
    after = jnp.concatenate(
        [
            jnp.concatenate([zeros((6, units)), weight_out, zeros((7, units))], axis=0),
            jnp.concatenate([weight_in, zeros((10, units))], axis=0),
        ],
        axis=1,
    )
    pieces = [piece.astype(jnp.float32) for piece in split(before, 3)]
    before = jnp.concatenate([pieces[turn] for turn in RIGHT_PIECES + (1, 2)], axis=0)
    before = before.T.astype(jnp.bfloat16)
    pieces = split(after, 3)
    after = jnp.concatenate(
        [
            jnp.concatenate([pieces[0], pieces[0]], axis=1),
            jnp.concatenate([pieces[1], pieces[1]], axis=1),
            jnp.concatenate([pieces[2], jnp.zeros_like(pieces[2])], axis=1),
        ],
        axis=0,
    )
    return before, after


def middle_kernel(
    x_devices,
    in_ref,
    weight_in_ref,
    bias_ref,
    weight_out_ref,
    y_ref,
    y_back_ref,
    out_ref,
    tail_ref,
):
    y_devices = in_ref.shape[0] // SENT // x_devices
    x_rows = y_devices
    x_length = x_devices * x_rows
    units = weight_in_ref.shape[1]
    y_rows = LANES // y_devices // x_rows
    row8 = lax.broadcasted_iota(jnp.int32, (8, LANES), 0)

    planes = []
    for x_device in range(x_devices):
        places = [(turn * x_devices + x_device) * SENT for turn in range(y_devices)]
        parts = [in_ref[place : place + 8, :] for place in places]
        planes.extend(exchange(parts, y_rows))
    tails = [
        in_ref[pl.ds(turn * x_devices * SENT + 8, x_devices, stride=SENT), :]
        for turn in range(y_devices)
    ]
    tails = exchange(tails, y_rows)

    smoothed = smooth_rows(planes)
    along_y = on_rows(smoothed, y_ref[...])
    upper_rows = []
    lower_rows = []
    for x in range(x_length):
        features = jnp.where(row8 < 3, along_y[x], smoothed[x])
        features = jnp.where(row8 < 6, features, jnp.where(row8 == 6, 1.0, 0.0))
        last = tails[x % x_rows][x // x_rows : x // x_rows + 1]
        upper_rows.append(features)
        lower_rows.append(jnp.where(row8 == 5, last, planes[x]))

    before, after = network_matrices(weight_in_ref, bias_ref, weight_out_ref)
    at_once = x_length
    sums = jnp.zeros((32, 4 * units), jnp.float32)
    results = []
    for start in range(0, x_length, at_once):
        stop = start + at_once
        cells = jnp.concatenate(
            [
                jnp.concatenate(upper_rows[start:stop], axis=1),
                jnp.concatenate(lower_rows[start:stop], axis=1),
            ],
            axis=0,
        )
        pieces = split(cells, 3)
        both = times(before, jnp.concatenate([pieces[turn] for turn in LEFT_PIECES + (2, 1)], axis=0))
        hidden = jnp.tanh(both[:units])
        grad_pre = both[units:] * (1.0 - hidden * hidden)
        both = jnp.concatenate([hidden, grad_pre], axis=0)
        both = jnp.concatenate(split(both, 2), axis=0)
        sums = sums + times(jnp.concatenate(pieces[:2], axis=0), both, (1, 1))
        result = times(after, both)
        result = result[:16] + result[16:32] + result[32:]
        for turn in range(at_once):
            results.append(result[:8, turn * LANES : (turn + 1) * LANES])
            x = start + turn
            place = (x % x_rows) * x_devices + x // x_rows
            tail_ref[place : place + 1, :] = result[8:9, turn * LANES : (turn + 1) * LANES]

    back_y = on_rows(results, y_back_ref[...])
    back = [jnp.where(row8 < 3, back_y[x], results[x]) for x in range(x_length)]
    back = smooth_rows(back)
    back = [jnp.where(row8 < 6, value, result) for value, result in zip(back, results)]
    for x_device in range(x_devices):
        first = x_device * x_rows
        parts = exchange(back[first : first + x_rows], y_rows)
        for turn in range(y_devices):
            place = (turn * x_devices + x_device) * RETURNED
            out_ref[place : place + 8, :] = parts[turn]
    tails = [tail_ref[x * x_devices : (x + 1) * x_devices, :] for x in range(x_rows)]
    tails = exchange(tails, y_rows)
    for turn in range(y_devices):
        place = turn * x_devices * RETURNED + 8
        out_ref[pl.ds(place, x_devices, stride=RETURNED), :] = tails[turn]

    sums = sums[:, : 2 * units] + sums[:, 2 * units :]
    sums = sums[:16] + sums[16:]
    moved = jnp.concatenate([sums[5:7, units:], STEP_SIZE * sums[13:16, :units]], axis=0)
    packed = jnp.concatenate([sums[:5, units:], moved], axis=1)
    for device in range(x_devices * y_devices):
        place = device * RETURNED + SENT
        out_ref[place : place + 5, :] = packed


def unpack_kernel(
    cells,
    in_ref,
    velocity_ref,
    cotangent_ref,
    z_ref,
    new_ref,
    grad_ref,
    in_grad_ref,
    bias_grad_ref,
    out_grad_ref,
):
    _, x_rows, y_rows, z_length = velocity_ref.shape
    block = x_rows * y_rows
    groups = LANES // block
    devices = z_length // groups
    units = in_grad_ref.shape[1]
    fields = []
    for start in range(0, SENT, groups):
        parts = [
            in_ref[pl.ds(min(field, SENT - 1), devices, stride=RETURNED), :]
            for field in range(start, start + groups)
        ]
        turned = jnp.concatenate(exchange(parts, block), axis=0).T
        fields.extend(turned[turn * block : (turn + 1) * block] for turn in range(groups))
    shape = (3, x_rows, y_rows, z_length)
    forcing = jnp.concatenate(fields[6:9], axis=0).reshape(shape)
    new_ref[...] = velocity_ref[...] + STEP_SIZE * forcing
    back_z = times_table(jnp.concatenate(fields[3:6], axis=0), z_ref[...])
    back = jnp.concatenate(fields[:3], axis=0) + back_z
    grad_ref[...] = cotangent_ref[...] + back.reshape(shape)

    sums = in_ref[SENT : SENT + 5, :]
    for device in range(1, devices):
        place = device * RETURNED + SENT
        sums = sums + in_ref[place : place + 5, :]
    sums = sums * (1.0 / cells)
    in_grad_ref[:5, :] = sums[:, :units]
    in_grad_ref[5:, :] = sums[:1, units:]
    bias_grad_ref[...] = sums[1:2, units:]
    out_grad_ref[...] = sums[2:, units:]


def on_device(kernel, shapes, scratch=(), **more):
    return pl.pallas_call(
        kernel,
        out_shape=[jax.ShapeDtypeStruct(shape, kind) for shape, kind in shapes],
        scratch_shapes=[*scratch],
        compiler_params=pltpu.CompilerParams(vmem_limit_bytes=32 * 1024 * 1024),
        **more,
    )


def fits(velocity, units):
    x_devices, y_devices = lax.axis_size("gx"), lax.axis_size("gy")
    _, x_rows, y_rows, z_length = velocity.shape
    return (
        z_length == LANES
        and x_rows * y_rows * LANES == LANES * LANES // 4
        and x_devices * y_devices * 4 == LANES
        and x_devices == 8
        and y_devices == x_rows
        and y_rows % 8 == 0
        and 2 * units == LANES
    )


def local_kernels(velocity, cotangent, weight_in, bias_in, weight_out):
    axes = ("gy", "gx")
    x_devices, y_devices = lax.axis_size("gx"), lax.axis_size("gy")
    devices = x_devices * y_devices
    _, x_rows, y_rows, z_length = velocity.shape
    units = weight_in.shape[1]
    cells = x_rows * x_devices * y_rows * y_devices * z_length
    z_table = derivative_table(z_length)
    y_table = np.kron(np.eye(z_length // devices), derivative_table(y_rows * y_devices))
    single = jnp.float32

    in_place = pl.BlockSpec(memory_space=pltpu.HBM)

    arguments = [
        velocity,
        cotangent,
        table(z_table),
        weight_in,
        bias_in[None],
        weight_out.T,
    ]
    arguments = [pltpu.with_memory_space_constraint(each, pltpu.HBM) for each in arguments]
    sent, *prepared = on_device(
        pack_kernel,
        [
            ((devices * SENT, LANES), single),
            *((values.shape, single) for values in arguments[3:]),
        ],
        [pltpu.VMEM(values.shape, values.dtype) for values in arguments[:3]]
        + [pltpu.SemaphoreType.DMA((len(arguments),))],
        in_specs=[in_place] * len(arguments),
    )(*arguments)
    sent = sent.reshape(devices, 1, SENT * LANES)
    sent = lax.all_to_all(sent, axes, 0, 0, tiled=True).reshape(devices * SENT, LANES)
    (back,) = on_device(
        functools.partial(middle_kernel, x_devices),
        [((devices * RETURNED, LANES), single)],
        [pltpu.VMEM((x_devices * x_rows, LANES), single)],
    )(sent, *prepared, split_table(y_table.T), split_table(y_table))
    back = back.reshape(devices, 1, RETURNED * LANES)
    back = lax.all_to_all(back, axes, 0, 0, tiled=True).reshape(devices * RETURNED, LANES)
    shapes = [velocity.shape, velocity.shape, (6, units), (1, units), (3, units)]
    new, grad, grad_in, grad_bias, grad_out = on_device(
        functools.partial(unpack_kernel, float(cells)), [(shape, single) for shape in shapes]
    )(back, velocity, cotangent, split_table(z_table))
    return (new, grad, grad_in, grad_bias[0], grad_out.T)


def local(velocity, cotangent, weight_in, bias_in, weight_out):
    chosen = local_kernels if fits(velocity, weight_in.shape[1]) else local_plain
    return chosen(velocity, cotangent, weight_in, bias_in, weight_out)


def solution(mesh):
    in_specs = (P(None, "gx", "gy", None), P(None, "gx", "gy", None), P(), P(), P())
    out_specs = (P(None, "gx", "gy", None), P(None, "gx", "gy", None), P(), P(), P())
    return jax.shard_map(local, mesh=mesh, in_specs=in_specs, out_specs=out_specs, check_vma=False)
```

```python
import functools

import jax
import jax.numpy as jnp
import ml_dtypes
import numpy as np
from jax import lax
from jax.experimental import pallas as pl
from jax.experimental.pallas import tpu as pltpu
from jax.sharding import PartitionSpec as P

FILTER_ALPHA = 0.499
FILTER_GAIN = 0.5 + FILTER_ALPHA
COMPACT_ALPHA = 1.0 / 3.0
STEP_SIZE = 0.5
PRECISE = lax.Precision.HIGHEST
LANES = 128
SENT = 9
RETURNED = 14
LEFT_PIECES = (0, 1, 0, 2, 1, 0)
RIGHT_PIECES = (0, 0, 1, 0, 1, 2)


def beside(length, offset):
    return np.eye(length, k=offset) + np.eye(length, k=-offset)


def smooth_table(length):
    left = np.eye(length) + FILTER_ALPHA * beside(length, 1)
    right = FILTER_GAIN * np.eye(length) + 0.5 * FILTER_GAIN * beside(length, 1)
    return np.linalg.solve(left, right)


def derivative_table(length):
    left = np.eye(length) + COMPACT_ALPHA * beside(length, 1)
    right = 7.0 / 9.0 * (np.eye(length, k=1) - np.eye(length, k=-1)) + 1.0 / 36.0 * (
        np.eye(length, k=2) - np.eye(length, k=-2)
    )
    return np.linalg.solve(left, right)


def table(values):
    return jnp.asarray(values.astype(np.float32))


def split_table(values):
    pieces = []
    rest = values.astype(np.float32)
    for _ in range(3):
        pieces.append(rest.astype(ml_dtypes.bfloat16))
        rest = rest - pieces[-1].astype(np.float32)
    return jnp.asarray(np.concatenate([pieces[turn] for turn in RIGHT_PIECES], axis=0))


def local_plain(velocity, cotangent, weight_in, bias_in, weight_out):
    axes = ("gx", "gy")
    x_devices, y_devices = lax.axis_size("gx"), lax.axis_size("gy")
    devices = x_devices * y_devices
    _, x_rows, y_rows, z_length = velocity.shape
    x_length, y_length = x_rows * x_devices, y_rows * y_devices
    units = weight_in.shape[1]
    z_rows = -(-z_length // devices)
    padding = z_rows * devices - z_length

    z_table = table(derivative_table(z_length))
    y_table = table(derivative_table(y_length))
    x_table = table(smooth_table(x_length))

    along_z = jnp.einsum("ab,kxyb->kxya", z_table, velocity, precision=PRECISE)
    fields = jnp.concatenate([velocity, along_z, cotangent], axis=0)
    fields = jnp.pad(fields, ((0, 0), (0, 0), (0, 0), (0, padding)))
    fields = fields.reshape(9, x_rows, y_rows, z_rows, devices)
    fields = fields.transpose(4, 0, 3, 1, 2).reshape(devices, 9, z_rows * x_rows * y_rows)
    fields = lax.all_to_all(fields, axes, 0, 0, tiled=True)
    fields = fields.reshape(x_devices, y_devices, 9, z_rows, x_rows, y_rows)
    fields = fields.transpose(2, 0, 4, 3, 1, 5).reshape(9, x_length, z_rows, y_length)

    smoothed = jnp.einsum("ab,kbzy->kazy", x_table, fields[:6], precision=PRECISE)
    along_y = jnp.einsum("ab,kxzb->kxza", y_table, smoothed[:3], precision=PRECISE)
    features = jnp.concatenate([along_y, smoothed[3:]], axis=0).reshape(6, -1)
    grad_out = STEP_SIZE * fields[6:].reshape(3, -1)

    hidden = jnp.tanh(jnp.dot(weight_in.T, features, precision=PRECISE) + bias_in[:, None])
    forcing = jnp.dot(weight_out.T, hidden, precision=PRECISE)
    grad_pre = jnp.dot(weight_out, grad_out, precision=PRECISE) * (1.0 - hidden * hidden)
    grad_features = jnp.dot(weight_in, grad_pre, precision=PRECISE)
    sum_in = jnp.dot(features, grad_pre.T, precision=PRECISE)
    sum_bias = jnp.sum(grad_pre, axis=1)
    sum_out = jnp.dot(grad_out, hidden.T, precision=PRECISE)

    grad_features = grad_features.reshape(6, x_length, z_rows, y_length)
    back_y = jnp.einsum("ba,kxzb->kxza", y_table, grad_features[:3], precision=PRECISE)
    back = jnp.concatenate([back_y, grad_features[3:]], axis=0)
    back = jnp.einsum("ab,kbzy->kazy", x_table, back, precision=PRECISE)
    back = jnp.concatenate([forcing.reshape(3, x_length, z_rows, y_length), back], axis=0)
    back = back.reshape(9, x_devices, x_rows, z_rows, y_devices, y_rows)
    back = back.transpose(1, 4, 0, 3, 2, 5).reshape(devices, -1)
    sums = jnp.concatenate([sum_in, sum_bias[None], sum_out], axis=0).reshape(1, -1)
    cells = back.shape[1]
    back = jnp.concatenate([back, jnp.broadcast_to(sums, (devices, 10 * units))], axis=1)
    back = lax.all_to_all(back, axes, 0, 0, tiled=True)

    sums = jnp.sum(back[:, cells:], axis=0).reshape(10, units)
    sums = sums / float(x_length * y_length * z_length)
    back = back[:, :cells].reshape(devices, 9, z_rows, x_rows, y_rows)
    back = back.transpose(1, 3, 4, 2, 0).reshape(9, x_rows, y_rows, -1)[..., :z_length]
    new_velocity = velocity + STEP_SIZE * back[:3]
    back_z = jnp.einsum("ba,kxyb->kxya", z_table, back[6:], precision=PRECISE)
    grad_velocity = cotangent + back[3:6] + back_z
    return (new_velocity, grad_velocity, sums[:6], sums[6], sums[7:].T)


def exchange(parts, width):
    parts = list(parts)
    lane = lax.broadcasted_iota(jnp.int32, parts[0].shape, 1)
    step = len(parts) // 2
    while step:
        shift = step * width
        upper = (lane & shift) != 0
        for low in range(len(parts)):
            if low & step == 0:
                first, second = parts[low], parts[low + step]
                parts[low] = jnp.where(upper, pltpu.roll(second, shift, 1), first)
                parts[low + step] = jnp.where(upper, second, pltpu.roll(first, LANES - shift, 1))
        step //= 2
    return parts


def smooth_rows(rows):
    length = len(rows)
    half = length // 2
    scales = []
    before = 0.0
    for _ in range(half):
        scales.append(1.0 / (1.0 - FILTER_ALPHA * FILTER_ALPHA * before))
        before = scales[-1]
    factors = [-FILTER_ALPHA * scale for scale in scales]
    forward = np.cumprod([1.0] + factors[1:])
    backward = np.cumprod([1.0] + factors[-2::-1])[::-1]
    own = 0.5 * FILTER_GAIN / FILTER_ALPHA

    sides = [list(range(half)), list(range(length - 1, half - 1, -1))]
    running = []
    for side in sides:
        sums = []
        for turn, row in enumerate(side):
            value = rows[row] * float(scales[turn] / forward[turn])
            sums.append(value if turn == 0 else sums[-1] + value)
        running.append(sums)
    middle = forward[-1] / (1.0 - factors[-1] * factors[-1])
    cross = middle * factors[-1]
    smoothed = [None] * length
    for side, sums, others in zip(sides, running, running[::-1]):
        value = float(middle) * sums[-1] + float(cross) * others[-1]
        for turn in reversed(range(half)):
            if turn < half - 1:
                value = value + float(forward[turn] / backward[turn]) * sums[turn]
            row = side[turn]
            smoothed[row] = own * rows[row] + float((FILTER_GAIN - own) * backward[turn]) * value
    return smoothed


def times(left, right, contract=(1, 0)):
    dims = (((contract[0],), (contract[1],)), ((), ()))
    return lax.dot_general(left, right, dims, preferred_element_type=jnp.float32)


def split(values, count):
    pieces = []
    for turn in range(count):
        pieces.append(values.astype(jnp.bfloat16))
        if turn + 1 < count:
            values = values - pieces[-1].astype(jnp.float32)
    return pieces


def times_table(values, wide_table):
    pieces = split(values, 3)
    return times(jnp.concatenate([pieces[turn] for turn in LEFT_PIECES], axis=1), wide_table)


def on_rows(rows, wide_table):
    out = times_table(jnp.concatenate(rows, axis=0), wide_table)
    return [out[8 * turn : 8 * turn + 8] for turn in range(len(rows))]


def pack_kernel(
    velocity_hbm,
    cotangent_hbm,
    z_hbm,
    weight_in_hbm,
    bias_hbm,
    weight_out_hbm,
    out_ref,
    weight_in_ref,
    bias_ref,
    weight_out_ref,
    velocity_ref,
    cotangent_ref,
    z_ref,
    arrived,
):
    pairs = [
        (weight_in_hbm, weight_in_ref),
        (bias_hbm, bias_ref),
        (weight_out_hbm, weight_out_ref),
        (velocity_hbm, velocity_ref),
        (cotangent_hbm, cotangent_ref),
        (z_hbm, z_ref),
    ]
    copies = [
        pltpu.make_async_copy(source, target, arrived.at[turn])
        for turn, (source, target) in enumerate(pairs)
    ]
    for copy in copies:
        copy.start()

    for copy in copies[3:]:
        copy.wait()
    _, x_rows, y_rows, z_length = velocity_ref.shape
    block = x_rows * y_rows
    groups = LANES // block
    devices = z_length // groups
    velocity = [velocity_ref[part].reshape(block, z_length) for part in range(3)]
    cotangent = [cotangent_ref[part].reshape(block, z_length) for part in range(3)]

    table_pieces = split(z_ref[...], 3)
    pieces = split(jnp.concatenate([*velocity, velocity[0]], axis=0), 3)
    along_z = times(
        jnp.concatenate([table_pieces[turn] for turn in RIGHT_PIECES], axis=1),
        jnp.concatenate([pieces[turn] for turn in LEFT_PIECES], axis=1),
        (1, 1),
    )
    fill = jnp.zeros_like(velocity[0])
    turned = [
        (jnp.concatenate([*velocity, cotangent[1]], axis=0).T, (0, 1, 2, 6)),
        (jnp.concatenate([cotangent[2], cotangent[0], fill, fill], axis=0).T, (7, 8)),
        (along_z, (3, 4, 5)),
    ]
    for fields, places in turned:
        parts = [fields[group * devices : (group + 1) * devices] for group in range(groups)]
        for part, place in zip(exchange(parts, block), places):
            out_ref[pl.ds(place, devices, stride=SENT), :] = part
    for copy in copies[:3]:
        copy.wait()


def network_matrices(weight_in_ref, bias_ref, weight_out_ref):
    weight_in = weight_in_ref[...]
    weight_out = weight_out_ref[...]
    units = weight_in.shape[1]
    zeros = functools.partial(jnp.zeros, dtype=jnp.float32)
    before = jnp.concatenate(
        [
            jnp.concatenate([weight_in, bias_ref[...], zeros((9, units))], axis=0),
            jnp.concatenate([zeros((13, units)), STEP_SIZE * weight_out], axis=0),
        ],
        axis=1,
    )
    after = jnp.concatenate(
        [
            jnp.concatenate([zeros((6, units)), weight_out, zeros((7, units))], axis=0),
            jnp.concatenate([weight_in, zeros((10, units))], axis=0),
        ],
        axis=1,
    )
    pieces = [piece.astype(jnp.float32) for piece in split(before, 3)]
    before = jnp.concatenate([pieces[turn] for turn in RIGHT_PIECES + (1, 2)], axis=0)
    before = before.T.astype(jnp.bfloat16)
    pieces = split(after, 3)
    after = jnp.concatenate(
        [
            jnp.concatenate([pieces[0], pieces[0]], axis=1),
            jnp.concatenate([pieces[1], pieces[1]], axis=1),
            jnp.concatenate([pieces[2], jnp.zeros_like(pieces[2])], axis=1),
        ],
        axis=0,
    )
    return before, after


def middle_kernel(
    x_devices,
    in_ref,
    weight_in_ref,
    bias_ref,
    weight_out_ref,
    y_ref,
    y_back_ref,
    out_ref,
    tail_ref,
):
    y_devices = in_ref.shape[0] // SENT // x_devices
    x_rows = y_devices
    x_length = x_devices * x_rows
    units = weight_in_ref.shape[1]
    y_rows = LANES // y_devices // x_rows
    row8 = lax.broadcasted_iota(jnp.int32, (8, LANES), 0)

    planes = []
    for x_device in range(x_devices):
        places = [(turn * x_devices + x_device) * SENT for turn in range(y_devices)]
        parts = [in_ref[place : place + 8, :] for place in places]
        planes.extend(exchange(parts, y_rows))
    tails = [
        in_ref[pl.ds(turn * x_devices * SENT + 8, x_devices, stride=SENT), :]
        for turn in range(y_devices)
    ]
    tails = exchange(tails, y_rows)

    smoothed = smooth_rows(planes)
    along_y = on_rows(smoothed, y_ref[...])
    upper_rows = []
    lower_rows = []
    for x in range(x_length):
        features = jnp.where(row8 < 3, along_y[x], smoothed[x])
        features = jnp.where(row8 < 6, features, jnp.where(row8 == 6, 1.0, 0.0))
        last = tails[x % x_rows][x // x_rows : x // x_rows + 1]
        upper_rows.append(features)
        lower_rows.append(jnp.where(row8 == 5, last, planes[x]))

    before, after = network_matrices(weight_in_ref, bias_ref, weight_out_ref)
    at_once = x_length
    sums = jnp.zeros((32, 4 * units), jnp.float32)
    results = []
    for start in range(0, x_length, at_once):
        stop = start + at_once
        cells = jnp.concatenate(
            [
                jnp.concatenate(upper_rows[start:stop], axis=1),
                jnp.concatenate(lower_rows[start:stop], axis=1),
            ],
            axis=0,
        )
        pieces = split(cells, 3)
        both = times(before, jnp.concatenate([pieces[turn] for turn in LEFT_PIECES + (2, 1)], axis=0))
        hidden = jnp.tanh(both[:units])
        grad_pre = both[units:] * (1.0 - hidden * hidden)
        both = jnp.concatenate([hidden, grad_pre], axis=0)
        both = jnp.concatenate(split(both, 2), axis=0)
        sums = sums + times(jnp.concatenate(pieces[:2], axis=0), both, (1, 1))
        result = times(after, both)
        result = result[:16] + result[16:32] + result[32:]
        for turn in range(at_once):
            results.append(result[:8, turn * LANES : (turn + 1) * LANES])
            x = start + turn
            place = (x % x_rows) * x_devices + x // x_rows
            tail_ref[place : place + 1, :] = result[8:9, turn * LANES : (turn + 1) * LANES]

    back_y = on_rows(results, y_back_ref[...])
    back = [jnp.where(row8 < 3, back_y[x], results[x]) for x in range(x_length)]
    back = smooth_rows(back)
    back = [jnp.where(row8 < 6, value, result) for value, result in zip(back, results)]
    for x_device in range(x_devices):
        first = x_device * x_rows
        parts = exchange(back[first : first + x_rows], y_rows)
        for turn in range(y_devices):
            place = (turn * x_devices + x_device) * RETURNED
            out_ref[place : place + 8, :] = parts[turn]
    tails = [tail_ref[x * x_devices : (x + 1) * x_devices, :] for x in range(x_rows)]
    tails = exchange(tails, y_rows)
    for turn in range(y_devices):
        place = turn * x_devices * RETURNED + 8
        out_ref[pl.ds(place, x_devices, stride=RETURNED), :] = tails[turn]

    sums = sums[:, : 2 * units] + sums[:, 2 * units :]
    sums = sums[:16] + sums[16:]
    moved = jnp.concatenate([sums[5:7, units:], STEP_SIZE * sums[13:16, :units]], axis=0)
    packed = jnp.concatenate([sums[:5, units:], moved], axis=1)
    for device in range(x_devices * y_devices):
        place = device * RETURNED + SENT
        out_ref[place : place + 5, :] = packed


def unpack_kernel(
    cells,
    in_ref,
    velocity_ref,
    cotangent_ref,
    z_ref,
    new_ref,
    grad_ref,
    in_grad_ref,
    bias_grad_ref,
    out_grad_ref,
):
    _, x_rows, y_rows, z_length = velocity_ref.shape
    block = x_rows * y_rows
    groups = LANES // block
    devices = z_length // groups
    units = in_grad_ref.shape[1]

    def three_fields(start):
        parts = [
            in_ref[pl.ds(start + min(field, 2), devices, stride=RETURNED), :]
            for field in range(groups)
        ]
        return jnp.concatenate(exchange(parts, block), axis=0).T[: 3 * block]

    back_z = times_table(three_fields(3), z_ref[...])
    back = three_fields(0)
    forcing = three_fields(6)
    shape = (3, x_rows, y_rows, z_length)
    forcing = forcing.reshape(shape)
    new_ref[...] = velocity_ref[...] + STEP_SIZE * forcing
    back = back + back_z
    grad_ref[...] = cotangent_ref[...] + back.reshape(shape)

    sums = in_ref[SENT : SENT + 5, :]
    for device in range(1, devices):
        place = device * RETURNED + SENT
        sums = sums + in_ref[place : place + 5, :]
    sums = sums * (1.0 / cells)
    in_grad_ref[:5, :] = sums[:, :units]
    in_grad_ref[5:, :] = sums[:1, units:]
    bias_grad_ref[...] = sums[1:2, units:]
    out_grad_ref[...] = sums[2:, units:]


def on_device(kernel, shapes, scratch=(), **more):
    return pl.pallas_call(
        kernel,
        out_shape=[jax.ShapeDtypeStruct(shape, kind) for shape, kind in shapes],
        scratch_shapes=[*scratch],
        compiler_params=pltpu.CompilerParams(vmem_limit_bytes=32 * 1024 * 1024),
        **more,
    )


def fits(velocity, units):
    x_devices, y_devices = lax.axis_size("gx"), lax.axis_size("gy")
    _, x_rows, y_rows, z_length = velocity.shape
    return (
        z_length == LANES
        and x_rows * y_rows * LANES == LANES * LANES // 4
        and x_devices * y_devices * 4 == LANES
        and x_devices == 8
        and y_devices == x_rows
        and y_rows % 8 == 0
        and 2 * units == LANES
    )


def local_kernels(velocity, cotangent, weight_in, bias_in, weight_out):
    axes = ("gy", "gx")
    x_devices, y_devices = lax.axis_size("gx"), lax.axis_size("gy")
    devices = x_devices * y_devices
    _, x_rows, y_rows, z_length = velocity.shape
    units = weight_in.shape[1]
    cells = x_rows * x_devices * y_rows * y_devices * z_length
    z_table = derivative_table(z_length)
    y_table = np.kron(np.eye(z_length // devices), derivative_table(y_rows * y_devices))
    single = jnp.float32

    in_place = pl.BlockSpec(memory_space=pltpu.HBM)

    arguments = [
        velocity,
        cotangent,
        table(z_table),
        weight_in,
        bias_in[None],
        weight_out.T,
    ]
    arguments = [pltpu.with_memory_space_constraint(each, pltpu.HBM) for each in arguments]
    sent, *prepared = on_device(
        pack_kernel,
        [
            ((devices * SENT, LANES), single),
            *((values.shape, single) for values in arguments[3:]),
        ],
        [pltpu.VMEM(values.shape, values.dtype) for values in arguments[:3]]
        + [pltpu.SemaphoreType.DMA((len(arguments),))],
        in_specs=[in_place] * len(arguments),
    )(*arguments)
    sent = sent.reshape(devices, 1, SENT * LANES)
    sent = lax.all_to_all(sent, axes, 0, 0, tiled=True).reshape(devices * SENT, LANES)
    (back,) = on_device(
        functools.partial(middle_kernel, x_devices),
        [((devices * RETURNED, LANES), single)],
        [pltpu.VMEM((x_devices * x_rows, LANES), single)],
    )(sent, *prepared, split_table(y_table.T), split_table(y_table))
    back = back.reshape(devices, 1, RETURNED * LANES)
    back = lax.all_to_all(back, axes, 0, 0, tiled=True).reshape(devices * RETURNED, LANES)
    shapes = [velocity.shape, velocity.shape, (6, units), (1, units), (3, units)]
    new, grad, grad_in, grad_bias, grad_out = on_device(
        functools.partial(unpack_kernel, float(cells)), [(shape, single) for shape in shapes]
    )(back, velocity, cotangent, split_table(z_table))
    return (new, grad, grad_in, grad_bias[0], grad_out.T)


def local(velocity, cotangent, weight_in, bias_in, weight_out):
    chosen = local_kernels if fits(velocity, weight_in.shape[1]) else local_plain
    return chosen(velocity, cotangent, weight_in, bias_in, weight_out)


def solution(mesh):
    in_specs = (P(None, "gx", "gy", None), P(None, "gx", "gy", None), P(), P(), P())
    out_specs = (P(None, "gx", "gy", None), P(None, "gx", "gy", None), P(), P(), P())
    return jax.shard_map(local, mesh=mesh, in_specs=in_specs, out_specs=out_specs, check_vma=False)
```
